256 devices in a mesh: long: 64 (over z_hi, y, x, core), short: 4 (over z_lo).
Axes of the slice: x: 4, y: 4, z: 8 (z_hi: 2, z_lo: 4; z = z_hi * 4 + z_lo), core: 2. Of those that a mesh axis runs over, the one named last changes fastest.
Arguments:
- field: bfloat16 [64, 1024, 1024], P(None, 'long', 'short'), may hold values from -6 to 6
- cotangent: bfloat16 [64, 1024, 1024], P(None, 'long', 'short'), may hold values from -6 to 6
- first_filter: bfloat16 [9, 64, 64], replicated, may hold values from -0.25 to 0.25
- second_filter: bfloat16 [9, 64, 64], replicated, may hold values from -0.25 to 0.25
Outputs:
- grad_field: bfloat16 [64, 1024, 1024], P(None, 'long', 'short')
- grad_first: float32 [9, 64, 64], replicated
- grad_second: float32 [9, 64, 64], replicated
The draws below stay inside these ranges and needn't reach their ends.
All inputs are finite; a program needn't handle non-finite values.
Results may differ from the reference program's by a relative error of at most 0.0095.
Values may be sent and summed in bfloat16 or wider, within the bound.
A program may use at most 64 MiB of HBM per device.

```python
import math
import jax
import jax.numpy as jnp
from jax import lax

CH = 64
NR = 1024
NC = 1024


def block_levels(key, shape, cuts, low, high):
    factor_of = 1.0
    for axis_at, blocks in cuts:
        steps = jax.random.uniform(jax.random.fold_in(jax.random.fold_in(key, 6), axis_at), (blocks,), jnp.float32, low / len(cuts), high / len(cuts))
        factor_of = factor_of * jnp.repeat(jnp.exp(steps), shape[axis_at] // blocks).reshape((-1,) + (1,) * (len(shape) - 1 - axis_at))
    return factor_of


def noise(stream_key, extent, scale, most, pieces=(), held_as=jnp.bfloat16):
    values = jax.random.normal(stream_key, extent, jnp.float32) * scale
    if len(pieces) > 0:
        values = block_levels(stream_key, extent, pieces, -0.22, 0.18) * values
    return jnp.clip(values, min=-most, max=most).astype(held_as)


def setup_inputs(seed: int = 0) -> dict:
    key_list = jax.random.split(jax.random.key(seed), 5)
    return {
        "field": noise(key_list[0], (CH, NR, NC), 1.0, 6.0, ((1, 64), (2, 4))),
        "cotangent": noise(key_list[1], (CH, NR, NC), 1.0, 6.0, ((1, 64), (2, 4))),
        "first_filter": noise(key_list[2], (9, CH, CH), (9 * CH) ** -0.5, 0.25),
        "second_filter": noise(key_list[3], (9, CH, CH), (9 * CH) ** -0.5, 0.25),
    }


def dilated_full(values, taps, dilation):
    width = taps.shape[1]
    kernel = taps.astype(jnp.float32).reshape(3, 3, width, width).transpose(2, 3, 0, 1)
    result = lax.conv_general_dilated(values.astype(jnp.float32)[None], kernel, (1, 1), ((dilation, dilation), (dilation, dilation)), rhs_dilation=(dilation, dilation), precision=lax.Precision.HIGHEST)
    return result[0]

def flipped(taps):
    return taps[::-1].transpose(0, 2, 1)

def correlate(grad, act, dilation):
    height = grad.shape[1]
    breadth = grad.shape[2]
    padded = jnp.pad(act.astype(jnp.float32), ((0, 0), (dilation, dilation), (dilation, dilation)))
    grad_wide = grad.astype(jnp.float32)
    terms = []
    for row_tap in range(3):
        for col_tap in range(3):
            window = padded[:, row_tap * dilation:row_tap * dilation + height, col_tap * dilation:col_tap * dilation + breadth]
            terms.append(jnp.einsum('orc,irc->oi', grad_wide, window, precision=lax.Precision.HIGHEST))
    return jnp.stack(terms)

def reference(field, cotangent, first_filter, second_filter):
    act_first = jnp.maximum(field, 0)
    hidden = (field.astype(jnp.float32) + dilated_full(act_first, first_filter, 4)).astype(jnp.bfloat16)
    act_second = jnp.maximum(hidden, 0)
    upstream = dilated_full(cotangent, flipped(second_filter), 8)
    grad_hidden = (cotangent.astype(jnp.float32) + jnp.where(hidden > 0, upstream, 0.0)).astype(jnp.bfloat16)
    back_term = dilated_full(grad_hidden, flipped(first_filter), 4)
    grad_field = (grad_hidden.astype(jnp.float32) + jnp.where(field > 0, back_term, 0.0)).astype(jnp.bfloat16)
    grad_scale = 1.0 / math.sqrt(NR * NC)
    grad_first = correlate(grad_hidden, act_first, 4) * grad_scale
    grad_second = correlate(cotangent, act_second, 8) * grad_scale
    return (grad_field, grad_first, grad_second)
```

```python
import math

import jax
import jax.numpy as jnp
from jax import lax
from jax.experimental import pallas as pl
from jax.experimental.pallas import tpu as pltpu
from jax.sharding import PartitionSpec as P

BF = jnp.bfloat16
F32 = jnp.float32
MESH = pl.DeviceIdType.MESH
CH, TR, TC = 64, 16, 256
K = 9 * CH
LONG, SHORT = 64, 4
PLANE = 32
NZ = LONG // PLANE * SHORT
CHUNK = 32
NCHUNK = K // CHUNK
OWNERS = tuple(range(0, 32, 2)) + (1, 21)

ROWS = ((-1, 0), (1, 0))
PACKS = ((0, -1), (0, 1), (-1, -1), (-1, 1), (1, -1), (1, 1))


def nt_dot(a, b):
    return lax.dot_general(a, b, (((1,), (1,)), ((), ())), preferred_element_type=F32)


def dot(a, b):
    return jnp.dot(a, b, preferred_element_type=F32)


def kernel(scale, field_hbm, cot_hbm, w1_ref, w2_ref, gf_ref, gr_ref,
           raw_f, raw_c, xf, a2, fs, cs, gs, ps, pleft, pright, gps, gleft, gright,
           w1c, w1t, w2t, acc2, acc1, gb, ra, rb, fin, in_sem,
           h_send, h_recv, g_send, g_recv, a_send, a_recv, b_send, b_recv, c_send, c_recv):
    l = lax.axis_index("long")
    s = lax.axis_index("short")
    place = lax.rem(l, PLANE)
    base = l - place
    z = lax.div(l, PLANE) * SHORT + s

    in_f = pltpu.make_async_copy(field_hbm, raw_f, in_sem.at[0])
    in_c = pltpu.make_async_copy(cot_hbm, raw_c, in_sem.at[1])
    in_f.start()
    in_c.start()

    barrier = pltpu.get_barrier_semaphore()

    def greet(dev_l, dev_s):
        pl.semaphore_signal(barrier, inc=1, device_id=(dev_l, dev_s), device_id_type=MESH)

    for dl, ds in ROWS + PACKS:
        greet(lax.rem(l + dl + LONG, LONG), lax.rem(s + ds + SHORT, SHORT))

    @pl.loop(1, PLANE)
    def _(k):
        greet(base + lax.rem(place + k, PLANE), s)

    def z_peer(k):
        other = lax.rem(z + k, NZ)
        return lax.div(other, SHORT) * PLANE + place, lax.rem(other, SHORT)

    for k in range(1, NZ):
        greet(*z_peer(k))

    def there(dl, ds):
        ok = None
        for d, at, n in ((dl, l, LONG), (ds, s, SHORT)):
            if d == 0:
                continue
            here = at + d >= 0 if d < 0 else at + d < n
            ok = here if ok is None else jnp.logical_and(ok, here)
        return ok

    def exchange(messages, send_sems, recv_sems):
        copies = []
        for i, (dl, ds, src, dst) in enumerate(messages):
            copies.append(pltpu.make_async_remote_copy(
                src_ref=src, dst_ref=dst, send_sem=send_sems.at[i], recv_sem=recv_sems.at[i],
                device_id=(l + dl, s + ds), device_id_type=MESH))

        def start(i):
            dl, ds = messages[i][:2]
            pl.when(there(dl, ds))(lambda: copies[i].start())

        def wait_recv(i):
            dl, ds, _, dst = messages[i]
            from_there = there(-dl, -ds)
            pl.when(from_there)(lambda: copies[i].wait_recv())

            @pl.when(jnp.logical_not(from_there))
            def _():
                dst[...] = jnp.zeros(dst.shape, dst.dtype)

        def wait_send(i):
            dl, ds = messages[i][:2]
            pl.when(there(dl, ds))(lambda: copies[i].wait_send())

        return start, wait_recv, wait_send

    halo = [
        (-1, 0, fs.at[1, pl.ds(4, 4)], fs.at[1, pl.ds(20, 4)]),
        (1, 0, fs.at[1, pl.ds(16, 4)], fs.at[1, pl.ds(0, 4)]),
        (-1, 0, cs.at[1, pl.ds(8, 8)], cs.at[1, pl.ds(24, 8)]),
        (1, 0, cs.at[1, pl.ds(16, 8)], cs.at[1, pl.ds(0, 8)]),
        (0, -1, ps.at[0], pright.at[pl.ds(1, 2)]),
        (0, 1, ps.at[1], pleft.at[pl.ds(1, 2)]),
        (-1, -1, ps.at[0, pl.ds(0, 1)], pright.at[pl.ds(3, 1)]),
        (-1, 1, ps.at[1, pl.ds(0, 1)], pleft.at[pl.ds(3, 1)]),
        (1, -1, ps.at[0, pl.ds(1, 1)], pright.at[pl.ds(0, 1)]),
        (1, 1, ps.at[1, pl.ds(1, 1)], pleft.at[pl.ds(0, 1)]),
    ]
    h_start, h_wait, h_sent = exchange(halo, h_send, h_recv)
    ghalo = [
        (-1, 0, gs.at[1, pl.ds(4, 4)], gs.at[1, pl.ds(20, 4)]),
        (1, 0, gs.at[1, pl.ds(16, 4)], gs.at[1, pl.ds(0, 4)]),
        (0, -1, gps.at[0], gright.at[1]),
        (0, 1, gps.at[1], gleft.at[1]),
        (-1, -1, gps.at[0], gright.at[2]),
        (-1, 1, gps.at[1], gleft.at[2]),
        (1, -1, gps.at[0], gright.at[0]),
        (1, 1, gps.at[1], gleft.at[0]),
    ]
    g_start, g_wait, g_sent = exchange(ghalo, g_send, g_recv)

    for t in range(9):
        w1c[:, CH * t:CH * (t + 1)] = w1_ref[t]
    w1t[...] = w1_ref[...].reshape(K, CH).T
    w2t[...] = w2_ref[...].reshape(K, CH).T

    in_f.wait()
    own_f = jnp.swapaxes(raw_f[...], 0, 1)
    xf[...] = own_f
    fs[1, 4:20] = jnp.maximum(own_f, 0)
    in_c.wait()
    cs[1, 8:24] = jnp.swapaxes(raw_c[...], 0, 1)

    pl.semaphore_wait(barrier, len(ROWS + PACKS) + PLANE - 1 + NZ - 1)
    for i in range(4):
        h_start(i)
    for half in range(2):
        for side in range(2):
            c8 = 0 if side == 0 else TC - 8
            c4 = 0 if side == 0 else TC - 4
            pieces = [cs[1, 8 + 8 * half + k][:, c8:c8 + 8] for k in range(8)]
            pieces += [fs[1, 4 + 8 * half + k][:, c4:c4 + 4] for k in range(8)]
            pieces += [jnp.zeros((CH, 32), BF)]
            ps[side, half] = jnp.concatenate(pieces, axis=1)
    for i in range(4, 10):
        h_start(i)

    def shift_left(x, h, at, d):
        return jnp.concatenate([x[:, d:], h[:, at:at + d]], axis=1)

    def shift_right(x, h, at, d):
        return jnp.concatenate([h[:, at:at + d], x[:, :TC - d]], axis=1)

    def f_row(blk, k):
        e = 8 * blk + k - 4
        x = fs[1, e]
        fs[0, e] = shift_right(x, pleft[blk], 64 + 4 * k, 4)
        fs[2, e] = shift_left(x, pright[blk], 64 + 4 * k, 4)

    def c_row(blk, k):
        e = 8 * blk + k
        x = cs[1, e]
        cs[2, e] = shift_right(x, pleft[blk], 8 * k, 8)
        cs[0, e] = shift_left(x, pright[blk], 8 * k, 8)

    h_wait(4)
    h_wait(5)

    @pl.loop(1, 3)
    def _(blk):
        for k in range(8):
            f_row(blk, k)
            c_row(blk, k)

    for i in (6, 7, 8, 9, 0, 1):
        h_wait(i)
    for k in range(4):
        f_row(0, k + 4)
        f_row(3, k)

    def taps(ref, r, first, step):
        return jnp.concatenate([ref[b, r + first + step * a] for a in range(3) for b in range(3)], axis=0)

    @pl.loop(0, TR // 4)
    def _(g):
        for k in range(4):
            r = 4 * g + k
            h = xf[r].astype(F32) + dot(w1c[...], taps(fs, r, 0, 4))
            a2[r] = jnp.maximum(h.astype(BF), 0)

    h_wait(2)
    h_wait(3)

    @pl.loop(0, 2)
    def _(i):
        for k in range(8):
            c_row(3 * i, k)

    @pl.loop(0, TR // 4)
    def _(g):
        for k in range(4):
            r = 4 * g + k
            up = dot(w2t[...], taps(cs, r, 16, -8))
            gh = cs[1, r + 8].astype(F32) + jnp.where(a2[r].astype(F32) > 0, up, 0.0)
            gs[1, r + 4] = gh.astype(BF)

    g_start(0)
    g_start(1)
    for side in range(2):
        c4 = 0 if side == 0 else TC - 4
        pieces = [gs[1, 4 + k][:, c4:c4 + 4] for k in range(16)] + [jnp.zeros((CH, 64), BF)]
        gps[side] = jnp.concatenate(pieces, axis=1)
    for i in range(2, 8):
        g_start(i)

    acc2[...] = jnp.zeros_like(acc2)
    acc1[...] = jnp.zeros_like(acc1)

    @pl.loop(0, TR // 4)
    def _(g):
        r0 = 4 * g
        u2 = jnp.concatenate([taps(cs, r0 + k, 16, -8) for k in range(4)], axis=1)
        v2 = jnp.concatenate([a2[r0 + k] for k in range(4)], axis=1)
        acc2[...] += nt_dot(u2, v2)
        u1 = jnp.concatenate([taps(fs, r0 + k, 0, 4) for k in range(4)], axis=1)
        v1 = jnp.concatenate([gs[1, r0 + 4 + k] for k in range(4)], axis=1)
        acc1[...] += nt_dot(v1, u1)

    for t in range(9):
        gb[CH * t:CH * (t + 1), :] = jnp.concatenate(
            [acc2[CH * t:CH * (t + 1), :], acc1[:, CH * t:CH * (t + 1)]], axis=1).astype(BF)

    def a_copy(j):
        owner = OWNERS[j]
        slot = lax.rem(place - owner + PLANE - 1, PLANE)
        return pltpu.make_async_remote_copy(
            src_ref=gb.at[pl.ds(CHUNK * j, CHUNK)], dst_ref=ra.at[slot],
            send_sem=a_send.at[j], recv_sem=a_recv,
            device_id=(base + owner, s), device_id_type=MESH)

    for j in range(NCHUNK):
        pl.when(place != OWNERS[j])(lambda j=j: a_copy(j).start())

    for i in range(8):
        g_wait(i)

    def g_row(blk, e, at):
        x = gs[1, e]
        gs[2, e] = shift_right(x, gleft[blk], at, 4)
        gs[0, e] = shift_left(x, gright[blk], at, 4)

    for k in range(16):
        g_row(1, 4 + k, 4 * k)
    for k in range(4):
        g_row(0, k, 4 * (12 + k))
        g_row(2, 20 + k, 4 * k)

    @pl.loop(0, TR // 4)
    def _(g):
        for k in range(4):
            r = 4 * g + k
            back = dot(w1t[...], taps(gs, r, 8, -4))
            out = gs[1, r + 4].astype(F32) + jnp.where(xf[r].astype(F32) > 0, back, 0.0)
            gf_ref[r] = out.astype(BF)

    is_owner = jnp.logical_or(lax.rem(place, 2) == 0, jnp.logical_or(place == 1, place == 21))
    mine = jnp.where(place == 1, 16, jnp.where(place == 21, 17, lax.div(place, 2)))
    my_rows = pl.ds(pl.multiple_of(CHUNK * mine, CHUNK), CHUNK)

    def b_copy(k):
        return pltpu.make_async_remote_copy(
            src_ref=rb.at[0], dst_ref=rb.at[k], send_sem=b_send.at[k - 1], recv_sem=b_recv.at[k - 1],
            device_id=z_peer(k), device_id_type=MESH)

    def c_copy(k):
        return pltpu.make_async_remote_copy(
            src_ref=fin.at[my_rows], dst_ref=fin.at[my_rows], send_sem=c_send.at[k - 1],
            recv_sem=c_recv.at[mine], device_id=(base + lax.rem(place + k, PLANE), s),
            device_id_type=MESH)

    @pl.when(is_owner)
    def _():
        pltpu.make_async_copy(ra, ra, a_recv).wait()
        total = gb[my_rows, :].astype(F32)
        for i in range(PLANE - 1):
            total += ra[i].astype(F32)
        rb[0] = total.astype(BF)
        for k in range(1, NZ):
            b_copy(k).start()
        for k in range(1, NZ):
            b_copy(k).wait_recv()
        full = rb[0].astype(F32)
        for k in range(1, NZ):
            full += rb[k].astype(F32)
        fin[my_rows, :] = (full * scale).astype(BF)

        @pl.loop(1, PLANE)
        def _(k):
            c_copy(k).start()

    for j in range(NCHUNK):
        @pl.when(place != OWNERS[j])
        def _(j=j):
            rows = fin.at[pl.ds(CHUNK * j, CHUNK)]
            pltpu.make_async_copy(rows, rows, c_recv.at[j]).wait()

    gr_ref[...] = fin[...]

    for i in range(10):
        h_sent(i)
    for i in range(8):
        g_sent(i)
    for j in range(NCHUNK):
        pl.when(place != OWNERS[j])(lambda j=j: a_copy(j).wait_send())

    @pl.when(is_owner)
    def _():
        for k in range(1, NZ):
            b_copy(k).wait_send()

        @pl.loop(1, PLANE)
        def _(k):
            c_copy(k).wait_send()


def shards(field, cotangent, first_filter, second_filter):
    scale = 1.0 / math.sqrt(TR * LONG * TC * SHORT)
    any_spec = pl.BlockSpec(memory_space=pl.ANY)
    vmem = pl.BlockSpec(memory_space=pltpu.VMEM)
    dma = pltpu.SemaphoreType.DMA

    def buf(*shape, dtype=BF):
        return pltpu.VMEM(shape, dtype)

    gf, gr = pl.pallas_call(
        lambda *refs: kernel(scale, *refs),
        out_shape=(jax.ShapeDtypeStruct((TR, CH, TC), BF), jax.ShapeDtypeStruct((K, 2 * CH), BF)),
        in_specs=[any_spec, any_spec, vmem, vmem],
        out_specs=(vmem, vmem),
        scratch_shapes=[
            buf(CH, TR, TC), buf(CH, TR, TC), buf(TR, CH, TC), buf(TR, CH, TC),
            buf(3, TR + 8, CH, TC), buf(3, TR + 16, CH, TC), buf(3, TR + 8, CH, TC),
            buf(2, 2, CH, 128), buf(4, CH, 128), buf(4, CH, 128),
            buf(2, CH, 128), buf(3, CH, 128), buf(3, CH, 128),
            buf(CH, K), buf(CH, K), buf(CH, K),
            buf(K, CH, dtype=F32), buf(CH, K, dtype=F32), buf(K, 2 * CH),
            buf(PLANE - 1, CHUNK, 2 * CH), buf(NZ, CHUNK, 2 * CH), buf(K, 2 * CH),
            dma((2,)), dma((10,)), dma((10,)), dma((8,)), dma((8,)),
            dma((NCHUNK,)), dma, dma((NZ - 1,)), dma((NZ - 1,)), dma((PLANE - 1,)), dma((NCHUNK,)),
        ],
        compiler_params=pltpu.CompilerParams(
            collective_id=0, has_side_effects=True, vmem_limit_bytes=40 << 20),
        name="dilated_backward",
    )(field, cotangent, first_filter, second_filter)
    grads = gr.astype(F32).reshape(9, CH, 2 * CH)
    return gf.transpose(1, 0, 2), grads[:, :, CH:], grads[:, :, :CH]


def solution(mesh):
    in_specs = (P(None, "long", "short"), P(None, "long", "short"), P(), P())
    out_specs = (P(None, "long", "short"), P(), P())
    return jax.shard_map(shards, mesh=mesh, in_specs=in_specs, out_specs=out_specs, check_vma=False)
```

```python
import math

import jax
import jax.numpy as jnp
from jax import lax
from jax.experimental import pallas as pl
from jax.experimental.pallas import tpu as pltpu
from jax.sharding import PartitionSpec as P

BF = jnp.bfloat16
F32 = jnp.float32
MESH = pl.DeviceIdType.MESH
CH, TR, TC = 64, 16, 256
K = 9 * CH
LONG, SHORT = 64, 4
PLANE = 32
NZ = LONG // PLANE * SHORT
CHUNK = 32
NCHUNK = K // CHUNK
OWNERS = (1,) + tuple(range(2, 32, 2)) + (11, 21)

NEAR = ((-1, 0), (1, 0), (0, -1), (0, 1), (-1, -1), (-1, 1), (1, -1), (1, 1))


def ring_distance(a, n):
    return min(a % n, -a % n)


PLANE_STEPS = sorted(
    [(y, x, c) for y in range(4) for x in range(4) for c in range(2) if (y, x, c) != (0, 0, 0)],
    key=lambda t: -(ring_distance(t[0], 4) + ring_distance(t[1], 4)))
Z_STEPS = sorted(range(1, NZ), key=lambda k: -ring_distance(k, NZ))


def nt_dot(a, b):
    return lax.dot_general(a, b, (((1,), (1,)), ((), ())), preferred_element_type=F32)


def dot(a, b):
    return jnp.dot(a, b, preferred_element_type=F32)


def arrived(ref, sem):
    pltpu.make_async_copy(ref, ref, sem).wait()


def kernel(scale, field_hbm, cot_hbm, w1_hbm, w2_hbm, gf_ref, gr_ref,
           raw_f, raw_c, raw_w1, raw_w2, xf, a2, fs, cs, gs, ps, pleft, pright, gps, gleft, gright,
           w1c, w1t, w2own, w2halo, up_own, acc2, acc1, gb, ra, rb, fin, in_sem,
           f_send, f_recv, c_send, c_recv, p_send, p_recv, g_send, g_recv,
           a_send, a_recv, b_send, b_recv, o_send, o_recv):
    l = lax.axis_index("long")
    s = lax.axis_index("short")
    place = lax.rem(l, PLANE)
    base = l - place
    core = lax.rem(l, 2)
    z = lax.div(l, PLANE) * SHORT + s

    fetch = [pltpu.make_async_copy(src, dst, in_sem.at[i]) for i, (src, dst) in enumerate(
        ((field_hbm, raw_f), (cot_hbm, raw_c), (w1_hbm, raw_w1), (w2_hbm, raw_w2)))]
    for copy in fetch:
        copy.start()

    barrier = pltpu.get_barrier_semaphore()

    def greet(dev):
        pl.semaphore_signal(barrier, inc=1, device_id=dev, device_id_type=MESH)

    def there(dl, ds):
        ok = None
        for d, at, n in ((dl, l, LONG), (ds, s, SHORT)):
            if d == 0:
                continue
            here = at + d >= 0 if d < 0 else at + d < n
            ok = here if ok is None else jnp.logical_and(ok, here)
        return ok

    def plane_peer(step):
        y, x, c = step
        py = lax.rem(lax.div(place, 8) + y, 4)
        px = lax.rem(lax.div(place, 2) + x, 4)
        return base + py * 8 + px * 2 + lax.rem(core + c, 2), s

    def z_peer(k):
        other = lax.rem(z + k, NZ)
        return lax.div(other, SHORT) * PLANE + place, lax.rem(other, SHORT)

    greetings = jnp.int32(PLANE - 1 + NZ - 1)
    for dl, ds in NEAR:
        pl.when(there(dl, ds))(lambda dl=dl, ds=ds: greet((l + dl, s + ds)))
        greetings = greetings + there(dl, ds).astype(jnp.int32)
    for k in Z_STEPS:
        greet(z_peer(k))
    for step in PLANE_STEPS:
        greet(plane_peer(step))

    def message(dl, ds, src, dst, send_sem, recv_sem):
        copy = pltpu.make_async_remote_copy(
            src_ref=src, dst_ref=dst, send_sem=send_sem, recv_sem=recv_sem,
            device_id=(l + dl, s + ds), device_id_type=MESH)
        ok = there(dl, ds)
        return (lambda: pl.when(ok)(lambda: copy.start()),
                lambda: pl.when(ok)(lambda: copy.wait_send()))

    def receive(ok, dst, sem):
        pl.when(ok)(lambda: arrived(dst, sem))

        @pl.when(jnp.logical_not(ok))
        def _():
            dst[...] = jnp.zeros(dst.shape, dst.dtype)

    f_out = [message(-1, 0, fs.at[1, pl.ds(4, 4)], fs.at[1, pl.ds(20, 4)], f_send.at[0], f_recv.at[1]),
             message(1, 0, fs.at[1, pl.ds(16, 4)], fs.at[1, pl.ds(0, 4)], f_send.at[1], f_recv.at[0])]
    c_out = [message(-1, 0, cs.at[1, pl.ds(8, 8)], cs.at[1, pl.ds(24, 8)], c_send.at[0], c_recv.at[1]),
             message(1, 0, cs.at[1, pl.ds(16, 8)], cs.at[1, pl.ds(0, 8)], c_send.at[1], c_recv.at[0])]
    g_out = [message(-1, 0, gs.at[1, pl.ds(4, 4)], gs.at[1, pl.ds(20, 4)], g_send.at[0], g_recv.at[7]),
             message(1, 0, gs.at[1, pl.ds(16, 4)], gs.at[1, pl.ds(0, 4)], g_send.at[1], g_recv.at[6])]
    p_out = []
    for side, (ds, into, g_into) in enumerate(((-1, pright, gright), (1, pleft, gleft))):
        p_out.append(message(0, ds, ps.at[side], into.at[pl.ds(1, 2)], p_send.at[side], p_recv.at[1 - side]))
        g_out.append(message(0, ds, gps.at[side], g_into.at[1], g_send.at[2 + side], g_recv.at[1 - side]))
    for half, dl in ((0, -1), (1, 1)):
        for side, (ds, into, g_into) in enumerate(((-1, pright, gright), (1, pleft, gleft))):
            out, back = 2 + 2 * half + side, 2 + 2 * (1 - half) + 1 - side
            p_out.append(message(
                dl, ds, ps.at[side, pl.ds(half, 1)], into.at[pl.ds(3 - 3 * half, 1)], p_send.at[out], p_recv.at[back]))
            g_out.append(message(
                dl, ds, gps.at[side], g_into.at[2 - 2 * half], g_send.at[2 + out], g_recv.at[back]))

    fetch[0].wait()
    own_f = jnp.swapaxes(raw_f[...], 0, 1)
    xf[...] = own_f
    fs[1, 4:20] = jnp.maximum(own_f, 0)
    fetch[1].wait()
    cs[1, 8:24] = jnp.swapaxes(raw_c[...], 0, 1)
    for half in range(2):
        for side in range(2):
            c8 = 0 if side == 0 else TC - 8
            c4 = 0 if side == 0 else TC - 4
            pieces = [cs[1, 8 + 8 * half + k][:, c8:c8 + 8] for k in range(8)]
            pieces += [fs[1, 4 + 8 * half + k][:, c4:c4 + 4] for k in range(8)]
            pieces += [jnp.zeros((CH, 32), BF)]
            ps[side, half] = jnp.concatenate(pieces, axis=1)

    pl.semaphore_wait(barrier, greetings)
    for start, _ in f_out + p_out + c_out:
        start()

    fetch[2].wait()
    fetch[3].wait()
    for t in range(9):
        w1c[:, CH * t:CH * (t + 1)] = raw_w1[t]
    w1t[...] = raw_w1[...].reshape(K, CH).T
    taps_of = [raw_w2[3 * a:3 * a + 3].reshape(3 * CH, CH).T for a in range(3)]
    for half in range(2):
        w2own[half] = jnp.concatenate([taps_of[1], taps_of[2 * half]], axis=1)
        w2halo[half] = taps_of[2 - 2 * half]

    acc2[...] = jnp.zeros_like(acc2)
    acc1[...] = jnp.zeros_like(acc1)

    def shift_left(x, h, at, d):
        return jnp.concatenate([x[:, d:], h[:, at:at + d]], axis=1)

    def shift_right(x, h, at, d):
        return jnp.concatenate([h[:, at:at + d], x[:, :TC - d]], axis=1)

    def f_row(blk, k, e):
        x = fs[1, e]
        fs[0, e] = shift_right(x, pleft[blk], 64 + 4 * k, 4)
        fs[2, e] = shift_left(x, pright[blk], 64 + 4 * k, 4)

    def c_row(blk, k):
        e = 8 * blk + k
        x = cs[1, e]
        cs[2, e] = shift_right(x, pleft[blk], 8 * k, 8)
        cs[0, e] = shift_left(x, pright[blk], 8 * k, 8)

    def taps(ref, rows):
        return [ref[b, e] for e in rows for b in range(3)]

    def stack(parts):
        return jnp.concatenate(parts, axis=0)

    receive(there(0, -1), pleft.at[pl.ds(1, 2)], p_recv.at[0])
    receive(there(0, 1), pright.at[pl.ds(1, 2)], p_recv.at[1])

    @pl.loop(1, 3)
    def _(blk):
        for k in range(8):
            f_row(blk, k, 8 * blk + k - 4)
            c_row(blk, k)

    def hidden_row(r):
        h = xf[r].astype(F32) + dot(w1c[...], stack(taps(fs, [r, r + 4, r + 8])))
        a2[r] = jnp.maximum(h.astype(BF), 0)

    @pl.loop(1, 3)
    def _(g):
        for k in range(4):
            hidden_row(4 * g + k)

    for half in range(2):
        @pl.loop(0, 2)
        def _(g):
            for k in range(4):
                r = 8 * half + 4 * g + k
                up_own[r] = dot(w2own[half], stack(taps(cs, [r + 8, r + 16 - 16 * half])))

    @pl.loop(0, 2)
    def _(i):
        half = (1 - core) + i * (2 * core - 1)
        ok = jnp.logical_or(jnp.logical_and(half == 0, l > 0), jnp.logical_and(half == 1, l < LONG - 1))
        receive(jnp.logical_and(ok, s > 0), pleft.at[pl.ds(3 * half, 1)], p_recv.at[2 + 2 * half])
        receive(jnp.logical_and(ok, s < SHORT - 1), pright.at[pl.ds(3 * half, 1)], p_recv.at[3 + 2 * half])
        receive(ok, fs.at[1, pl.ds(20 * half, 4)], f_recv.at[half])
        for k in range(4):
            e = 20 * half + k
            x = fs[1, e]
            for b, shift, pack in ((0, shift_right, pleft), (2, shift_left, pright)):
                low = shift(x, pack[3 * half], 64 + 4 * k, 4)
                high = shift(x, pack[3 * half], 64 + 4 * (k + 4), 4)
                fs[b, e] = jnp.where(half == 1, low, high)
        for k in range(4):
            hidden_row(12 * half + k)

        rows = [8 * half + k for k in range(8)]
        act = jnp.concatenate([a2[r] for r in rows], axis=1)
        own = nt_dot(
            jnp.concatenate([stack(taps(cs, [r + 8, r + 16 - 16 * half])) for r in rows], axis=1), act)
        acc2[1] += own[:3 * CH]
        acc2[2 * half] += own[3 * CH:]

        receive(ok, cs.at[1, pl.ds(24 * half, 8)], c_recv.at[half])
        for k in range(8):
            c_row(3 * half, k)
        beyond = [stack(taps(cs, [24 * half + k])) for k in range(8)]
        for k, r in enumerate(rows):
            up = up_own[r] + dot(w2halo[half], beyond[k])
            gh = cs[1, r + 8].astype(F32) + jnp.where(a2[r].astype(F32) > 0, up, 0.0)
            gs[1, r + 4] = gh.astype(BF)
        acc2[2 - 2 * half] += nt_dot(jnp.concatenate(beyond, axis=1), act)
        acc1[...] += nt_dot(
            jnp.concatenate([gs[1, r + 4] for r in rows], axis=1),
            jnp.concatenate([stack(taps(fs, [r, r + 4, r + 8])) for r in rows], axis=1))

    for t in range(9):
        gb[CH * t:CH * (t + 1), :] = jnp.concatenate(
            [acc2[t // 3, CH * (t % 3):CH * (t % 3 + 1), :], acc1[:, CH * t:CH * (t + 1)]], axis=1).astype(BF)

    def a_copy(j):
        owner = OWNERS[j]
        slot = lax.rem(place - owner + PLANE - 1, PLANE)
        return pltpu.make_async_remote_copy(
            src_ref=gb.at[pl.ds(CHUNK * j, CHUNK)], dst_ref=ra.at[slot],
            send_sem=a_send.at[j], recv_sem=a_recv,
            device_id=(base + owner, s), device_id_type=MESH)

    for j in range(NCHUNK):
        pl.when(place != OWNERS[j])(lambda j=j: a_copy(j).start())

    for start, _ in g_out[:2]:
        start()
    for side in range(2):
        c4 = 0 if side == 0 else TC - 4
        pieces = [gs[1, 4 + k][:, c4:c4 + 4] for k in range(16)] + [jnp.zeros((CH, 64), BF)]
        gps[side] = jnp.concatenate(pieces, axis=1)
    for start, _ in g_out[2:]:
        start()

    is_owner = jnp.logical_or(
        jnp.logical_and(core == 0, place > 0),
        jnp.logical_or(place == 1, jnp.logical_or(place == 11, place == 21)))
    mine = jnp.where(place == 11, 16, jnp.where(place == 21, 17, lax.div(place, 2)))
    my_rows = pl.ds(pl.multiple_of(CHUNK * mine, CHUNK), CHUNK)

    def b_copy(k):
        return pltpu.make_async_remote_copy(
            src_ref=rb.at[0], dst_ref=rb.at[k], send_sem=b_send.at[k - 1], recv_sem=b_recv.at[k - 1],
            device_id=z_peer(k), device_id_type=MESH)

    def o_copy(n):
        return pltpu.make_async_remote_copy(
            src_ref=fin.at[my_rows], dst_ref=fin.at[my_rows], send_sem=o_send.at[n],
            recv_sem=o_recv.at[mine], device_id=plane_peer(PLANE_STEPS[n]), device_id_type=MESH)

    @pl.when(is_owner)
    def _():
        arrived(ra, a_recv)
        total = gb[my_rows, :].astype(F32)
        for i in range(PLANE - 1):
            total += ra[i].astype(F32)
        rb[0] = total.astype(BF)
        for k in Z_STEPS:
            b_copy(k).start()

    receive(there(-1, 0), gs.at[1, pl.ds(0, 4)], g_recv.at[6])
    receive(there(1, 0), gs.at[1, pl.ds(20, 4)], g_recv.at[7])
    for side, (ds, into) in enumerate(((-1, gleft), (1, gright))):
        receive(there(0, ds), into.at[1], g_recv.at[side])
        receive(there(-1, ds), into.at[0], g_recv.at[2 + side])
        receive(there(1, ds), into.at[2], g_recv.at[4 + side])

    def g_row(blk, e, at):
        x = gs[1, e]
        gs[2, e] = shift_right(x, gleft[blk], at, 4)
        gs[0, e] = shift_left(x, gright[blk], at, 4)

    for k in range(16):
        g_row(1, 4 + k, 4 * k)
    for k in range(4):
        g_row(0, k, 4 * (12 + k))
        g_row(2, 20 + k, 4 * k)

    @pl.loop(0, TR // 4)
    def _(g):
        for k in range(4):
            r = 4 * g + k
            back = dot(w1t[...], stack(taps(gs, [r + 8, r + 4, r])))
            out = gs[1, r + 4].astype(F32) + jnp.where(xf[r].astype(F32) > 0, back, 0.0)
            gf_ref[r] = out.astype(BF)

    @pl.when(is_owner)
    def _():
        full = rb[0].astype(F32)
        for k in reversed(Z_STEPS):
            b_copy(k).wait_recv()
            full += rb[k].astype(F32)
        fin[my_rows, :] = (full * scale).astype(BF)
        for n in range(PLANE - 1):
            o_copy(n).start()

    for _, sent in f_out + p_out + c_out + g_out:
        sent()
    for j in range(NCHUNK):
        pl.when(place != OWNERS[j])(lambda j=j: a_copy(j).wait_send())

    for j in range(NCHUNK):
        pl.when(place != OWNERS[j])(
            lambda j=j: arrived(fin.at[pl.ds(CHUNK * j, CHUNK)], o_recv.at[j]))
    gr_ref[...] = fin[...]

    @pl.when(is_owner)
    def _():
        for k in Z_STEPS:
            b_copy(k).wait_send()
        for n in range(PLANE - 1):
            o_copy(n).wait_send()


def shards(field, cotangent, first_filter, second_filter):
    scale = 1.0 / math.sqrt(TR * LONG * TC * SHORT)
    hbm = pl.BlockSpec(memory_space=pltpu.HBM)
    vmem = pl.BlockSpec(memory_space=pltpu.VMEM)
    dma = pltpu.SemaphoreType.DMA

    def buf(*shape, dtype=BF):
        return pltpu.VMEM(shape, dtype)

    gf, gr = pl.pallas_call(
        lambda *refs: kernel(scale, *refs),
        out_shape=(jax.ShapeDtypeStruct((TR, CH, TC), BF), jax.ShapeDtypeStruct((K, 2 * CH), BF)),
        in_specs=[hbm] * 4,
        out_specs=(vmem, vmem),
        scratch_shapes=[
            buf(CH, TR, TC), buf(CH, TR, TC), buf(9, CH, CH), buf(9, CH, CH),
            buf(TR, CH, TC), buf(TR, CH, TC),
            buf(3, TR + 8, CH, TC), buf(3, TR + 16, CH, TC), buf(3, TR + 8, CH, TC),
            buf(2, 2, CH, 128), buf(4, CH, 128), buf(4, CH, 128),
            buf(2, CH, 128), buf(3, CH, 128), buf(3, CH, 128),
            buf(CH, K), buf(CH, K), buf(2, CH, 6 * CH), buf(2, CH, 3 * CH),
            buf(TR, CH, TC, dtype=F32),
            buf(3, 3 * CH, CH, dtype=F32), buf(CH, K, dtype=F32), buf(K, 2 * CH),
            buf(PLANE - 1, CHUNK, 2 * CH), buf(NZ, CHUNK, 2 * CH), buf(K, 2 * CH),
            dma((4,)),
            dma((2,)), dma((2,)), dma((2,)), dma((2,)), dma((6,)), dma((6,)), dma((8,)), dma((8,)),
            dma((NCHUNK,)), dma, dma((NZ - 1,)), dma((NZ - 1,)), dma((PLANE - 1,)), dma((NCHUNK,)),
        ],
        compiler_params=pltpu.CompilerParams(
            collective_id=0, has_side_effects=True, vmem_limit_bytes=60 << 20),
        name="dilated_backward",
    )(field, cotangent, first_filter, second_filter)
    grads = gr.astype(F32).reshape(9, CH, 2 * CH)
    return gf.transpose(1, 0, 2), grads[:, :, CH:], grads[:, :, :CH]


def solution(mesh):
    in_specs = (P(None, "long", "short"), P(None, "long", "short"), P(), P())
    out_specs = (P(None, "long", "short"), P(), P())
    return jax.shard_map(shards, mesh=mesh, in_specs=in_specs, out_specs=out_specs, check_vma=False)
```

```python
import math

import jax
import jax.numpy as jnp
from jax import lax
from jax.experimental import pallas as pl
from jax.experimental.pallas import tpu as pltpu
from jax.sharding import PartitionSpec as P

BF = jnp.bfloat16
F32 = jnp.float32
MESH = pl.DeviceIdType.MESH
CH, TR, TC = 64, 16, 256
K = 9 * CH
LONG, SHORT = 64, 4
PLANE = 32
NZ = LONG // PLANE * SHORT
CHUNK = 32
NCHUNK = K // CHUNK
OWNERS = (8, 9, 22, 23, 2, 28, 16, 17, 4, 5, 14, 15, 26, 27, 24, 25, 6, 7)

NEAR = ((-1, 0), (1, 0), (0, -1), (0, 1), (-1, -1), (-1, 1), (1, -1), (1, 1))


def ring_distance(a, n):
    return min(a % n, -a % n)


PLANE_STEPS = sorted(
    [(y, x, c) for y in range(4) for x in range(4) for c in range(2) if (y, x, c) != (0, 0, 0)],
    key=lambda t: -(ring_distance(t[0], 4) + ring_distance(t[1], 4)))
Z_STEPS = sorted(range(1, NZ), key=lambda k: -ring_distance(k, NZ))


def nt_dot(a, b):
    return lax.dot_general(a, b, (((1,), (1,)), ((), ())), preferred_element_type=F32)


def dot(a, b):
    return jnp.dot(a, b, preferred_element_type=F32)


def arrived(ref, sem):
    pltpu.make_async_copy(ref, ref, sem).wait()


def kernel(scale, field_hbm, cot_hbm, w1_hbm, w2_hbm, gf_ref, gr_ref,
           raw_f, raw_c, raw_w1, raw_w2, xf, a2, fs, cs, gs, ps, pleft, pright, gps, gleft, gright,
           w1c, w1t, w2own, w2halo, up_own, acc2, acc1, gb, ra, rb, fin, in_sem,
           f_send, f_recv, c_send, c_recv, p_send, p_recv, g_send, g_recv,
           a_send, a_recv, b_send, b_recv, o_send, o_recv, ready, out_sem):
    l = lax.axis_index("long")
    s = lax.axis_index("short")
    place = lax.rem(l, PLANE)
    base = l - place
    core = lax.rem(l, 2)
    z = lax.div(l, PLANE) * SHORT + s

    fetch = [pltpu.make_async_copy(src, dst, in_sem.at[i]) for i, (src, dst) in enumerate(
        ((field_hbm, raw_f), (cot_hbm, raw_c), (w1_hbm, raw_w1), (w2_hbm, raw_w2)))]
    for copy in fetch:
        copy.start()

    barrier = pltpu.get_barrier_semaphore()

    def greet(dev):
        pl.semaphore_signal(barrier, inc=1, device_id=dev, device_id_type=MESH)

    def there(dl, ds):
        ok = None
        for d, at, n in ((dl, l, LONG), (ds, s, SHORT)):
            if d == 0:
                continue
            here = at + d >= 0 if d < 0 else at + d < n
            ok = here if ok is None else jnp.logical_and(ok, here)
        return ok

    def plane_peer(step):
        y, x, c = step
        py = lax.rem(lax.div(place, 8) + y, 4)
        px = lax.rem(lax.div(place, 2) + x, 4)
        return base + py * 8 + px * 2 + lax.rem(core + c, 2), s

    def z_peer(k):
        other = lax.rem(z + k, NZ)
        return lax.div(other, SHORT) * PLANE + place, lax.rem(other, SHORT)

    row_steps = [step for step in PLANE_STEPS if step[0] == 0]
    column_steps = [step for step in PLANE_STEPS if step[1:] == (0, 0)]
    first = [plane_peer(step) for step in row_steps + column_steps] + [z_peer(1), z_peer(NZ - 1)]
    greetings = jnp.int32(len(first))
    for dl, ds in NEAR:
        pl.when(there(dl, ds))(lambda dl=dl, ds=ds: greet((l + dl, s + ds)))
        greetings = greetings + there(dl, ds).astype(jnp.int32)
    for dev in first:
        greet(dev)

    def pass_on(n, devs):
        for dev in devs:
            pl.semaphore_signal(ready.at[n], inc=1, device_id=dev, device_id_type=MESH)

    def message(dl, ds, src, dst, send_sem, recv_sem):
        copy = pltpu.make_async_remote_copy(
            src_ref=src, dst_ref=dst, send_sem=send_sem, recv_sem=recv_sem,
            device_id=(l + dl, s + ds), device_id_type=MESH)
        ok = there(dl, ds)
        return (lambda: pl.when(ok)(lambda: copy.start()),
                lambda: pl.when(ok)(lambda: copy.wait_send()))

    def receive(ok, dst, sem):
        pl.when(ok)(lambda: arrived(dst, sem))

        @pl.when(jnp.logical_not(ok))
        def _():
            dst[...] = jnp.zeros(dst.shape, dst.dtype)

    f_out = [message(-1, 0, fs.at[1, pl.ds(4, 4)], fs.at[1, pl.ds(20, 4)], f_send.at[0], f_recv.at[1]),
             message(1, 0, fs.at[1, pl.ds(16, 4)], fs.at[1, pl.ds(0, 4)], f_send.at[1], f_recv.at[0])]
    c_out = [message(-1, 0, cs.at[1, pl.ds(8, 8)], cs.at[1, pl.ds(24, 8)], c_send.at[0], c_recv.at[1]),
             message(1, 0, cs.at[1, pl.ds(16, 8)], cs.at[1, pl.ds(0, 8)], c_send.at[1], c_recv.at[0])]
    g_out = [message(-1, 0, gs.at[1, pl.ds(4, 4)], gs.at[1, pl.ds(20, 4)], g_send.at[0], g_recv.at[7]),
             message(1, 0, gs.at[1, pl.ds(16, 4)], gs.at[1, pl.ds(0, 4)], g_send.at[1], g_recv.at[6])]
    p_out = []
    for side, (ds, into, g_into) in enumerate(((-1, pright, gright), (1, pleft, gleft))):
        p_out.append(message(0, ds, ps.at[side], into.at[pl.ds(1, 2)], p_send.at[side], p_recv.at[1 - side]))
        g_out.append(message(0, ds, gps.at[side], g_into.at[1], g_send.at[2 + side], g_recv.at[1 - side]))
    for half, dl in ((0, -1), (1, 1)):
        for side, (ds, into, g_into) in enumerate(((-1, pright, gright), (1, pleft, gleft))):
            out, back = 2 + 2 * half + side, 2 + 2 * (1 - half) + 1 - side
            p_out.append(message(
                dl, ds, ps.at[side, pl.ds(half, 1)], into.at[pl.ds(3 - 3 * half, 1)], p_send.at[out], p_recv.at[back]))
            g_out.append(message(
                dl, ds, gps.at[side], g_into.at[2 - 2 * half], g_send.at[2 + out], g_recv.at[back]))

    fetch[0].wait()
    own_f = jnp.swapaxes(raw_f[...], 0, 1)
    xf[...] = own_f
    fs[1, 4:20] = jnp.maximum(own_f, 0)
    fetch[1].wait()
    cs[1, 8:24] = jnp.swapaxes(raw_c[...], 0, 1)
    for half in range(2):
        for side in range(2):
            c8 = 0 if side == 0 else TC - 8
            c4 = 0 if side == 0 else TC - 4
            pieces = [cs[1, 8 + 8 * half + k][:, c8:c8 + 8] for k in range(8)]
            pieces += [fs[1, 4 + 8 * half + k][:, c4:c4 + 4] for k in range(8)]
            pieces += [jnp.zeros((CH, 32), BF)]
            ps[side, half] = jnp.concatenate(pieces, axis=1)

    pl.semaphore_wait(barrier, greetings)
    for start, _ in f_out + p_out + c_out:
        start()
    pass_on(0, [plane_peer(step) for step in row_steps])
    pass_on(1, [z_peer(1), z_peer(NZ - 1)])

    fetch[2].wait()
    fetch[3].wait()
    for t in range(9):
        w1c[:, CH * t:CH * (t + 1)] = raw_w1[t]
    w1t[...] = raw_w1[...].reshape(K, CH).T
    taps_of = [raw_w2[3 * a:3 * a + 3].reshape(3 * CH, CH).T for a in range(3)]
    for half in range(2):
        w2own[half] = jnp.concatenate([taps_of[1], taps_of[2 * half]], axis=1)
        w2halo[half] = taps_of[2 - 2 * half]

    acc2[...] = jnp.zeros_like(acc2)
    acc1[...] = jnp.zeros_like(acc1)

    def shift_left(x, h, at, d):
        return jnp.concatenate([x[:, d:], h[:, at:at + d]], axis=1)

    def shift_right(x, h, at, d):
        return jnp.concatenate([h[:, at:at + d], x[:, :TC - d]], axis=1)

    def f_row(blk, k, e):
        x = fs[1, e]
        fs[0, e] = shift_right(x, pleft[blk], 64 + 4 * k, 4)
        fs[2, e] = shift_left(x, pright[blk], 64 + 4 * k, 4)

    def c_row(blk, k):
        e = 8 * blk + k
        x = cs[1, e]
        cs[2, e] = shift_right(x, pleft[blk], 8 * k, 8)
        cs[0, e] = shift_left(x, pright[blk], 8 * k, 8)

    def taps(ref, rows):
        return [ref[b, e] for e in rows for b in range(3)]

    def stack(parts):
        return jnp.concatenate(parts, axis=0)

    receive(there(0, -1), pleft.at[pl.ds(1, 2)], p_recv.at[0])
    receive(there(0, 1), pright.at[pl.ds(1, 2)], p_recv.at[1])
    pl.semaphore_wait(ready.at[0], len(row_steps))
    pl.semaphore_wait(ready.at[1], 2)
    pass_on(2, [z_peer(2), z_peer(NZ - 2)])

    @pl.loop(1, 3)
    def _(blk):
        for k in range(8):
            f_row(blk, k, 8 * blk + k - 4)
            c_row(blk, k)

    def hidden_row(r):
        h = xf[r].astype(F32) + dot(w1c[...], stack(taps(fs, [r, r + 4, r + 8])))
        a2[r] = jnp.maximum(h.astype(BF), 0)

    @pl.loop(1, 3)
    def _(g):
        for k in range(4):
            hidden_row(4 * g + k)

    for half in range(2):
        @pl.loop(0, 2)
        def _(g):
            for k in range(4):
                r = 8 * half + 4 * g + k
                up_own[r] = dot(w2own[half], stack(taps(cs, [r + 8, r + 16 - 16 * half])))

    @pl.loop(0, 2)
    def _(i):
        half = (1 - core) + i * (2 * core - 1)
        ok = jnp.logical_or(jnp.logical_and(half == 0, l > 0), jnp.logical_and(half == 1, l < LONG - 1))
        receive(jnp.logical_and(ok, s > 0), pleft.at[pl.ds(3 * half, 1)], p_recv.at[2 + 2 * half])
        receive(jnp.logical_and(ok, s < SHORT - 1), pright.at[pl.ds(3 * half, 1)], p_recv.at[3 + 2 * half])
        receive(ok, fs.at[1, pl.ds(20 * half, 4)], f_recv.at[half])
        for k in range(4):
            e = 20 * half + k
            x = fs[1, e]
            for b, shift, pack in ((0, shift_right, pleft), (2, shift_left, pright)):
                low = shift(x, pack[3 * half], 64 + 4 * k, 4)
                high = shift(x, pack[3 * half], 64 + 4 * (k + 4), 4)
                fs[b, e] = jnp.where(half == 1, low, high)
        for k in range(4):
            hidden_row(12 * half + k)

        rows = [8 * half + k for k in range(8)]
        act = jnp.concatenate([a2[r] for r in rows], axis=1)
        own = nt_dot(
            jnp.concatenate([stack(taps(cs, [r + 8, r + 16 - 16 * half])) for r in rows], axis=1), act)
        acc2[1] += own[:3 * CH]
        acc2[2 * half] += own[3 * CH:]

        receive(ok, cs.at[1, pl.ds(24 * half, 8)], c_recv.at[half])
        for k in range(8):
            c_row(3 * half, k)
        beyond = [stack(taps(cs, [24 * half + k])) for k in range(8)]
        for k, r in enumerate(rows):
            up = up_own[r] + dot(w2halo[half], beyond[k])
            gh = cs[1, r + 8].astype(F32) + jnp.where(a2[r].astype(F32) > 0, up, 0.0)
            gs[1, r + 4] = gh.astype(BF)
        acc2[2 - 2 * half] += nt_dot(jnp.concatenate(beyond, axis=1), act)
        acc1[...] += nt_dot(
            jnp.concatenate([gs[1, r + 4] for r in rows], axis=1),
            jnp.concatenate([stack(taps(fs, [r, r + 4, r + 8])) for r in rows], axis=1))

    for t in range(9):
        gb[CH * t:CH * (t + 1), :] = jnp.concatenate(
            [acc2[t // 3, CH * (t % 3):CH * (t % 3 + 1), :], acc1[:, CH * t:CH * (t + 1)]], axis=1).astype(BF)

    def a_copy(j):
        owner = OWNERS[j]
        slot = lax.rem(place - owner + PLANE - 1, PLANE)
        return pltpu.make_async_remote_copy(
            src_ref=gb.at[pl.ds(CHUNK * j, CHUNK)], dst_ref=ra.at[slot],
            send_sem=a_send.at[j], recv_sem=a_recv,
            device_id=(base + owner, s), device_id_type=MESH)

    for j in range(NCHUNK):
        pl.when(place != OWNERS[j])(lambda j=j: a_copy(j).start())
    pl.semaphore_wait(ready.at[2], 2)

    for start, _ in g_out[:2]:
        start()
    for side in range(2):
        c4 = 0 if side == 0 else TC - 4
        pieces = [gs[1, 4 + k][:, c4:c4 + 4] for k in range(16)] + [jnp.zeros((CH, 64), BF)]
        gps[side] = jnp.concatenate(pieces, axis=1)
    for start, _ in g_out[2:]:
        start()

    mine = jnp.int32(0)
    is_owner = place < 0
    for j, owner in enumerate(OWNERS):
        mine = jnp.where(place == owner, j, mine)
        is_owner = jnp.logical_or(is_owner, place == owner)
    my_rows = pl.ds(pl.multiple_of(CHUNK * mine, CHUNK), CHUNK)

    def b_copy(k):
        return pltpu.make_async_remote_copy(
            src_ref=rb.at[0], dst_ref=rb.at[k], send_sem=b_send.at[k - 1], recv_sem=b_recv.at[k - 1],
            device_id=z_peer(k), device_id_type=MESH)

    def o_copy(n):
        return pltpu.make_async_remote_copy(
            src_ref=fin.at[my_rows], dst_ref=fin.at[my_rows], send_sem=o_send.at[n],
            recv_sem=o_recv.at[mine], device_id=plane_peer(PLANE_STEPS[n]), device_id_type=MESH)

    @pl.when(is_owner)
    def _():
        arrived(ra, a_recv)
        total = gb[my_rows, :].astype(F32)
        for i in range(PLANE - 1):
            total += ra[i].astype(F32)
        rb[0] = total.astype(BF)
        for k in Z_STEPS:
            b_copy(k).start()

    receive(there(-1, 0), gs.at[1, pl.ds(0, 4)], g_recv.at[6])
    receive(there(1, 0), gs.at[1, pl.ds(20, 4)], g_recv.at[7])
    for side, (ds, into) in enumerate(((-1, gleft), (1, gright))):
        receive(there(0, ds), into.at[1], g_recv.at[side])
        receive(there(-1, ds), into.at[0], g_recv.at[2 + side])
        receive(there(1, ds), into.at[2], g_recv.at[4 + side])

    def g_row(blk, e, at):
        x = gs[1, e]
        gs[2, e] = shift_right(x, gleft[blk], at, 4)
        gs[0, e] = shift_left(x, gright[blk], at, 4)

    for k in range(16):
        g_row(1, 4 + k, 4 * k)
    for k in range(4):
        g_row(0, k, 4 * (12 + k))
        g_row(2, 20 + k, 4 * k)

    @pl.loop(0, TR // 4)
    def _(g):
        for k in range(4):
            r = 4 * g + k
            back = dot(w1t[...], stack(taps(gs, [r + 8, r + 4, r])))
            out = gs[1, r + 4].astype(F32) + jnp.where(xf[r].astype(F32) > 0, back, 0.0)
            xf[r] = out.astype(BF)

    raw_f[...] = jnp.swapaxes(xf[...], 0, 1)
    write_gf = pltpu.make_async_copy(raw_f, gf_ref, out_sem.at[0])
    write_gf.start()

    @pl.when(is_owner)
    def _():
        full = rb[0].astype(F32)
        for k in reversed(Z_STEPS):
            b_copy(k).wait_recv()
            full += rb[k].astype(F32)
        fin[my_rows, :] = (full * scale).astype(BF)
        for n in range(PLANE - 1):
            o_copy(n).start()

    for _, sent in f_out + p_out + c_out + g_out:
        sent()
    for j in range(NCHUNK):
        pl.when(place != OWNERS[j])(lambda j=j: a_copy(j).wait_send())

    for j in range(NCHUNK):
        pl.when(place != OWNERS[j])(
            lambda j=j: arrived(fin.at[pl.ds(CHUNK * j, CHUNK)], o_recv.at[j]))
    write_gr = pltpu.make_async_copy(fin, gr_ref, out_sem.at[1])
    write_gr.start()

    @pl.when(is_owner)
    def _():
        for k in Z_STEPS:
            b_copy(k).wait_send()
        for n in range(PLANE - 1):
            o_copy(n).wait_send()

    write_gf.wait()
    write_gr.wait()


def finish(gf_hbm, gr_hbm, out_hbm, first_hbm, second_hbm, gf, gr, first, second, load, store):
    parts = 4
    step = CH // parts
    read = pltpu.make_async_copy(gr_hbm, gr, load.at[parts])
    read.start()
    blocks = [pl.ds(i * step, step) for i in range(parts)]
    loads = [pltpu.make_async_copy(gf_hbm.at[b], gf.at[b], load.at[i]) for i, b in enumerate(blocks)]
    stores = [pltpu.make_async_copy(gf.at[b], out_hbm.at[b], store.at[i]) for i, b in enumerate(blocks)]
    for copy in loads:
        copy.start()
    read.wait()
    both = gr[...].astype(F32).reshape(9, CH, 2 * CH)
    first[...] = both[:, :, CH:]
    second[...] = both[:, :, :CH]
    stores.append(pltpu.make_async_copy(first, first_hbm, store.at[parts]))
    stores.append(pltpu.make_async_copy(second, second_hbm, store.at[parts + 1]))
    stores[parts].start()
    stores[parts + 1].start()
    for i in range(parts):
        loads[i].wait()
        stores[i].start()
    for copy in stores:
        copy.wait()


def shards(field, cotangent, first_filter, second_filter):
    scale = 1.0 / math.sqrt(TR * LONG * TC * SHORT)
    hbm = pl.BlockSpec(memory_space=pltpu.HBM)
    vmem = pl.BlockSpec(memory_space=pltpu.VMEM)
    dma = pltpu.SemaphoreType.DMA

    def buf(*shape, dtype=BF):
        return pltpu.VMEM(shape, dtype)

    gf, gr = pl.pallas_call(
        lambda *refs: kernel(scale, *refs),
        out_shape=(jax.ShapeDtypeStruct((CH, TR, TC), BF), jax.ShapeDtypeStruct((K, 2 * CH), BF)),
        in_specs=[hbm] * 4,
        out_specs=(hbm, hbm),
        scratch_shapes=[
            buf(CH, TR, TC), buf(CH, TR, TC), buf(9, CH, CH), buf(9, CH, CH),
            buf(TR, CH, TC), buf(TR, CH, TC),
            buf(3, TR + 8, CH, TC), buf(3, TR + 16, CH, TC), buf(3, TR + 8, CH, TC),
            buf(2, 2, CH, 128), buf(4, CH, 128), buf(4, CH, 128),
            buf(2, CH, 128), buf(3, CH, 128), buf(3, CH, 128),
            buf(CH, K), buf(CH, K), buf(2, CH, 6 * CH), buf(2, CH, 3 * CH),
            buf(TR, CH, TC, dtype=F32),
            buf(3, 3 * CH, CH, dtype=F32), buf(CH, K, dtype=F32), buf(K, 2 * CH),
            buf(PLANE - 1, CHUNK, 2 * CH), buf(NZ, CHUNK, 2 * CH), buf(K, 2 * CH),
            dma((4,)),
            dma((2,)), dma((2,)), dma((2,)), dma((2,)), dma((6,)), dma((6,)), dma((8,)), dma((8,)),
            dma((NCHUNK,)), dma, dma((NZ - 1,)), dma((NZ - 1,)), dma((PLANE - 1,)), dma((NCHUNK,)),
            pltpu.SemaphoreType.REGULAR((3,)), dma((2,)),
        ],
        compiler_params=pltpu.CompilerParams(
            collective_id=0, has_side_effects=True, vmem_limit_bytes=60 << 20),
        name="dilated_backward",
    )(field, cotangent, first_filter, second_filter)
    taps = jax.ShapeDtypeStruct((9, CH, CH), F32)
    return pl.pallas_call(
        finish,
        out_shape=(jax.ShapeDtypeStruct((CH, TR, TC), BF), taps, taps),
        in_specs=[hbm, hbm],
        out_specs=(hbm, hbm, hbm),
        scratch_shapes=[
            buf(CH, TR, TC), buf(K, 2 * CH), buf(9, CH, CH, dtype=F32), buf(9, CH, CH, dtype=F32), dma((5,)), dma((6,))],
        compiler_params=pltpu.CompilerParams(vmem_limit_bytes=60 << 20),
        name="finish",
    )(gf, gr)


def solution(mesh):
    in_specs = (P(None, "long", "short"), P(None, "long", "short"), P(), P())
    out_specs = (P(None, "long", "short"), P(), P())
    return jax.shard_map(shards, mesh=mesh, in_specs=in_specs, out_specs=out_specs, check_vma=False)
```

```python
import math

import jax
import jax.numpy as jnp
from jax import lax
from jax.experimental import pallas as pl
from jax.experimental.pallas import tpu as pltpu
from jax.sharding import PartitionSpec as P

BF = jnp.bfloat16
F32 = jnp.float32
MESH = pl.DeviceIdType.MESH
CH, TR, TC = 64, 16, 256
K = 9 * CH
LONG, SHORT = 64, 4
PLANE = 32
NZ = LONG // PLANE * SHORT
CHUNK = 32
NCHUNK = K // CHUNK
OWNERS = (8, 9, 22, 23, 2, 28, 16, 17, 4, 5, 14, 15, 26, 27, 24, 25, 6, 7)

NEAR = ((-1, 0), (1, 0), (0, -1), (0, 1), (-1, -1), (-1, 1), (1, -1), (1, 1))


def ring_distance(a, n):
    return min(a % n, -a % n)


PLANE_STEPS = sorted(
    [(y, x, c) for y in range(4) for x in range(4) for c in range(2) if (y, x, c) != (0, 0, 0)],
    key=lambda t: -(ring_distance(t[0], 4) + ring_distance(t[1], 4)))
Z_STEPS = sorted(range(1, NZ), key=lambda k: -ring_distance(k, NZ))


def nt_dot(a, b):
    return lax.dot_general(a, b, (((1,), (1,)), ((), ())), preferred_element_type=F32)


def dot(a, b):
    return jnp.dot(a, b, preferred_element_type=F32)


def arrived(ref, sem):
    pltpu.make_async_copy(ref, ref, sem).wait()


def kernel(scale, field_hbm, cot_hbm, w1_hbm, w2_hbm, gf_ref, gr_ref,
           raw_f, raw_c, raw_w1, raw_w2, xf, a2, fs, cs, gs, ps, pleft, pright, gps, gleft, gright,
           w1c, w1t, w2own, w2halo, up_own, acc2, acc1, gb, ra, rb, fin, in_sem,
           f_send, f_recv, c_send, c_recv, p_send, p_recv, g_send, g_recv,
           a_send, a_recv, b_send, b_recv, o_send, o_recv, ready, out_sem,
           relay, r_send, r_recv, w_send, w_recv):
    l = lax.axis_index("long")
    s = lax.axis_index("short")
    place = lax.rem(l, PLANE)
    base = l - place
    core = lax.rem(l, 2)
    z = lax.div(l, PLANE) * SHORT + s

    fetch = [pltpu.make_async_copy(src, dst, in_sem.at[i]) for i, (src, dst) in enumerate(
        ((field_hbm, raw_f), (cot_hbm, raw_c), (w1_hbm, raw_w1), (w2_hbm, raw_w2)))]
    for copy in fetch:
        copy.start()

    barrier = pltpu.get_barrier_semaphore()

    def greet(dev):
        pl.semaphore_signal(barrier, inc=1, device_id=dev, device_id_type=MESH)

    def there(dl, ds):
        ok = None
        for d, at, n in ((dl, l, LONG), (ds, s, SHORT)):
            if d == 0:
                continue
            here = at + d >= 0 if d < 0 else at + d < n
            ok = here if ok is None else jnp.logical_and(ok, here)
        return ok

    def plane_peer(step):
        y, x, c = step
        py = lax.rem(lax.div(place, 8) + y, 4)
        px = lax.rem(lax.div(place, 2) + x, 4)
        return base + py * 8 + px * 2 + lax.rem(core + c, 2), s

    def z_peer(k):
        other = lax.rem(z + k, NZ)
        return lax.div(other, SHORT) * PLANE + place, lax.rem(other, SHORT)

    row_steps = [step for step in PLANE_STEPS if step[0] == 0]
    column_steps = [step for step in PLANE_STEPS if step[1:] == (0, 0)]
    first = [plane_peer(step) for step in row_steps + column_steps] + [z_peer(1), z_peer(NZ - 1)]
    greetings = jnp.int32(len(first))
    for dl, ds in NEAR:
        pl.when(there(dl, ds))(lambda dl=dl, ds=ds: greet((l + dl, s + ds)))
        greetings = greetings + there(dl, ds).astype(jnp.int32)
    for dev in first:
        greet(dev)

    def pass_on(n, devs):
        for dev in devs:
            pl.semaphore_signal(ready.at[n], inc=1, device_id=dev, device_id_type=MESH)

    def message(dl, ds, src, dst, send_sem, recv_sem, only=None):
        copy = pltpu.make_async_remote_copy(
            src_ref=src, dst_ref=dst, send_sem=send_sem, recv_sem=recv_sem,
            device_id=(l + dl, s + ds), device_id_type=MESH)
        ok = there(dl, ds) if only is None else only
        return (lambda: pl.when(ok)(lambda: copy.start()),
                lambda: pl.when(ok)(lambda: copy.wait_send()))

    def receive(ok, dst, sem):
        pl.when(ok)(lambda: arrived(dst, sem))

        @pl.when(jnp.logical_not(ok))
        def _():
            dst[...] = jnp.zeros(dst.shape, dst.dtype)

    f_out = [message(-1, 0, fs.at[1, pl.ds(4, 4)], fs.at[1, pl.ds(20, 4)], f_send.at[0], f_recv.at[1]),
             message(1, 0, fs.at[1, pl.ds(16, 4)], fs.at[1, pl.ds(0, 4)], f_send.at[1], f_recv.at[0])]
    seam_down = jnp.logical_and(place == PLANE - 1, l < LONG - 1)
    seam_up = jnp.logical_and(place == 0, l > 0)
    up, down = jnp.logical_and(l > 0, place != 0), jnp.logical_and(l < LONG - 1, place != PLANE - 1)
    c_out = [message(-1, 0, cs.at[1, pl.ds(8, 8)], cs.at[1, pl.ds(24, 8)], c_send.at[0], c_recv.at[1], up),
             message(1, 0, cs.at[1, pl.ds(16, 8)], cs.at[1, pl.ds(0, 8)], c_send.at[1], c_recv.at[0], down),
             message(-1, 0, cs.at[1, pl.ds(8, 4)], cs.at[1, pl.ds(24, 4)], c_send.at[0], c_recv.at[1], seam_up),
             message(1, 0, cs.at[1, pl.ds(16, 4)], cs.at[1, pl.ds(0, 4)], c_send.at[1], c_recv.at[0], seam_down)]
    relay_out, relay_on = [], []
    for n, hop in enumerate((2, 8)):
        for at_seam, way, low in ((seam_down, 1, 16), (seam_up, -1, 8)):
            rows = pl.ds(low + 4 + 2 * n, 2)
            relay_out.append(message(-way * hop, 0, cs.at[1, rows], relay, r_send.at[n], r_recv, at_seam))
            end = PLANE - 1 - hop if way == 1 else hop
            here = jnp.logical_and(place == end, l < PLANE if way == 1 else l >= LONG - PLANE)
            into = pl.ds((0 if way == 1 else 24) + 4 + 2 * n, 2)
            relay_on.append((here, message(
                way * (hop + 1), 0, relay, cs.at[1, into], w_send, w_recv.at[n], here)))
    g_out = [message(-1, 0, gs.at[1, pl.ds(4, 4)], gs.at[1, pl.ds(20, 4)], g_send.at[0], g_recv.at[7]),
             message(1, 0, gs.at[1, pl.ds(16, 4)], gs.at[1, pl.ds(0, 4)], g_send.at[1], g_recv.at[6])]
    p_out = []
    for side, (ds, into, g_into) in enumerate(((-1, pright, gright), (1, pleft, gleft))):
        p_out.append(message(0, ds, ps.at[side], into.at[pl.ds(1, 2)], p_send.at[side], p_recv.at[1 - side]))
        g_out.append(message(0, ds, gps.at[side], g_into.at[1], g_send.at[2 + side], g_recv.at[1 - side]))
    for half, dl in ((0, -1), (1, 1)):
        for side, (ds, into, g_into) in enumerate(((-1, pright, gright), (1, pleft, gleft))):
            out, back = 2 + 2 * half + side, 2 + 2 * (1 - half) + 1 - side
            p_out.append(message(
                dl, ds, ps.at[side, pl.ds(half, 1)], into.at[pl.ds(3 - 3 * half, 1)], p_send.at[out], p_recv.at[back]))
            g_out.append(message(
                dl, ds, gps.at[side], g_into.at[2 - 2 * half], g_send.at[2 + out], g_recv.at[back]))

    fetch[0].wait()
    own_f = jnp.swapaxes(raw_f[...], 0, 1)
    xf[...] = own_f
    fs[1, 4:20] = jnp.maximum(own_f, 0)
    fetch[1].wait()
    cs[1, 8:24] = jnp.swapaxes(raw_c[...], 0, 1)
    for half in range(2):
        for side in range(2):
            c8 = 0 if side == 0 else TC - 8
            c4 = 0 if side == 0 else TC - 4
            pieces = [cs[1, 8 + 8 * half + k][:, c8:c8 + 8] for k in range(8)]
            pieces += [fs[1, 4 + 8 * half + k][:, c4:c4 + 4] for k in range(8)]
            pieces += [jnp.zeros((CH, 32), BF)]
            ps[side, half] = jnp.concatenate(pieces, axis=1)

    pl.semaphore_wait(barrier, greetings)
    for start, _ in relay_out + f_out + p_out + c_out:
        start()
    pass_on(0, [plane_peer(step) for step in row_steps])
    pass_on(1, [z_peer(1), z_peer(NZ - 1)])

    fetch[2].wait()
    fetch[3].wait()
    for t in range(9):
        w1c[:, CH * t:CH * (t + 1)] = raw_w1[t]
    w1t[...] = raw_w1[...].reshape(K, CH).T
    taps_of = [raw_w2[3 * a:3 * a + 3].reshape(3 * CH, CH).T for a in range(3)]
    for half in range(2):
        w2own[half] = jnp.concatenate([taps_of[1], taps_of[2 * half]], axis=1)
        w2halo[half] = taps_of[2 - 2 * half]

    acc2[...] = jnp.zeros_like(acc2)
    acc1[...] = jnp.zeros_like(acc1)

    def shift_left(x, h, at, d):
        return jnp.concatenate([x[:, d:], h[:, at:at + d]], axis=1)

    def shift_right(x, h, at, d):
        return jnp.concatenate([h[:, at:at + d], x[:, :TC - d]], axis=1)

    def f_row(blk, k, e):
        x = fs[1, e]
        fs[0, e] = shift_right(x, pleft[blk], 64 + 4 * k, 4)
        fs[2, e] = shift_left(x, pright[blk], 64 + 4 * k, 4)

    def c_row(blk, k):
        e = 8 * blk + k
        x = cs[1, e]
        cs[2, e] = shift_right(x, pleft[blk], 8 * k, 8)
        cs[0, e] = shift_left(x, pright[blk], 8 * k, 8)

    def taps(ref, rows):
        return [ref[b, e] for e in rows for b in range(3)]

    def stack(parts):
        return jnp.concatenate(parts, axis=0)

    receive(there(0, -1), pleft.at[pl.ds(1, 2)], p_recv.at[0])
    receive(there(0, 1), pright.at[pl.ds(1, 2)], p_recv.at[1])
    for here, (start, _) in relay_on:
        pl.when(here)(lambda: arrived(relay, r_recv))
        start()
    pl.semaphore_wait(ready.at[0], len(row_steps))
    pl.semaphore_wait(ready.at[1], 2)
    pass_on(2, [z_peer(2), z_peer(NZ - 2)])

    @pl.loop(1, 3)
    def _(blk):
        for k in range(8):
            f_row(blk, k, 8 * blk + k - 4)
            c_row(blk, k)

    def hidden_row(r):
        h = xf[r].astype(F32) + dot(w1c[...], stack(taps(fs, [r, r + 4, r + 8])))
        a2[r] = jnp.maximum(h.astype(BF), 0)

    @pl.loop(1, 3)
    def _(g):
        for k in range(4):
            hidden_row(4 * g + k)

    for half in range(2):
        @pl.loop(0, 2)
        def _(g):
            for k in range(4):
                r = 8 * half + 4 * g + k
                up_own[r] = dot(w2own[half], stack(taps(cs, [r + 8, r + 16 - 16 * half])))

    @pl.loop(0, 2)
    def _(i):
        half = (1 - core) + i * (2 * core - 1)
        ok = jnp.logical_or(jnp.logical_and(half == 0, l > 0), jnp.logical_and(half == 1, l < LONG - 1))
        receive(jnp.logical_and(ok, s > 0), pleft.at[pl.ds(3 * half, 1)], p_recv.at[2 + 2 * half])
        receive(jnp.logical_and(ok, s < SHORT - 1), pright.at[pl.ds(3 * half, 1)], p_recv.at[3 + 2 * half])
        receive(ok, fs.at[1, pl.ds(20 * half, 4)], f_recv.at[half])
        for k in range(4):
            e = 20 * half + k
            x = fs[1, e]
            for b, shift, pack in ((0, shift_right, pleft), (2, shift_left, pright)):
                low = shift(x, pack[3 * half], 64 + 4 * k, 4)
                high = shift(x, pack[3 * half], 64 + 4 * (k + 4), 4)
                fs[b, e] = jnp.where(half == 1, low, high)
        for k in range(4):
            hidden_row(12 * half + k)

        rows = [8 * half + k for k in range(8)]
        act = jnp.concatenate([a2[r] for r in rows], axis=1)
        own = nt_dot(
            jnp.concatenate([stack(taps(cs, [r + 8, r + 16 - 16 * half])) for r in rows], axis=1), act)
        acc2[1] += own[:3 * CH]
        acc2[2 * half] += own[3 * CH:]

        far = jnp.logical_or(jnp.logical_and(half == 1, seam_down), jnp.logical_and(half == 0, seam_up))
        edge = 24 * half

        @pl.when(far)
        def _():
            arrived(cs.at[1, pl.ds(edge, 4)], c_recv.at[half])
            for n in range(2):
                arrived(cs.at[1, pl.ds(edge + 4 + 2 * n, 2)], w_recv.at[n])

        pl.when(jnp.logical_not(far))(lambda: receive(ok, cs.at[1, pl.ds(edge, 8)], c_recv.at[half]))
        for k in range(8):
            c_row(3 * half, k)
        beyond = [stack(taps(cs, [24 * half + k])) for k in range(8)]
        for k, r in enumerate(rows):
            up = up_own[r] + dot(w2halo[half], beyond[k])
            gh = cs[1, r + 8].astype(F32) + jnp.where(a2[r].astype(F32) > 0, up, 0.0)
            gs[1, r + 4] = gh.astype(BF)
        acc2[2 - 2 * half] += nt_dot(jnp.concatenate(beyond, axis=1), act)
        acc1[...] += nt_dot(
            jnp.concatenate([gs[1, r + 4] for r in rows], axis=1),
            jnp.concatenate([stack(taps(fs, [r, r + 4, r + 8])) for r in rows], axis=1))

    for t in range(9):
        gb[CH * t:CH * (t + 1), :] = jnp.concatenate(
            [acc2[t // 3, CH * (t % 3):CH * (t % 3 + 1), :], acc1[:, CH * t:CH * (t + 1)]], axis=1).astype(BF)

    def a_copy(j):
        owner = OWNERS[j]
        slot = lax.rem(place - owner + PLANE - 1, PLANE)
        return pltpu.make_async_remote_copy(
            src_ref=gb.at[pl.ds(CHUNK * j, CHUNK)], dst_ref=ra.at[slot],
            send_sem=a_send.at[j], recv_sem=a_recv,
            device_id=(base + owner, s), device_id_type=MESH)

    for j in range(NCHUNK):
        pl.when(place != OWNERS[j])(lambda j=j: a_copy(j).start())
    pl.semaphore_wait(ready.at[2], 2)

    for start, _ in g_out[:2]:
        start()
    for side in range(2):
        c4 = 0 if side == 0 else TC - 4
        pieces = [gs[1, 4 + k][:, c4:c4 + 4] for k in range(16)] + [jnp.zeros((CH, 64), BF)]
        gps[side] = jnp.concatenate(pieces, axis=1)
    for start, _ in g_out[2:]:
        start()

    receive(there(-1, 0), gs.at[1, pl.ds(0, 4)], g_recv.at[6])
    receive(there(1, 0), gs.at[1, pl.ds(20, 4)], g_recv.at[7])
    for side, (ds, into) in enumerate(((-1, gleft), (1, gright))):
        receive(there(0, ds), into.at[1], g_recv.at[side])
        receive(there(-1, ds), into.at[0], g_recv.at[2 + side])
        receive(there(1, ds), into.at[2], g_recv.at[4 + side])

    def g_row(blk, e, at):
        x = gs[1, e]
        gs[2, e] = shift_right(x, gleft[blk], at, 4)
        gs[0, e] = shift_left(x, gright[blk], at, 4)

    for k in range(16):
        g_row(1, 4 + k, 4 * k)
    for k in range(4):
        g_row(0, k, 4 * (12 + k))
        g_row(2, 20 + k, 4 * k)

    @pl.loop(0, TR // 4)
    def _(g):
        for k in range(4):
            r = 4 * g + k
            back = dot(w1t[...], stack(taps(gs, [r + 8, r + 4, r])))
            out = gs[1, r + 4].astype(F32) + jnp.where(xf[r].astype(F32) > 0, back, 0.0)
            xf[r] = out.astype(BF)

    raw_f[...] = jnp.swapaxes(xf[...], 0, 1)
    write_gf = pltpu.make_async_copy(raw_f, gf_ref, out_sem.at[0])
    write_gf.start()

    mine = jnp.int32(0)
    is_owner = place < 0
    for j, owner in enumerate(OWNERS):
        mine = jnp.where(place == owner, j, mine)
        is_owner = jnp.logical_or(is_owner, place == owner)
    my_rows = pl.ds(pl.multiple_of(CHUNK * mine, CHUNK), CHUNK)

    def b_copy(k):
        return pltpu.make_async_remote_copy(
            src_ref=rb.at[0], dst_ref=rb.at[k], send_sem=b_send.at[k - 1], recv_sem=b_recv.at[k - 1],
            device_id=z_peer(k), device_id_type=MESH)

    def o_copy(n):
        return pltpu.make_async_remote_copy(
            src_ref=fin.at[my_rows], dst_ref=fin.at[my_rows], send_sem=o_send.at[n],
            recv_sem=o_recv.at[mine], device_id=plane_peer(PLANE_STEPS[n]), device_id_type=MESH)

    @pl.when(is_owner)
    def _():
        arrived(ra, a_recv)
        total = gb[my_rows, :].astype(F32)
        for i in range(PLANE - 1):
            total += ra[i].astype(F32)
        rb[0] = total.astype(BF)
        for k in Z_STEPS:
            b_copy(k).start()

    @pl.when(is_owner)
    def _():
        full = rb[0].astype(F32)
        for k in reversed(Z_STEPS):
            b_copy(k).wait_recv()
            full += rb[k].astype(F32)
        fin[my_rows, :] = (full * scale).astype(BF)
        for n in range(PLANE - 1):
            o_copy(n).start()

    for _, sent in f_out + p_out + c_out + g_out + relay_out + [out for _, out in relay_on]:
        sent()
    for j in range(NCHUNK):
        pl.when(place != OWNERS[j])(lambda j=j: a_copy(j).wait_send())

    for j in range(NCHUNK):
        pl.when(place != OWNERS[j])(
            lambda j=j: arrived(fin.at[pl.ds(CHUNK * j, CHUNK)], o_recv.at[j]))
    write_gr = pltpu.make_async_copy(fin, gr_ref, out_sem.at[1])
    write_gr.start()

    @pl.when(is_owner)
    def _():
        for k in Z_STEPS:
            b_copy(k).wait_send()
        for n in range(PLANE - 1):
            o_copy(n).wait_send()

    write_gf.wait()
    write_gr.wait()


def finish(gf_hbm, gr_hbm, out_hbm, first_hbm, second_hbm, gf, gr, first, second, load, store):
    parts = 4
    step = CH // parts
    read = pltpu.make_async_copy(gr_hbm, gr, load.at[parts])
    read.start()
    blocks = [pl.ds(i * step, step) for i in range(parts)]
    loads = [pltpu.make_async_copy(gf_hbm.at[b], gf.at[b], load.at[i]) for i, b in enumerate(blocks)]
    stores = [pltpu.make_async_copy(gf.at[b], out_hbm.at[b], store.at[i]) for i, b in enumerate(blocks)]
    for copy in loads:
        copy.start()
    read.wait()
    both = gr[...].astype(F32).reshape(9, CH, 2 * CH)
    first[...] = both[:, :, CH:]
    second[...] = both[:, :, :CH]
    stores.append(pltpu.make_async_copy(first, first_hbm, store.at[parts]))
    stores.append(pltpu.make_async_copy(second, second_hbm, store.at[parts + 1]))
    stores[parts].start()
    stores[parts + 1].start()
    for i in range(parts):
        loads[i].wait()
        stores[i].start()
    for copy in stores:
        copy.wait()


def shards(field, cotangent, first_filter, second_filter):
    scale = 1.0 / math.sqrt(TR * LONG * TC * SHORT)
    hbm = pl.BlockSpec(memory_space=pltpu.HBM)
    vmem = pl.BlockSpec(memory_space=pltpu.VMEM)
    dma = pltpu.SemaphoreType.DMA

    def buf(*shape, dtype=BF):
        return pltpu.VMEM(shape, dtype)

    gf, gr = pl.pallas_call(
        lambda *refs: kernel(scale, *refs),
        out_shape=(jax.ShapeDtypeStruct((CH, TR, TC), BF), jax.ShapeDtypeStruct((K, 2 * CH), BF)),
        in_specs=[hbm] * 4,
        out_specs=(hbm, hbm),
        scratch_shapes=[
            buf(CH, TR, TC), buf(CH, TR, TC), buf(9, CH, CH), buf(9, CH, CH),
            buf(TR, CH, TC), buf(TR, CH, TC),
            buf(3, TR + 8, CH, TC), buf(3, TR + 16, CH, TC), buf(3, TR + 8, CH, TC),
            buf(2, 2, CH, 128), buf(4, CH, 128), buf(4, CH, 128),
            buf(2, CH, 128), buf(3, CH, 128), buf(3, CH, 128),
            buf(CH, K), buf(CH, K), buf(2, CH, 6 * CH), buf(2, CH, 3 * CH),
            buf(TR, CH, TC, dtype=F32),
            buf(3, 3 * CH, CH, dtype=F32), buf(CH, K, dtype=F32), buf(K, 2 * CH),
            buf(PLANE - 1, CHUNK, 2 * CH), buf(NZ, CHUNK, 2 * CH), buf(K, 2 * CH),
            dma((4,)),
            dma((2,)), dma((2,)), dma((2,)), dma((2,)), dma((6,)), dma((6,)), dma((8,)), dma((8,)),
            dma((NCHUNK,)), dma, dma((NZ - 1,)), dma((NZ - 1,)), dma((PLANE - 1,)), dma((NCHUNK,)),
            pltpu.SemaphoreType.REGULAR((3,)), dma((2,)),
            buf(2, CH, TC), dma((2,)), dma, dma, dma((2,)),
        ],
        compiler_params=pltpu.CompilerParams(
            collective_id=0, has_side_effects=True, vmem_limit_bytes=60 << 20),
        name="dilated_backward",
    )(field, cotangent, first_filter, second_filter)
    taps = jax.ShapeDtypeStruct((9, CH, CH), F32)
    return pl.pallas_call(
        finish,
        out_shape=(jax.ShapeDtypeStruct((CH, TR, TC), BF), taps, taps),
        in_specs=[hbm, hbm],
        out_specs=(hbm, hbm, hbm),
        scratch_shapes=[
            buf(CH, TR, TC), buf(K, 2 * CH), buf(9, CH, CH, dtype=F32), buf(9, CH, CH, dtype=F32), dma((5,)), dma((6,))],
        compiler_params=pltpu.CompilerParams(vmem_limit_bytes=60 << 20),
        name="finish",
    )(gf, gr)


def solution(mesh):
    in_specs = (P(None, "long", "short"), P(None, "long", "short"), P(), P())
    out_specs = (P(None, "long", "short"), P(), P())
    return jax.shard_map(shards, mesh=mesh, in_specs=in_specs, out_specs=out_specs, check_vma=False)
```

```python
import math

import jax
import jax.numpy as jnp
from jax import lax
from jax.experimental import pallas as pl
from jax.experimental.pallas import tpu as pltpu
from jax.sharding import PartitionSpec as P

BF = jnp.bfloat16
F32 = jnp.float32
MESH = pl.DeviceIdType.MESH
CH, TR, TC = 64, 16, 256
K = 9 * CH
LONG, SHORT = 64, 4
PLANE = 32
NZ = LONG // PLANE * SHORT
CHUNK = 32
NCHUNK = K // CHUNK
OWNERS = (10, 21, 12, 19, 2, 9, 22, 29, 4, 13, 15, 16, 27, 18, 6, 7, 24, 25)

NEAR = ((-1, 0), (1, 0), (0, -1), (0, 1), (-1, -1), (-1, 1), (1, -1), (1, 1))


PLANE_FLIPS = sorted(
    range(1, PLANE), key=lambda m: -((2 if m // 2 % 4 == 2 else min(m // 2 % 4, 1)) + (2 if m // 8 == 2 else min(m // 8, 1))))
ROW_FLIPS = [m for m in PLANE_FLIPS if m < 8]
COLUMN_FLIPS = [m for m in PLANE_FLIPS if m % 8 == 0]
Z_FLIPS = (4, 5, 3, 7, 6, 2, 1)


def nt_dot(a, b):
    return lax.dot_general(a, b, (((1,), (1,)), ((), ())), preferred_element_type=F32)


def dot(a, b):
    return jnp.dot(a, b, preferred_element_type=F32)


def arrived(ref, sem):
    pltpu.make_async_copy(ref, ref, sem).wait()


def kernel(scale, field_hbm, cot_hbm, w1_hbm, w2_hbm, gf_ref, gr_ref,
           raw_f, raw_c, raw_w1, raw_w2, xf, a2, fs, cs, gs, ps, pleft, pright, gps, gleft, gright,
           w1c, w1t, w2own, w2halo, up_own, acc2, acc1, gb, ra, rb, fin, in_sem,
           f_send, f_recv, c_send, c_recv, p_send, p_recv, g_send, g_recv,
           a_send, a_recv, b_send, b_recv, o_send, o_recv, ready, out_sem,
           relay, r_send, r_recv, w_send, w_recv):
    l = lax.axis_index("long")
    s = lax.axis_index("short")
    place = lax.rem(l, PLANE)
    base = l - place
    core = lax.rem(l, 2)
    z = lax.div(l, PLANE) * SHORT + s

    fetch = [pltpu.make_async_copy(src, dst, in_sem.at[i]) for i, (src, dst) in enumerate(
        ((field_hbm, raw_f), (cot_hbm, raw_c), (w1_hbm, raw_w1), (w2_hbm, raw_w2)))]
    for copy in fetch:
        copy.start()

    barrier = pltpu.get_barrier_semaphore()

    def greet(dev):
        pl.semaphore_signal(barrier, inc=1, device_id=dev, device_id_type=MESH)

    def there(dl, ds):
        ok = None
        for d, at, n in ((dl, l, LONG), (ds, s, SHORT)):
            if d == 0:
                continue
            here = at + d >= 0 if d < 0 else at + d < n
            ok = here if ok is None else jnp.logical_and(ok, here)
        return ok

    def flips(at, bits):
        return [b - 2 * b * lax.rem(lax.div(at, b), 2) for b in bits]

    place_flips = flips(place, (1, 2, 4, 8, 16))
    short_flips = flips(s, (1, 2))
    group_flip = PLANE - 2 * PLANE * lax.div(l, PLANE)

    def flipped(at, steps, m):
        for n, step in enumerate(steps):
            if m >> n & 1:
                at = at + step
        return at

    def plane_peer(m):
        return flipped(l, place_flips, m), s

    def z_flip(m):
        return (l + group_flip if m & 4 else l), flipped(s, short_flips, m & 3)

    def z_peer(k):
        other = lax.rem(z + k, NZ)
        return lax.div(other, SHORT) * PLANE + place, lax.rem(other, SHORT)

    first = [plane_peer(m) for m in ROW_FLIPS + COLUMN_FLIPS] + [z_peer(1), z_peer(NZ - 1)]
    greetings = jnp.int32(len(first))
    for dl, ds in NEAR:
        pl.when(there(dl, ds))(lambda dl=dl, ds=ds: greet((l + dl, s + ds)))
        greetings = greetings + there(dl, ds).astype(jnp.int32)
    for dev in first:
        greet(dev)

    def pass_on(n, devs):
        for dev in devs:
            pl.semaphore_signal(ready.at[n], inc=1, device_id=dev, device_id_type=MESH)

    def message(dl, ds, src, dst, send_sem, recv_sem, only=None):
        copy = pltpu.make_async_remote_copy(
            src_ref=src, dst_ref=dst, send_sem=send_sem, recv_sem=recv_sem,
            device_id=(l + dl, s + ds), device_id_type=MESH)
        ok = there(dl, ds) if only is None else only
        return (lambda: pl.when(ok)(lambda: copy.start()),
                lambda: pl.when(ok)(lambda: copy.wait_send()))

    def receive(ok, dst, sem):
        pl.when(ok)(lambda: arrived(dst, sem))

        @pl.when(jnp.logical_not(ok))
        def _():
            dst[...] = jnp.zeros(dst.shape, dst.dtype)

    f_out = [message(-1, 0, fs.at[1, pl.ds(4, 4)], fs.at[1, pl.ds(20, 4)], f_send.at[0], f_recv.at[1]),
             message(1, 0, fs.at[1, pl.ds(16, 4)], fs.at[1, pl.ds(0, 4)], f_send.at[1], f_recv.at[0])]
    seam_down = jnp.logical_and(place == PLANE - 1, l < LONG - 1)
    seam_up = jnp.logical_and(place == 0, l > 0)
    up, down = jnp.logical_and(l > 0, place != 0), jnp.logical_and(l < LONG - 1, place != PLANE - 1)
    c_out = [message(-1, 0, cs.at[1, pl.ds(8, 8)], cs.at[1, pl.ds(24, 8)], c_send.at[0], c_recv.at[1], up),
             message(1, 0, cs.at[1, pl.ds(16, 8)], cs.at[1, pl.ds(0, 8)], c_send.at[1], c_recv.at[0], down),
             message(-1, 0, cs.at[1, pl.ds(8, 4)], cs.at[1, pl.ds(24, 4)], c_send.at[0], c_recv.at[1], seam_up),
             message(1, 0, cs.at[1, pl.ds(16, 4)], cs.at[1, pl.ds(0, 4)], c_send.at[1], c_recv.at[0], seam_down)]
    relay_out, relay_on = [], []
    for n, hop in enumerate((2, 8)):
        for at_seam, way, low in ((seam_down, 1, 16), (seam_up, -1, 8)):
            rows = pl.ds(low + 4 + 2 * n, 2)
            relay_out.append(message(-way * hop, 0, cs.at[1, rows], relay, r_send.at[n], r_recv, at_seam))
            end = PLANE - 1 - hop if way == 1 else hop
            here = jnp.logical_and(place == end, l < PLANE if way == 1 else l >= LONG - PLANE)
            into = pl.ds((0 if way == 1 else 24) + 4 + 2 * n, 2)
            relay_on.append((here, message(
                way * (hop + 1), 0, relay, cs.at[1, into], w_send, w_recv.at[n], here)))
    g_out = [message(-1, 0, gs.at[1, pl.ds(4, 4)], gs.at[1, pl.ds(20, 4)], g_send.at[0], g_recv.at[7]),
             message(1, 0, gs.at[1, pl.ds(16, 4)], gs.at[1, pl.ds(0, 4)], g_send.at[1], g_recv.at[6])]
    p_out = []
    for side, (ds, into, g_into) in enumerate(((-1, pright, gright), (1, pleft, gleft))):
        p_out.append(message(0, ds, ps.at[side], into.at[pl.ds(1, 2)], p_send.at[side], p_recv.at[1 - side]))
        g_out.append(message(0, ds, gps.at[side], g_into.at[1], g_send.at[2 + side], g_recv.at[1 - side]))
    for half, dl in ((0, -1), (1, 1)):
        for side, (ds, into, g_into) in enumerate(((-1, pright, gright), (1, pleft, gleft))):
            out, back = 2 + 2 * half + side, 2 + 2 * (1 - half) + 1 - side
            p_out.append(message(
                dl, ds, ps.at[side, pl.ds(half, 1)], into.at[pl.ds(3 - 3 * half, 1)], p_send.at[out], p_recv.at[back]))
            g_out.append(message(
                dl, ds, gps.at[side], g_into.at[2 - 2 * half], g_send.at[2 + out], g_recv.at[back]))

    fetch[0].wait()
    own_f = jnp.swapaxes(raw_f[...], 0, 1)
    xf[...] = own_f
    fs[1, 4:20] = jnp.maximum(own_f, 0)
    fetch[1].wait()
    cs[1, 8:24] = jnp.swapaxes(raw_c[...], 0, 1)
    for half in range(2):
        for side in range(2):
            c8 = 0 if side == 0 else TC - 8
            c4 = 0 if side == 0 else TC - 4
            pieces = [cs[1, 8 + 8 * half + k][:, c8:c8 + 8] for k in range(8)]
            pieces += [fs[1, 4 + 8 * half + k][:, c4:c4 + 4] for k in range(8)]
            pieces += [jnp.zeros((CH, 32), BF)]
            ps[side, half] = jnp.concatenate(pieces, axis=1)

    pl.semaphore_wait(barrier, greetings)
    for start, _ in relay_out + f_out + p_out + c_out:
        start()
    pass_on(0, [plane_peer(m) for m in ROW_FLIPS])
    pass_on(1, [z_peer(1), z_peer(NZ - 1)])

    fetch[2].wait()
    fetch[3].wait()
    for t in range(9):
        w1c[:, CH * t:CH * (t + 1)] = raw_w1[t]
    w1t[...] = raw_w1[...].reshape(K, CH).T
    taps_of = [raw_w2[3 * a:3 * a + 3].reshape(3 * CH, CH).T for a in range(3)]
    for half in range(2):
        w2own[half] = jnp.concatenate([taps_of[1], taps_of[2 * half]], axis=1)
        w2halo[half] = taps_of[2 - 2 * half]

    acc2[...] = jnp.zeros_like(acc2)
    acc1[...] = jnp.zeros_like(acc1)

    def shift_left(x, h, at, d):
        return jnp.concatenate([x[:, d:], h[:, at:at + d]], axis=1)

    def shift_right(x, h, at, d):
        return jnp.concatenate([h[:, at:at + d], x[:, :TC - d]], axis=1)

    def f_row(blk, k, e):
        x = fs[1, e]
        fs[0, e] = shift_right(x, pleft[blk], 64 + 4 * k, 4)
        fs[2, e] = shift_left(x, pright[blk], 64 + 4 * k, 4)

    def c_row(blk, k):
        e = 8 * blk + k
        x = cs[1, e]
        cs[2, e] = shift_right(x, pleft[blk], 8 * k, 8)
        cs[0, e] = shift_left(x, pright[blk], 8 * k, 8)

    def taps(ref, rows):
        return [ref[b, e] for e in rows for b in range(3)]

    def stack(parts):
        return jnp.concatenate(parts, axis=0)

    receive(there(0, -1), pleft.at[pl.ds(1, 2)], p_recv.at[0])
    receive(there(0, 1), pright.at[pl.ds(1, 2)], p_recv.at[1])
    for here, (start, _) in relay_on:
        pl.when(here)(lambda: arrived(relay, r_recv))
        start()
    pl.semaphore_wait(ready.at[0], len(ROW_FLIPS))
    pl.semaphore_wait(ready.at[1], 2)
    pass_on(2, [z_peer(2), z_peer(NZ - 2)])

    @pl.loop(1, 3)
    def _(blk):
        for k in range(8):
            f_row(blk, k, 8 * blk + k - 4)
            c_row(blk, k)

    def hidden_row(r):
        h = xf[r].astype(F32) + dot(w1c[...], stack(taps(fs, [r, r + 4, r + 8])))
        a2[r] = jnp.maximum(h.astype(BF), 0)

    @pl.loop(1, 3)
    def _(g):
        for k in range(4):
            hidden_row(4 * g + k)

    for half in range(2):
        @pl.loop(0, 2)
        def _(g):
            for k in range(4):
                r = 8 * half + 4 * g + k
                up_own[r] = dot(w2own[half], stack(taps(cs, [r + 8, r + 16 - 16 * half])))

    @pl.loop(0, 2)
    def _(i):
        half = (1 - core) + i * (2 * core - 1)
        ok = jnp.logical_or(jnp.logical_and(half == 0, l > 0), jnp.logical_and(half == 1, l < LONG - 1))
        receive(jnp.logical_and(ok, s > 0), pleft.at[pl.ds(3 * half, 1)], p_recv.at[2 + 2 * half])
        receive(jnp.logical_and(ok, s < SHORT - 1), pright.at[pl.ds(3 * half, 1)], p_recv.at[3 + 2 * half])
        receive(ok, fs.at[1, pl.ds(20 * half, 4)], f_recv.at[half])
        for k in range(4):
            e = 20 * half + k
            x = fs[1, e]
            for b, shift, pack in ((0, shift_right, pleft), (2, shift_left, pright)):
                low = shift(x, pack[3 * half], 64 + 4 * k, 4)
                high = shift(x, pack[3 * half], 64 + 4 * (k + 4), 4)
                fs[b, e] = jnp.where(half == 1, low, high)
        for k in range(4):
            hidden_row(12 * half + k)

        rows = [8 * half + k for k in range(8)]
        act = jnp.concatenate([a2[r] for r in rows], axis=1)
        own = nt_dot(
            jnp.concatenate([stack(taps(cs, [r + 8, r + 16 - 16 * half])) for r in rows], axis=1), act)
        acc2[1] += own[:3 * CH]
        acc2[2 * half] += own[3 * CH:]

        far = jnp.logical_or(jnp.logical_and(half == 1, seam_down), jnp.logical_and(half == 0, seam_up))
        edge = 24 * half

        @pl.when(far)
        def _():
            arrived(cs.at[1, pl.ds(edge, 4)], c_recv.at[half])
            for n in range(2):
                arrived(cs.at[1, pl.ds(edge + 4 + 2 * n, 2)], w_recv.at[n])

        pl.when(jnp.logical_not(far))(lambda: receive(ok, cs.at[1, pl.ds(edge, 8)], c_recv.at[half]))
        for k in range(8):
            c_row(3 * half, k)
        beyond = [stack(taps(cs, [24 * half + k])) for k in range(8)]
        for k, r in enumerate(rows):
            up = up_own[r] + dot(w2halo[half], beyond[k])
            gh = cs[1, r + 8].astype(F32) + jnp.where(a2[r].astype(F32) > 0, up, 0.0)
            gs[1, r + 4] = gh.astype(BF)
        acc2[2 - 2 * half] += nt_dot(jnp.concatenate(beyond, axis=1), act)
        acc1[...] += nt_dot(
            jnp.concatenate([gs[1, r + 4] for r in rows], axis=1),
            jnp.concatenate([stack(taps(fs, [r, r + 4, r + 8])) for r in rows], axis=1))

    for t in range(9):
        gb[CH * t:CH * (t + 1), :] = jnp.concatenate(
            [acc2[t // 3, CH * (t % 3):CH * (t % 3 + 1), :], acc1[:, CH * t:CH * (t + 1)]], axis=1).astype(BF)

    def a_copy(j):
        owner = OWNERS[j]
        slot = place - (place > owner).astype(jnp.int32)
        return pltpu.make_async_remote_copy(
            src_ref=gb.at[pl.ds(CHUNK * j, CHUNK)], dst_ref=ra.at[slot],
            send_sem=a_send.at[j], recv_sem=a_recv,
            device_id=(base + owner, s), device_id_type=MESH)

    for j in range(NCHUNK):
        pl.when(place != OWNERS[j])(lambda j=j: a_copy(j).start())
    pl.semaphore_wait(ready.at[2], 2)

    for start, _ in g_out[:2]:
        start()
    for side in range(2):
        c4 = 0 if side == 0 else TC - 4
        pieces = [gs[1, 4 + k][:, c4:c4 + 4] for k in range(16)] + [jnp.zeros((CH, 64), BF)]
        gps[side] = jnp.concatenate(pieces, axis=1)
    for start, _ in g_out[2:]:
        start()

    receive(there(-1, 0), gs.at[1, pl.ds(0, 4)], g_recv.at[6])
    receive(there(1, 0), gs.at[1, pl.ds(20, 4)], g_recv.at[7])
    for side, (ds, into) in enumerate(((-1, gleft), (1, gright))):
        receive(there(0, ds), into.at[1], g_recv.at[side])
        receive(there(-1, ds), into.at[0], g_recv.at[2 + side])
        receive(there(1, ds), into.at[2], g_recv.at[4 + side])

    def g_row(blk, e, at):
        x = gs[1, e]
        gs[2, e] = shift_right(x, gleft[blk], at, 4)
        gs[0, e] = shift_left(x, gright[blk], at, 4)

    for k in range(16):
        g_row(1, 4 + k, 4 * k)
    for k in range(4):
        g_row(0, k, 4 * (12 + k))
        g_row(2, 20 + k, 4 * k)

    @pl.loop(0, TR // 4)
    def _(g):
        for k in range(4):
            r = 4 * g + k
            back = dot(w1t[...], stack(taps(gs, [r + 8, r + 4, r])))
            out = gs[1, r + 4].astype(F32) + jnp.where(xf[r].astype(F32) > 0, back, 0.0)
            xf[r] = out.astype(BF)

    raw_f[...] = jnp.swapaxes(xf[...], 0, 1)
    write_gf = pltpu.make_async_copy(raw_f, gf_ref, out_sem)
    write_gf.start()

    mine = jnp.int32(0)
    is_owner = place < 0
    for j, owner in enumerate(OWNERS):
        mine = jnp.where(place == owner, j, mine)
        is_owner = jnp.logical_or(is_owner, place == owner)
    my_rows = pl.ds(pl.multiple_of(CHUNK * mine, CHUNK), CHUNK)

    def b_copy(k):
        return pltpu.make_async_remote_copy(
            src_ref=rb.at[0], dst_ref=rb.at[k], send_sem=b_send.at[k - 1], recv_sem=b_recv.at[k - 1],
            device_id=z_flip(k), device_id_type=MESH)

    def o_copy(n):
        return pltpu.make_async_remote_copy(
            src_ref=fin.at[my_rows], dst_ref=fin.at[my_rows], send_sem=o_send.at[n],
            recv_sem=o_recv, device_id=plane_peer(PLANE_FLIPS[n]), device_id_type=MESH)

    @pl.when(is_owner)
    def _():
        arrived(ra, a_recv)
        total = gb[my_rows, :].astype(F32)
        for i in range(PLANE - 1):
            total += ra[i].astype(F32)
        rb[0] = total.astype(BF)
        for k in Z_FLIPS:
            b_copy(k).start()

    @pl.when(is_owner)
    def _():
        full = rb[0].astype(F32)
        for k in reversed(Z_FLIPS):
            b_copy(k).wait_recv()
            full += rb[k].astype(F32)
        fin[my_rows, :] = (full * scale).astype(BF)
        for n in range(PLANE - 1):
            o_copy(n).start()

    for _, sent in f_out + p_out + c_out + g_out + relay_out + [out for _, out in relay_on]:
        sent()
    for j in range(NCHUNK):
        pl.when(place != OWNERS[j])(lambda j=j: a_copy(j).wait_send())

    pl.when(is_owner)(lambda: arrived(fin.at[pl.ds(0, K - CHUNK)], o_recv))
    pl.when(jnp.logical_not(is_owner))(lambda: arrived(fin, o_recv))
    gr_ref[...] = fin[...]

    @pl.when(is_owner)
    def _():
        for k in Z_FLIPS:
            b_copy(k).wait_send()
        for n in range(PLANE - 1):
            o_copy(n).wait_send()

    write_gf.wait()


def finish(gf_hbm, gr, out_hbm, first_hbm, second_hbm, gf, first, second, load, store):
    parts = 4
    step = CH // parts
    blocks = [pl.ds(i * step, step) for i in range(parts)]
    loads = [pltpu.make_async_copy(gf_hbm.at[b], gf.at[b], load.at[i]) for i, b in enumerate(blocks)]
    stores = [pltpu.make_async_copy(gf.at[b], out_hbm.at[b], store.at[i]) for i, b in enumerate(blocks)]
    for copy in loads:
        copy.start()
    both = gr[...].astype(F32).reshape(9, CH, 2 * CH)
    first[...] = both[:, :, CH:]
    second[...] = both[:, :, :CH]
    stores.append(pltpu.make_async_copy(first, first_hbm, store.at[parts]))
    stores.append(pltpu.make_async_copy(second, second_hbm, store.at[parts + 1]))
    stores[parts].start()
    stores[parts + 1].start()
    for i in range(parts):
        loads[i].wait()
        stores[i].start()
    for copy in stores:
        copy.wait()


def shards(field, cotangent, first_filter, second_filter):
    scale = 1.0 / math.sqrt(TR * LONG * TC * SHORT)
    hbm = pl.BlockSpec(memory_space=pltpu.HBM)
    vmem = pl.BlockSpec(memory_space=pltpu.VMEM)
    dma = pltpu.SemaphoreType.DMA

    def buf(*shape, dtype=BF):
        return pltpu.VMEM(shape, dtype)

    gf, gr = pl.pallas_call(
        lambda *refs: kernel(scale, *refs),
        out_shape=(jax.ShapeDtypeStruct((CH, TR, TC), BF), jax.ShapeDtypeStruct((K, 2 * CH), BF)),
        in_specs=[hbm] * 4,
        out_specs=(hbm, vmem),
        scratch_shapes=[
            buf(CH, TR, TC), buf(CH, TR, TC), buf(9, CH, CH), buf(9, CH, CH),
            buf(TR, CH, TC), buf(TR, CH, TC),
            buf(3, TR + 8, CH, TC), buf(3, TR + 16, CH, TC), buf(3, TR + 8, CH, TC),
            buf(2, 2, CH, 128), buf(4, CH, 128), buf(4, CH, 128),
            buf(2, CH, 128), buf(3, CH, 128), buf(3, CH, 128),
            buf(CH, K), buf(CH, K), buf(2, CH, 6 * CH), buf(2, CH, 3 * CH),
            buf(TR, CH, TC, dtype=F32),
            buf(3, 3 * CH, CH, dtype=F32), buf(CH, K, dtype=F32), buf(K, 2 * CH),
            buf(PLANE - 1, CHUNK, 2 * CH), buf(NZ, CHUNK, 2 * CH), buf(K, 2 * CH),
            dma((4,)),
            dma((2,)), dma((2,)), dma((2,)), dma((2,)), dma((6,)), dma((6,)), dma((8,)), dma((8,)),
            dma((NCHUNK,)), dma, dma((NZ - 1,)), dma((NZ - 1,)), dma((PLANE - 1,)), dma,
            pltpu.SemaphoreType.REGULAR((3,)), dma,
            buf(2, CH, TC), dma((2,)), dma, dma, dma((2,)),
        ],
        compiler_params=pltpu.CompilerParams(
            collective_id=0, has_side_effects=True, vmem_limit_bytes=215 << 18),
        name="dilated_backward",
    )(field, cotangent, first_filter, second_filter)
    taps = jax.ShapeDtypeStruct((9, CH, CH), F32)
    return pl.pallas_call(
        finish,
        out_shape=(jax.ShapeDtypeStruct((CH, TR, TC), BF), taps, taps),
        in_specs=[hbm, vmem],
        out_specs=(hbm, hbm, hbm),
        scratch_shapes=[
            buf(CH, TR, TC), buf(9, CH, CH, dtype=F32), buf(9, CH, CH, dtype=F32), dma((4,)), dma((6,))],
        compiler_params=pltpu.CompilerParams(vmem_limit_bytes=215 << 18),
        name="finish",
    )(gf, gr)


def solution(mesh):
    in_specs = (P(None, "long", "short"), P(None, "long", "short"), P(), P())
    out_specs = (P(None, "long", "short"), P(), P())
    return jax.shard_map(shards, mesh=mesh, in_specs=in_specs, out_specs=out_specs, check_vma=False)
```

```python
import math

import jax
import jax.numpy as jnp
from jax import lax
from jax.experimental import pallas as pl
from jax.experimental.pallas import tpu as pltpu
from jax.sharding import PartitionSpec as P

BF = jnp.bfloat16
F32 = jnp.float32
MESH = pl.DeviceIdType.MESH
CH, TR, TC = 64, 16, 256
K = 9 * CH
LONG, SHORT = 64, 4
PLANE = 32
NZ = LONG // PLANE * SHORT
CHUNK = 32
NCHUNK = K // CHUNK
OWNERS = (10, 21, 12, 19, 2, 9, 22, 29, 4, 13, 15, 16, 27, 18, 6, 7, 24, 25)

NEAR = ((-1, 0), (1, 0), (0, -1), (0, 1), (-1, -1), (-1, 1), (1, -1), (1, 1))


PLANE_FLIPS = sorted(
    range(1, PLANE), key=lambda m: -((2 if m // 2 % 4 == 2 else min(m // 2 % 4, 1)) + (2 if m // 8 == 2 else min(m // 8, 1))))
ROW_FLIPS = [m for m in PLANE_FLIPS if m < 8]
COLUMN_FLIPS = [m for m in PLANE_FLIPS if m % 8 == 0]
Z_FLIPS = (4, 5, 3, 7, 6, 2, 1)


def nt_dot(a, b):
    return lax.dot_general(a, b, (((1,), (1,)), ((), ())), preferred_element_type=F32)


def dot(a, b):
    return jnp.dot(a, b, preferred_element_type=F32)


def arrived(ref, sem):
    pltpu.make_async_copy(ref, ref, sem).wait()


def kernel(scale, field_hbm, cot_hbm, w1_hbm, w2_hbm, both_ref,
           raw_f, raw_c, raw_w1, raw_w2, xf, a2, fs, cs, gs, ps, pleft, pright, gps, gleft, gright,
           w1c, w1t, w2own, w2halo, up_own, acc2, acc1, gb, ra, rb, fin, in_sem,
           f_send, f_recv, c_send, c_recv, p_send, p_recv, g_send, g_recv,
           a_send, a_recv, b_send, b_recv, o_send, o_recv, ready,
           relay, r_send, r_recv, w_send, w_recv):
    l = lax.axis_index("long")
    s = lax.axis_index("short")
    place = lax.rem(l, PLANE)
    base = l - place
    core = lax.rem(l, 2)
    z = lax.div(l, PLANE) * SHORT + s

    fetch = [pltpu.make_async_copy(src, dst, in_sem.at[i]) for i, (src, dst) in enumerate(
        ((field_hbm, raw_f), (cot_hbm, raw_c), (w1_hbm, raw_w1), (w2_hbm, raw_w2)))]
    for copy in fetch:
        copy.start()

    barrier = pltpu.get_barrier_semaphore()

    def greet(dev):
        pl.semaphore_signal(barrier, inc=1, device_id=dev, device_id_type=MESH)

    def there(dl, ds):
        ok = None
        for d, at, n in ((dl, l, LONG), (ds, s, SHORT)):
            if d == 0:
                continue
            here = at + d >= 0 if d < 0 else at + d < n
            ok = here if ok is None else jnp.logical_and(ok, here)
        return ok

    def flips(at, bits):
        return [b - 2 * b * lax.rem(lax.div(at, b), 2) for b in bits]

    place_flips = flips(place, (1, 2, 4, 8, 16))
    short_flips = flips(s, (1, 2))
    group_flip = PLANE - 2 * PLANE * lax.div(l, PLANE)

    def flipped(at, steps, m):
        for n, step in enumerate(steps):
            if m >> n & 1:
                at = at + step
        return at

    def plane_peer(m):
        return flipped(l, place_flips, m), s

    def z_flip(m):
        return (l + group_flip if m & 4 else l), flipped(s, short_flips, m & 3)

    def z_peer(k):
        other = lax.rem(z + k, NZ)
        return lax.div(other, SHORT) * PLANE + place, lax.rem(other, SHORT)

    first = [plane_peer(m) for m in ROW_FLIPS + COLUMN_FLIPS] + [z_peer(1), z_peer(NZ - 1)]
    greetings = jnp.int32(len(first))
    for dl, ds in NEAR:
        pl.when(there(dl, ds))(lambda dl=dl, ds=ds: greet((l + dl, s + ds)))
        greetings = greetings + there(dl, ds).astype(jnp.int32)
    for dev in first:
        greet(dev)

    def pass_on(n, devs):
        for dev in devs:
            pl.semaphore_signal(ready.at[n], inc=1, device_id=dev, device_id_type=MESH)

    def message(dl, ds, src, dst, send_sem, recv_sem, only=None):
        copy = pltpu.make_async_remote_copy(
            src_ref=src, dst_ref=dst, send_sem=send_sem, recv_sem=recv_sem,
            device_id=(l + dl, s + ds), device_id_type=MESH)
        ok = there(dl, ds) if only is None else only
        return (lambda: pl.when(ok)(lambda: copy.start()),
                lambda: pl.when(ok)(lambda: copy.wait_send()))

    def receive(ok, dst, sem):
        pl.when(ok)(lambda: arrived(dst, sem))

        @pl.when(jnp.logical_not(ok))
        def _():
            dst[...] = jnp.zeros(dst.shape, dst.dtype)

    f_out = [message(-1, 0, fs.at[1, pl.ds(4, 4)], fs.at[1, pl.ds(20, 4)], f_send.at[0], f_recv.at[1]),
             message(1, 0, fs.at[1, pl.ds(16, 4)], fs.at[1, pl.ds(0, 4)], f_send.at[1], f_recv.at[0])]
    seam_down = jnp.logical_and(place == PLANE - 1, l < LONG - 1)
    seam_up = jnp.logical_and(place == 0, l > 0)
    up, down = jnp.logical_and(l > 0, place != 0), jnp.logical_and(l < LONG - 1, place != PLANE - 1)
    c_out = [message(-1, 0, cs.at[1, pl.ds(8, 8)], cs.at[1, pl.ds(24, 8)], c_send.at[0], c_recv.at[1], up),
             message(1, 0, cs.at[1, pl.ds(16, 8)], cs.at[1, pl.ds(0, 8)], c_send.at[1], c_recv.at[0], down),
             message(-1, 0, cs.at[1, pl.ds(8, 4)], cs.at[1, pl.ds(24, 4)], c_send.at[0], c_recv.at[1], seam_up),
             message(1, 0, cs.at[1, pl.ds(16, 4)], cs.at[1, pl.ds(0, 4)], c_send.at[1], c_recv.at[0], seam_down)]
    relay_out, relay_on = [], []
    for n, hop in enumerate((2, 8)):
        for at_seam, way, low in ((seam_down, 1, 16), (seam_up, -1, 8)):
            rows = pl.ds(low + 4 + 2 * n, 2)
            relay_out.append(message(-way * hop, 0, cs.at[1, rows], relay, r_send.at[n], r_recv, at_seam))
            end = PLANE - 1 - hop if way == 1 else hop
            here = jnp.logical_and(place == end, l < PLANE if way == 1 else l >= LONG - PLANE)
            into = pl.ds((0 if way == 1 else 24) + 4 + 2 * n, 2)
            relay_on.append((here, message(
                way * (hop + 1), 0, relay, cs.at[1, into], w_send, w_recv.at[n], here)))
    g_out = [message(-1, 0, gs.at[1, pl.ds(4, 4)], gs.at[1, pl.ds(20, 4)], g_send.at[0], g_recv.at[7]),
             message(1, 0, gs.at[1, pl.ds(16, 4)], gs.at[1, pl.ds(0, 4)], g_send.at[1], g_recv.at[6])]
    p_out = []
    for side, (ds, into, g_into) in enumerate(((-1, pright, gright), (1, pleft, gleft))):
        p_out.append(message(0, ds, ps.at[side], into.at[pl.ds(1, 2)], p_send.at[side], p_recv.at[1 - side]))
        g_out.append(message(0, ds, gps.at[side], g_into.at[1], g_send.at[2 + side], g_recv.at[1 - side]))
    for half, dl in ((0, -1), (1, 1)):
        for side, (ds, into, g_into) in enumerate(((-1, pright, gright), (1, pleft, gleft))):
            out, back = 2 + 2 * half + side, 2 + 2 * (1 - half) + 1 - side
            p_out.append(message(
                dl, ds, ps.at[side, pl.ds(half, 1)], into.at[pl.ds(3 - 3 * half, 1)], p_send.at[out], p_recv.at[back]))
            g_out.append(message(
                dl, ds, gps.at[side], g_into.at[2 - 2 * half], g_send.at[2 + out], g_recv.at[back]))

    fetch[0].wait()
    own_f = jnp.swapaxes(raw_f[...], 0, 1)
    xf[...] = own_f
    fs[1, 4:20] = jnp.maximum(own_f, 0)
    fetch[1].wait()
    cs[1, 8:24] = jnp.swapaxes(raw_c[...], 0, 1)
    for half in range(2):
        for side in range(2):
            c8 = 0 if side == 0 else TC - 8
            c4 = 0 if side == 0 else TC - 4
            pieces = [cs[1, 8 + 8 * half + k][:, c8:c8 + 8] for k in range(8)]
            pieces += [fs[1, 4 + 8 * half + k][:, c4:c4 + 4] for k in range(8)]
            pieces += [jnp.zeros((CH, 32), BF)]
            ps[side, half] = jnp.concatenate(pieces, axis=1)

    pl.semaphore_wait(barrier, greetings)
    for start, _ in relay_out + f_out + p_out + c_out:
        start()
    pass_on(0, [plane_peer(m) for m in ROW_FLIPS])
    pass_on(1, [z_peer(1), z_peer(NZ - 1)])

    fetch[2].wait()
    fetch[3].wait()
    for t in range(9):
        w1c[:, CH * t:CH * (t + 1)] = raw_w1[t]
    w1t[...] = raw_w1[...].reshape(K, CH).T
    taps_of = [raw_w2[3 * a:3 * a + 3].reshape(3 * CH, CH).T for a in range(3)]
    for half in range(2):
        w2own[half] = jnp.concatenate([taps_of[1], taps_of[2 * half]], axis=1)
        w2halo[half] = taps_of[2 - 2 * half]

    acc2[...] = jnp.zeros_like(acc2)
    acc1[...] = jnp.zeros_like(acc1)

    def shift_left(x, h, at, d):
        return jnp.concatenate([x[:, d:], h[:, at:at + d]], axis=1)

    def shift_right(x, h, at, d):
        return jnp.concatenate([h[:, at:at + d], x[:, :TC - d]], axis=1)

    def f_row(blk, k, e):
        x = fs[1, e]
        fs[0, e] = shift_right(x, pleft[blk], 64 + 4 * k, 4)
        fs[2, e] = shift_left(x, pright[blk], 64 + 4 * k, 4)

    def c_row(blk, k):
        e = 8 * blk + k
        x = cs[1, e]
        cs[2, e] = shift_right(x, pleft[blk], 8 * k, 8)
        cs[0, e] = shift_left(x, pright[blk], 8 * k, 8)

    def taps(ref, rows):
        return [ref[b, e] for e in rows for b in range(3)]

    def stack(parts):
        return jnp.concatenate(parts, axis=0)

    receive(there(0, -1), pleft.at[pl.ds(1, 2)], p_recv.at[0])
    receive(there(0, 1), pright.at[pl.ds(1, 2)], p_recv.at[1])
    for here, (start, _) in relay_on:
        pl.when(here)(lambda: arrived(relay, r_recv))
        start()
    pl.semaphore_wait(ready.at[0], len(ROW_FLIPS))
    pl.semaphore_wait(ready.at[1], 2)
    pass_on(2, [z_peer(2), z_peer(NZ - 2)])

    @pl.loop(1, 3)
    def _(blk):
        for k in range(8):
            f_row(blk, k, 8 * blk + k - 4)
            c_row(blk, k)

    def hidden_row(r):
        h = xf[r].astype(F32) + dot(w1c[...], stack(taps(fs, [r, r + 4, r + 8])))
        a2[r] = jnp.maximum(h.astype(BF), 0)

    @pl.loop(1, 3)
    def _(g):
        for k in range(4):
            hidden_row(4 * g + k)

    for half in range(2):
        @pl.loop(0, 2)
        def _(g):
            for k in range(4):
                r = 8 * half + 4 * g + k
                up_own[r] = dot(w2own[half], stack(taps(cs, [r + 8, r + 16 - 16 * half])))

    @pl.loop(0, 2)
    def _(i):
        half = (1 - core) + i * (2 * core - 1)
        ok = jnp.logical_or(jnp.logical_and(half == 0, l > 0), jnp.logical_and(half == 1, l < LONG - 1))
        receive(jnp.logical_and(ok, s > 0), pleft.at[pl.ds(3 * half, 1)], p_recv.at[2 + 2 * half])
        receive(jnp.logical_and(ok, s < SHORT - 1), pright.at[pl.ds(3 * half, 1)], p_recv.at[3 + 2 * half])
        receive(ok, fs.at[1, pl.ds(20 * half, 4)], f_recv.at[half])
        for k in range(4):
            e = 20 * half + k
            x = fs[1, e]
            for b, shift, pack in ((0, shift_right, pleft), (2, shift_left, pright)):
                low = shift(x, pack[3 * half], 64 + 4 * k, 4)
                high = shift(x, pack[3 * half], 64 + 4 * (k + 4), 4)
                fs[b, e] = jnp.where(half == 1, low, high)
        for k in range(4):
            hidden_row(12 * half + k)

        rows = [8 * half + k for k in range(8)]
        act = jnp.concatenate([a2[r] for r in rows], axis=1)
        own = nt_dot(
            jnp.concatenate([stack(taps(cs, [r + 8, r + 16 - 16 * half])) for r in rows], axis=1), act)
        acc2[1] += own[:3 * CH]
        acc2[2 * half] += own[3 * CH:]

        far = jnp.logical_or(jnp.logical_and(half == 1, seam_down), jnp.logical_and(half == 0, seam_up))
        edge = 24 * half

        @pl.when(far)
        def _():
            arrived(cs.at[1, pl.ds(edge, 4)], c_recv.at[half])
            for n in range(2):
                arrived(cs.at[1, pl.ds(edge + 4 + 2 * n, 2)], w_recv.at[n])

        pl.when(jnp.logical_not(far))(lambda: receive(ok, cs.at[1, pl.ds(edge, 8)], c_recv.at[half]))
        for k in range(8):
            c_row(3 * half, k)
        beyond = [stack(taps(cs, [24 * half + k])) for k in range(8)]
        for k, r in enumerate(rows):
            up = up_own[r] + dot(w2halo[half], beyond[k])
            gh = cs[1, r + 8].astype(F32) + jnp.where(a2[r].astype(F32) > 0, up, 0.0)
            gs[1, r + 4] = gh.astype(BF)
        acc2[2 - 2 * half] += nt_dot(jnp.concatenate(beyond, axis=1), act)
        acc1[...] += nt_dot(
            jnp.concatenate([gs[1, r + 4] for r in rows], axis=1),
            jnp.concatenate([stack(taps(fs, [r, r + 4, r + 8])) for r in rows], axis=1))

    for t in range(9):
        gb[CH * t:CH * (t + 1), :] = jnp.concatenate(
            [acc2[t // 3, CH * (t % 3):CH * (t % 3 + 1), :], acc1[:, CH * t:CH * (t + 1)]], axis=1).astype(BF)

    def a_copy(j):
        owner = OWNERS[j]
        slot = place - (place > owner).astype(jnp.int32)
        return pltpu.make_async_remote_copy(
            src_ref=gb.at[pl.ds(CHUNK * j, CHUNK)], dst_ref=ra.at[slot],
            send_sem=a_send.at[j], recv_sem=a_recv,
            device_id=(base + owner, s), device_id_type=MESH)

    for j in range(NCHUNK):
        pl.when(place != OWNERS[j])(lambda j=j: a_copy(j).start())
    pl.semaphore_wait(ready.at[2], 2)

    for start, _ in g_out[:2]:
        start()
    for side in range(2):
        c4 = 0 if side == 0 else TC - 4
        pieces = [gs[1, 4 + k][:, c4:c4 + 4] for k in range(16)] + [jnp.zeros((CH, 64), BF)]
        gps[side] = jnp.concatenate(pieces, axis=1)
    for start, _ in g_out[2:]:
        start()

    receive(there(-1, 0), gs.at[1, pl.ds(0, 4)], g_recv.at[6])
    receive(there(1, 0), gs.at[1, pl.ds(20, 4)], g_recv.at[7])
    for side, (ds, into) in enumerate(((-1, gleft), (1, gright))):
        receive(there(0, ds), into.at[1], g_recv.at[side])
        receive(there(-1, ds), into.at[0], g_recv.at[2 + side])
        receive(there(1, ds), into.at[2], g_recv.at[4 + side])

    def g_row(blk, e, at):
        x = gs[1, e]
        gs[2, e] = shift_right(x, gleft[blk], at, 4)
        gs[0, e] = shift_left(x, gright[blk], at, 4)

    for k in range(16):
        g_row(1, 4 + k, 4 * k)
    for k in range(4):
        g_row(0, k, 4 * (12 + k))
        g_row(2, 20 + k, 4 * k)

    @pl.loop(0, TR // 4)
    def _(g):
        for k in range(4):
            r = 4 * g + k
            back = dot(w1t[...], stack(taps(gs, [r + 8, r + 4, r])))
            out = gs[1, r + 4].astype(F32) + jnp.where(xf[r].astype(F32) > 0, back, 0.0)
            xf[r] = out.astype(BF)

    both_ref[:CH] = jnp.swapaxes(xf[...], 0, 1)

    mine = jnp.int32(0)
    is_owner = place < 0
    for j, owner in enumerate(OWNERS):
        mine = jnp.where(place == owner, j, mine)
        is_owner = jnp.logical_or(is_owner, place == owner)
    my_rows = pl.ds(pl.multiple_of(CHUNK * mine, CHUNK), CHUNK)

    def b_copy(k):
        return pltpu.make_async_remote_copy(
            src_ref=rb.at[0], dst_ref=rb.at[k], send_sem=b_send.at[k - 1], recv_sem=b_recv.at[k - 1],
            device_id=z_flip(k), device_id_type=MESH)

    def o_copy(n):
        return pltpu.make_async_remote_copy(
            src_ref=fin.at[my_rows], dst_ref=fin.at[my_rows], send_sem=o_send.at[n],
            recv_sem=o_recv, device_id=plane_peer(PLANE_FLIPS[n]), device_id_type=MESH)

    @pl.when(is_owner)
    def _():
        arrived(ra, a_recv)
        total = gb[my_rows, :].astype(F32)
        for i in range(PLANE - 1):
            total += ra[i].astype(F32)
        rb[0] = total.astype(BF)
        for k in Z_FLIPS:
            b_copy(k).start()

    @pl.when(is_owner)
    def _():
        full = rb[0].astype(F32)
        for k in reversed(Z_FLIPS):
            b_copy(k).wait_recv()
            full += rb[k].astype(F32)
        fin[my_rows, :] = (full * scale).astype(BF)
        for n in range(PLANE - 1):
            o_copy(n).start()

    for _, sent in f_out + p_out + c_out + g_out + relay_out + [out for _, out in relay_on]:
        sent()
    for j in range(NCHUNK):
        pl.when(place != OWNERS[j])(lambda j=j: a_copy(j).wait_send())

    pl.when(is_owner)(lambda: arrived(fin.at[pl.ds(0, K - CHUNK)], o_recv))
    pl.when(jnp.logical_not(is_owner))(lambda: arrived(fin, o_recv))
    for j in range(NCHUNK):
        both_ref[CH + j] = jnp.concatenate(
            [fin[CHUNK * j:CHUNK * j + TR, :], fin[CHUNK * j + TR:CHUNK * (j + 1), :]], axis=1)

    @pl.when(is_owner)
    def _():
        for k in Z_FLIPS:
            b_copy(k).wait_send()
        for n in range(PLANE - 1):
            o_copy(n).wait_send()


def finish(both, out_hbm, first_hbm, second_hbm, first, second, store):
    stores = [pltpu.make_async_copy(src, dst, store.at[i]) for i, (src, dst) in enumerate(
        ((both.at[pl.ds(0, CH)], out_hbm), (first, first_hbm), (second, second_hbm)))]
    stores[0].start()
    for t in range(9):
        for q in range(CH // TR):
            rows, lanes = slice(TR * q, TR * (q + 1)), slice(2 * CH * (q % 2), 2 * CH * (q % 2 + 1))
            part = both[CH + 2 * t + q // 2, :, lanes].astype(F32)
            first[t, rows] = part[:, CH:]
            second[t, rows] = part[:, :CH]
    stores[1].start()
    stores[2].start()
    for copy in stores:
        copy.wait()


def shards(field, cotangent, first_filter, second_filter):
    scale = 1.0 / math.sqrt(TR * LONG * TC * SHORT)
    hbm = pl.BlockSpec(memory_space=pltpu.HBM)
    vmem = pl.BlockSpec(memory_space=pltpu.VMEM)
    dma = pltpu.SemaphoreType.DMA

    def buf(*shape, dtype=BF):
        return pltpu.VMEM(shape, dtype)

    both = pl.pallas_call(
        lambda *refs: kernel(scale, *refs),
        out_shape=pltpu.VMEM((CH + NCHUNK, TR, TC), BF),
        in_specs=[hbm] * 4,
        out_specs=vmem,
        scratch_shapes=[
            buf(CH, TR, TC), buf(CH, TR, TC), buf(9, CH, CH), buf(9, CH, CH),
            buf(TR, CH, TC), buf(TR, CH, TC),
            buf(3, TR + 8, CH, TC), buf(3, TR + 16, CH, TC), buf(3, TR + 8, CH, TC),
            buf(2, 2, CH, 128), buf(4, CH, 128), buf(4, CH, 128),
            buf(2, CH, 128), buf(3, CH, 128), buf(3, CH, 128),
            buf(CH, K), buf(CH, K), buf(2, CH, 6 * CH), buf(2, CH, 3 * CH),
            buf(TR, CH, TC, dtype=F32),
            buf(3, 3 * CH, CH, dtype=F32), buf(CH, K, dtype=F32), buf(K, 2 * CH),
            buf(PLANE - 1, CHUNK, 2 * CH), buf(NZ, CHUNK, 2 * CH), buf(K, 2 * CH),
            dma((4,)),
            dma((2,)), dma((2,)), dma((2,)), dma((2,)), dma((6,)), dma((6,)), dma((8,)), dma((8,)),
            dma((NCHUNK,)), dma, dma((NZ - 1,)), dma((NZ - 1,)), dma((PLANE - 1,)), dma,
            pltpu.SemaphoreType.REGULAR((3,)),
            buf(2, CH, TC), dma((2,)), dma, dma, dma((2,)),
        ],
        compiler_params=pltpu.CompilerParams(
            collective_id=0, has_side_effects=True, vmem_limit_bytes=60 << 20),
        name="dilated_backward",
    )(field, cotangent, first_filter, second_filter)
    taps = jax.ShapeDtypeStruct((9, CH, CH), F32)
    return pl.pallas_call(
        finish,
        out_shape=(jax.ShapeDtypeStruct((CH, TR, TC), BF), taps, taps),
        in_specs=[vmem],
        out_specs=(hbm, hbm, hbm),
        scratch_shapes=[
            buf(9, CH, CH, dtype=F32), buf(9, CH, CH, dtype=F32), dma((3,))],
        compiler_params=pltpu.CompilerParams(vmem_limit_bytes=16 << 20),
        name="finish",
    )(both)


def solution(mesh):
    in_specs = (P(None, "long", "short"), P(None, "long", "short"), P(), P())
    out_specs = (P(None, "long", "short"), P(), P())
    return jax.shard_map(shards, mesh=mesh, in_specs=in_specs, out_specs=out_specs, check_vma=False)
```

```python
import math

import jax
import jax.numpy as jnp
from jax import lax
from jax.experimental import pallas as pl
from jax.experimental.pallas import tpu as pltpu
from jax.sharding import PartitionSpec as P

BF = jnp.bfloat16
F32 = jnp.float32
MESH = pl.DeviceIdType.MESH
CH, TR, TC = 64, 16, 256
K = 9 * CH
LONG, SHORT = 64, 4
PLANE = 32
NZ = LONG // PLANE * SHORT
CHUNK = 32
NCHUNK = K // CHUNK
OWNERS = (10, 21, 12, 19, 2, 9, 22, 29, 4, 13, 15, 16, 27, 18, 6, 7, 24, 25)

NEAR = ((-1, 0), (1, 0), (0, -1), (0, 1), (-1, -1), (-1, 1), (1, -1), (1, 1))


PLANE_FLIPS = sorted(
    range(1, PLANE), key=lambda m: -((2 if m // 2 % 4 == 2 else min(m // 2 % 4, 1)) + (2 if m // 8 == 2 else min(m // 8, 1))))
ROW_FLIPS = [m for m in PLANE_FLIPS if m < 8]
COLUMN_FLIPS = [m for m in PLANE_FLIPS if m % 8 == 0]
Z_FLIPS = (4, 5, 3, 7, 6, 2, 1)


def nt_dot(a, b):
    return lax.dot_general(a, b, (((1,), (1,)), ((), ())), preferred_element_type=F32)


def dot(a, b):
    return jnp.dot(a, b, preferred_element_type=F32)


def arrived(ref, sem):
    pltpu.make_async_copy(ref, ref, sem).wait()


def kernel(scale, field_hbm, cot_hbm, w1_hbm, w2_hbm, both_ref,
           raw_f, raw_c, raw_w1, raw_w2, xf, a2, fs, cs, gs, ps, pleft, pright, gps, gleft, gright,
           w1c, w1t, w2own, w2halo, up_own, acc2, acc1, gb, ra, rb, fin, in_sem,
           f_send, f_recv, c_send, c_recv, p_send, p_recv, g_send, g_recv,
           a_send, a_recv, b_send, b_recv, o_send, o_recv, ready,
           relay, r_send, r_recv, w_send, w_recv):
    l = lax.axis_index("long")
    s = lax.axis_index("short")
    place = lax.rem(l, PLANE)
    base = l - place
    core = lax.rem(l, 2)
    z = lax.div(l, PLANE) * SHORT + s

    fetch = [pltpu.make_async_copy(src, dst, in_sem.at[i]) for i, (src, dst) in enumerate(
        ((field_hbm, raw_f), (cot_hbm, raw_c), (w1_hbm, raw_w1), (w2_hbm, raw_w2)))]
    for copy in fetch:
        copy.start()

    barrier = pltpu.get_barrier_semaphore()

    def greet(dev):
        pl.semaphore_signal(barrier, inc=1, device_id=dev, device_id_type=MESH)

    def there(dl, ds):
        ok = None
        for d, at, n in ((dl, l, LONG), (ds, s, SHORT)):
            if d == 0:
                continue
            here = at + d >= 0 if d < 0 else at + d < n
            ok = here if ok is None else jnp.logical_and(ok, here)
        return ok

    def flips(at, bits):
        return [b - 2 * b * lax.rem(lax.div(at, b), 2) for b in bits]

    place_flips = flips(place, (1, 2, 4, 8, 16))
    short_flips = flips(s, (1, 2))
    group_flip = PLANE - 2 * PLANE * lax.div(l, PLANE)

    def flipped(at, steps, m):
        for n, step in enumerate(steps):
            if m >> n & 1:
                at = at + step
        return at

    def plane_peer(m):
        return flipped(l, place_flips, m), s

    def z_flip(m):
        return (l + group_flip if m & 4 else l), flipped(s, short_flips, m & 3)

    def z_peer(k):
        other = lax.rem(z + k, NZ)
        return lax.div(other, SHORT) * PLANE + place, lax.rem(other, SHORT)

    first = [plane_peer(m) for m in ROW_FLIPS + COLUMN_FLIPS] + [z_peer(1), z_peer(NZ - 1)]
    greetings = jnp.int32(len(first))
    for dl, ds in NEAR:
        pl.when(there(dl, ds))(lambda dl=dl, ds=ds: greet((l + dl, s + ds)))
        greetings = greetings + there(dl, ds).astype(jnp.int32)
    for dev in first:
        greet(dev)

    def pass_on(n, devs):
        for dev in devs:
            pl.semaphore_signal(ready.at[n], inc=1, device_id=dev, device_id_type=MESH)

    def message(dl, ds, src, dst, send_sem, recv_sem, only=None):
        copy = pltpu.make_async_remote_copy(
            src_ref=src, dst_ref=dst, send_sem=send_sem, recv_sem=recv_sem,
            device_id=(l + dl, s + ds), device_id_type=MESH)
        ok = there(dl, ds) if only is None else only
        return (lambda: pl.when(ok)(lambda: copy.start()),
                lambda: pl.when(ok)(lambda: copy.wait_send()))

    def receive(ok, dst, sem):
        pl.when(ok)(lambda: arrived(dst, sem))

        @pl.when(jnp.logical_not(ok))
        def _():
            dst[...] = jnp.zeros(dst.shape, dst.dtype)

    seam_down = jnp.logical_and(place == PLANE - 1, l < LONG - 1)
    seam_up = jnp.logical_and(place == 0, l > 0)
    up, down = jnp.logical_and(l > 0, place != 0), jnp.logical_and(l < LONG - 1, place != PLANE - 1)
    f_out = [message(-1, 0, fs.at[1, pl.ds(4, 4)], fs.at[1, pl.ds(20, 4)], f_send.at[0], f_recv.at[1], up),
             message(1, 0, fs.at[1, pl.ds(16, 4)], fs.at[1, pl.ds(0, 4)], f_send.at[1], f_recv.at[0], down)]
    f_far = [message(-1, 0, fs.at[1, pl.ds(4, 4)], fs.at[1, pl.ds(20, 4)], f_send.at[0], f_recv.at[1], seam_up),
             message(1, 0, fs.at[1, pl.ds(16, 4)], fs.at[1, pl.ds(0, 4)], f_send.at[1], f_recv.at[0], seam_down)]
    c_out = [message(-1, 0, cs.at[1, pl.ds(8, 8)], cs.at[1, pl.ds(24, 8)], c_send.at[0], c_recv.at[1], up),
             message(1, 0, cs.at[1, pl.ds(16, 8)], cs.at[1, pl.ds(0, 8)], c_send.at[1], c_recv.at[0], down)]
    c_far = [message(-1, 0, cs.at[1, pl.ds(8, 4)], cs.at[1, pl.ds(24, 4)], c_send.at[0], c_recv.at[1], seam_up),
             message(1, 0, cs.at[1, pl.ds(16, 4)], cs.at[1, pl.ds(0, 4)], c_send.at[1], c_recv.at[0], seam_down)]
    relay_out, relay_on = [], []
    for n, hop in enumerate((2, 8)):
        for at_seam, way, low in ((seam_down, 1, 16), (seam_up, -1, 8)):
            rows = pl.ds(low + 4 + 2 * n, 2)
            relay_out.append(message(-way * hop, 0, cs.at[1, rows], relay, r_send.at[n], r_recv, at_seam))
            end = PLANE - 1 - hop if way == 1 else hop
            here = jnp.logical_and(place == end, l < PLANE if way == 1 else l >= LONG - PLANE)
            into = pl.ds((0 if way == 1 else 24) + 4 + 2 * n, 2)
            relay_on.append((here, message(
                way * (hop + 1), 0, relay, cs.at[1, into], w_send, w_recv.at[n], here)))
    g_out = [message(-1, 0, gs.at[1, pl.ds(4, 4)], gs.at[1, pl.ds(20, 4)], g_send.at[0], g_recv.at[7]),
             message(1, 0, gs.at[1, pl.ds(16, 4)], gs.at[1, pl.ds(0, 4)], g_send.at[1], g_recv.at[6])]
    p_out = []
    for side, (ds, into, g_into) in enumerate(((-1, pright, gright), (1, pleft, gleft))):
        p_out.append(message(0, ds, ps.at[side], into.at[pl.ds(1, 2)], p_send.at[side], p_recv.at[1 - side]))
        g_out.append(message(0, ds, gps.at[side], g_into.at[1], g_send.at[2 + side], g_recv.at[1 - side]))
    for half, dl in ((0, -1), (1, 1)):
        for side, (ds, into, g_into) in enumerate(((-1, pright, gright), (1, pleft, gleft))):
            out, back = 2 + 2 * half + side, 2 + 2 * (1 - half) + 1 - side
            p_out.append(message(
                dl, ds, ps.at[side, pl.ds(half, 1)], into.at[pl.ds(3 - 3 * half, 1)], p_send.at[out], p_recv.at[back]))
            g_out.append(message(
                dl, ds, gps.at[side], g_into.at[2 - 2 * half], g_send.at[2 + out], g_recv.at[back]))

    fetch[0].wait()
    own_f = jnp.swapaxes(raw_f[...], 0, 1)
    xf[...] = own_f
    fs[1, 4:20] = jnp.maximum(own_f, 0)
    fetch[1].wait()
    cs[1, 8:24] = jnp.swapaxes(raw_c[...], 0, 1)
    for half in range(2):
        for side in range(2):
            c8 = 0 if side == 0 else TC - 8
            c4 = 0 if side == 0 else TC - 4
            pieces = [cs[1, 8 + 8 * half + k][:, c8:c8 + 8] for k in range(8)]
            pieces += [fs[1, 4 + 8 * half + k][:, c4:c4 + 4] for k in range(8)]
            pieces += [jnp.zeros((CH, 32), BF)]
            ps[side, half] = jnp.concatenate(pieces, axis=1)

    pl.semaphore_wait(barrier, greetings)
    for start, _ in f_far + p_out + relay_out + f_out + c_out:
        start()
    pass_on(0, [plane_peer(m) for m in ROW_FLIPS])
    pass_on(1, [z_peer(1), z_peer(NZ - 1)])

    fetch[2].wait()
    fetch[3].wait()
    for t in range(9):
        w1c[:, CH * t:CH * (t + 1)] = raw_w1[t]
    w1t[...] = raw_w1[...].reshape(K, CH).T
    taps_of = [raw_w2[3 * a:3 * a + 3].reshape(3 * CH, CH).T for a in range(3)]
    for half in range(2):
        w2own[half] = jnp.concatenate([taps_of[1], taps_of[2 * half]], axis=1)
        w2halo[half] = taps_of[2 - 2 * half]

    for _, sent in f_far:
        sent()
    for start, _ in c_far:
        start()

    acc2[...] = jnp.zeros_like(acc2)
    acc1[...] = jnp.zeros_like(acc1)

    def shift_left(x, h, at, d):
        return jnp.concatenate([x[:, d:], h[:, at:at + d]], axis=1)

    def shift_right(x, h, at, d):
        return jnp.concatenate([h[:, at:at + d], x[:, :TC - d]], axis=1)

    def f_row(blk, k, e):
        x = fs[1, e]
        fs[0, e] = shift_right(x, pleft[blk], 64 + 4 * k, 4)
        fs[2, e] = shift_left(x, pright[blk], 64 + 4 * k, 4)

    def c_row(blk, k):
        e = 8 * blk + k
        x = cs[1, e]
        cs[2, e] = shift_right(x, pleft[blk], 8 * k, 8)
        cs[0, e] = shift_left(x, pright[blk], 8 * k, 8)

    def taps(ref, rows):
        return [ref[b, e] for e in rows for b in range(3)]

    def stack(parts):
        return jnp.concatenate(parts, axis=0)

    receive(there(0, -1), pleft.at[pl.ds(1, 2)], p_recv.at[0])
    receive(there(0, 1), pright.at[pl.ds(1, 2)], p_recv.at[1])
    for here, (start, _) in relay_on:
        pl.when(here)(lambda: arrived(relay, r_recv))
        start()
    pl.semaphore_wait(ready.at[0], len(ROW_FLIPS))
    pl.semaphore_wait(ready.at[1], 2)
    pass_on(2, [z_peer(2), z_peer(NZ - 2)])

    @pl.loop(1, 3)
    def _(blk):
        for k in range(8):
            f_row(blk, k, 8 * blk + k - 4)
            c_row(blk, k)

    def hidden_row(r):
        h = xf[r].astype(F32) + dot(w1c[...], stack(taps(fs, [r, r + 4, r + 8])))
        a2[r] = jnp.maximum(h.astype(BF), 0)

    @pl.loop(1, 3)
    def _(g):
        for k in range(4):
            hidden_row(4 * g + k)

    for half in range(2):
        @pl.loop(0, 2)
        def _(g):
            for k in range(4):
                r = 8 * half + 4 * g + k
                up_own[r] = dot(w2own[half], stack(taps(cs, [r + 8, r + 16 - 16 * half])))

    @pl.loop(0, 2)
    def _(i):
        half = (1 - core) + i * (2 * core - 1)
        ok = jnp.logical_or(jnp.logical_and(half == 0, l > 0), jnp.logical_and(half == 1, l < LONG - 1))
        receive(jnp.logical_and(ok, s > 0), pleft.at[pl.ds(3 * half, 1)], p_recv.at[2 + 2 * half])
        receive(jnp.logical_and(ok, s < SHORT - 1), pright.at[pl.ds(3 * half, 1)], p_recv.at[3 + 2 * half])
        receive(ok, fs.at[1, pl.ds(20 * half, 4)], f_recv.at[half])
        for k in range(4):
            e = 20 * half + k
            x = fs[1, e]
            for b, shift, pack in ((0, shift_right, pleft), (2, shift_left, pright)):
                low = shift(x, pack[3 * half], 64 + 4 * k, 4)
                high = shift(x, pack[3 * half], 64 + 4 * (k + 4), 4)
                fs[b, e] = jnp.where(half == 1, low, high)
        for k in range(4):
            hidden_row(12 * half + k)

        rows = [8 * half + k for k in range(8)]
        act = jnp.concatenate([a2[r] for r in rows], axis=1)
        own = nt_dot(
            jnp.concatenate([stack(taps(cs, [r + 8, r + 16 - 16 * half])) for r in rows], axis=1), act)
        acc2[1] += own[:3 * CH]
        acc2[2 * half] += own[3 * CH:]

        far = jnp.logical_or(jnp.logical_and(half == 1, seam_down), jnp.logical_and(half == 0, seam_up))
        edge = 24 * half

        @pl.when(far)
        def _():
            arrived(cs.at[1, pl.ds(edge, 4)], c_recv.at[half])
            for n in range(2):
                arrived(cs.at[1, pl.ds(edge + 4 + 2 * n, 2)], w_recv.at[n])

        pl.when(jnp.logical_not(far))(lambda: receive(ok, cs.at[1, pl.ds(edge, 8)], c_recv.at[half]))
        for k in range(8):
            c_row(3 * half, k)
        beyond = [stack(taps(cs, [24 * half + k])) for k in range(8)]
        for k, r in enumerate(rows):
            up = up_own[r] + dot(w2halo[half], beyond[k])
            gh = cs[1, r + 8].astype(F32) + jnp.where(a2[r].astype(F32) > 0, up, 0.0)
            gs[1, r + 4] = gh.astype(BF)
        acc2[2 - 2 * half] += nt_dot(jnp.concatenate(beyond, axis=1), act)
        acc1[...] += nt_dot(
            jnp.concatenate([gs[1, r + 4] for r in rows], axis=1),
            jnp.concatenate([stack(taps(fs, [r, r + 4, r + 8])) for r in rows], axis=1))

    for t in range(9):
        gb[CH * t:CH * (t + 1), :] = jnp.concatenate(
            [acc2[t // 3, CH * (t % 3):CH * (t % 3 + 1), :], acc1[:, CH * t:CH * (t + 1)]], axis=1).astype(BF)

    def a_copy(j):
        owner = OWNERS[j]
        slot = place - (place > owner).astype(jnp.int32)
        return pltpu.make_async_remote_copy(
            src_ref=gb.at[pl.ds(CHUNK * j, CHUNK)], dst_ref=ra.at[slot],
            send_sem=a_send.at[j], recv_sem=a_recv,
            device_id=(base + owner, s), device_id_type=MESH)

    for j in range(NCHUNK):
        pl.when(place != OWNERS[j])(lambda j=j: a_copy(j).start())
    pl.semaphore_wait(ready.at[2], 2)

    for start, _ in g_out[:2]:
        start()
    for side in range(2):
        c4 = 0 if side == 0 else TC - 4
        pieces = [gs[1, 4 + k][:, c4:c4 + 4] for k in range(16)] + [jnp.zeros((CH, 64), BF)]
        gps[side] = jnp.concatenate(pieces, axis=1)
    for start, _ in g_out[2:]:
        start()

    receive(there(-1, 0), gs.at[1, pl.ds(0, 4)], g_recv.at[6])
    receive(there(1, 0), gs.at[1, pl.ds(20, 4)], g_recv.at[7])
    for side, (ds, into) in enumerate(((-1, gleft), (1, gright))):
        receive(there(0, ds), into.at[1], g_recv.at[side])
        receive(there(-1, ds), into.at[0], g_recv.at[2 + side])
        receive(there(1, ds), into.at[2], g_recv.at[4 + side])

    def g_row(blk, e, at):
        x = gs[1, e]
        gs[2, e] = shift_right(x, gleft[blk], at, 4)
        gs[0, e] = shift_left(x, gright[blk], at, 4)

    for k in range(16):
        g_row(1, 4 + k, 4 * k)
    for k in range(4):
        g_row(0, k, 4 * (12 + k))
        g_row(2, 20 + k, 4 * k)

    @pl.loop(0, TR // 4)
    def _(g):
        for k in range(4):
            r = 4 * g + k
            back = dot(w1t[...], stack(taps(gs, [r + 8, r + 4, r])))
            out = gs[1, r + 4].astype(F32) + jnp.where(xf[r].astype(F32) > 0, back, 0.0)
            xf[r] = out.astype(BF)

    both_ref[:CH] = jnp.swapaxes(xf[...], 0, 1)

    mine = jnp.int32(0)
    is_owner = place < 0
    for j, owner in enumerate(OWNERS):
        mine = jnp.where(place == owner, j, mine)
        is_owner = jnp.logical_or(is_owner, place == owner)
    my_rows = pl.ds(pl.multiple_of(CHUNK * mine, CHUNK), CHUNK)

    def b_copy(k):
        return pltpu.make_async_remote_copy(
            src_ref=rb.at[0], dst_ref=rb.at[k], send_sem=b_send.at[k - 1], recv_sem=b_recv.at[k - 1],
            device_id=z_flip(k), device_id_type=MESH)

    def o_copy(n):
        return pltpu.make_async_remote_copy(
            src_ref=fin.at[my_rows], dst_ref=fin.at[my_rows], send_sem=o_send.at[n],
            recv_sem=o_recv, device_id=plane_peer(PLANE_FLIPS[n]), device_id_type=MESH)

    @pl.when(is_owner)
    def _():
        arrived(ra, a_recv)
        total = gb[my_rows, :].astype(F32)
        for i in range(PLANE - 1):
            total += ra[i].astype(F32)
        rb[0] = total.astype(BF)
        for k in Z_FLIPS:
            b_copy(k).start()

    @pl.when(is_owner)
    def _():
        full = rb[0].astype(F32)
        for k in reversed(Z_FLIPS):
            b_copy(k).wait_recv()
            full += rb[k].astype(F32)
        fin[my_rows, :] = (full * scale).astype(BF)
        for n in range(PLANE - 1):
            o_copy(n).start()

    for _, sent in f_out + p_out + c_out + c_far + g_out + relay_out + [out for _, out in relay_on]:
        sent()
    for j in range(NCHUNK):
        pl.when(place != OWNERS[j])(lambda j=j: a_copy(j).wait_send())

    pl.when(is_owner)(lambda: arrived(fin.at[pl.ds(0, K - CHUNK)], o_recv))
    pl.when(jnp.logical_not(is_owner))(lambda: arrived(fin, o_recv))
    for j in range(NCHUNK):
        both_ref[CH + j] = jnp.concatenate(
            [fin[CHUNK * j:CHUNK * j + TR, :], fin[CHUNK * j + TR:CHUNK * (j + 1), :]], axis=1)

    @pl.when(is_owner)
    def _():
        for k in Z_FLIPS:
            b_copy(k).wait_send()
        for n in range(PLANE - 1):
            o_copy(n).wait_send()


def finish(both, out_hbm, first_hbm, second_hbm, first, second, store):
    stores = [pltpu.make_async_copy(src, dst, store.at[i]) for i, (src, dst) in enumerate(
        ((both.at[pl.ds(0, CH)], out_hbm), (first, first_hbm), (second, second_hbm)))]
    stores[0].start()
    for t in range(9):
        for q in range(CH // TR):
            rows, lanes = slice(TR * q, TR * (q + 1)), slice(2 * CH * (q % 2), 2 * CH * (q % 2 + 1))
            part = both[CH + 2 * t + q // 2, :, lanes].astype(F32)
            first[t, rows] = part[:, CH:]
            second[t, rows] = part[:, :CH]
    stores[1].start()
    stores[2].start()
    for copy in stores:
        copy.wait()


def shards(field, cotangent, first_filter, second_filter):
    scale = 1.0 / math.sqrt(TR * LONG * TC * SHORT)
    hbm = pl.BlockSpec(memory_space=pltpu.HBM)
    vmem = pl.BlockSpec(memory_space=pltpu.VMEM)
    dma = pltpu.SemaphoreType.DMA

    def buf(*shape, dtype=BF):
        return pltpu.VMEM(shape, dtype)

    both = pl.pallas_call(
        lambda *refs: kernel(scale, *refs),
        out_shape=pltpu.VMEM((CH + NCHUNK, TR, TC), BF),
        in_specs=[hbm] * 4,
        out_specs=vmem,
        scratch_shapes=[
            buf(CH, TR, TC), buf(CH, TR, TC), buf(9, CH, CH), buf(9, CH, CH),
            buf(TR, CH, TC), buf(TR, CH, TC),
            buf(3, TR + 8, CH, TC), buf(3, TR + 16, CH, TC), buf(3, TR + 8, CH, TC),
            buf(2, 2, CH, 128), buf(4, CH, 128), buf(4, CH, 128),
            buf(2, CH, 128), buf(3, CH, 128), buf(3, CH, 128),
            buf(CH, K), buf(CH, K), buf(2, CH, 6 * CH), buf(2, CH, 3 * CH),
            buf(TR, CH, TC, dtype=F32),
            buf(3, 3 * CH, CH, dtype=F32), buf(CH, K, dtype=F32), buf(K, 2 * CH),
            buf(PLANE - 1, CHUNK, 2 * CH), buf(NZ, CHUNK, 2 * CH), buf(K, 2 * CH),
            dma((4,)),
            dma((2,)), dma((2,)), dma((2,)), dma((2,)), dma((6,)), dma((6,)), dma((8,)), dma((8,)),
            dma((NCHUNK,)), dma, dma((NZ - 1,)), dma((NZ - 1,)), dma((PLANE - 1,)), dma,
            pltpu.SemaphoreType.REGULAR((3,)),
            buf(2, CH, TC), dma((2,)), dma, dma, dma((2,)),
        ],
        compiler_params=pltpu.CompilerParams(
            collective_id=0, has_side_effects=True, vmem_limit_bytes=60 << 20),
        name="dilated_backward",
    )(field, cotangent, first_filter, second_filter)
    taps = jax.ShapeDtypeStruct((9, CH, CH), F32)
    return pl.pallas_call(
        finish,
        out_shape=(jax.ShapeDtypeStruct((CH, TR, TC), BF), taps, taps),
        in_specs=[vmem],
        out_specs=(hbm, hbm, hbm),
        scratch_shapes=[
            buf(9, CH, CH, dtype=F32), buf(9, CH, CH, dtype=F32), dma((3,))],
        compiler_params=pltpu.CompilerParams(vmem_limit_bytes=16 << 20),
        name="finish",
    )(both)


def solution(mesh):
    in_specs = (P(None, "long", "short"), P(None, "long", "short"), P(), P())
    out_specs = (P(None, "long", "short"), P(), P())
    return jax.shard_map(shards, mesh=mesh, in_specs=in_specs, out_specs=out_specs, check_vma=False)
```

```python
import math

import jax
import jax.numpy as jnp
from jax import lax
from jax.experimental import pallas as pl
from jax.experimental.pallas import tpu as pltpu
from jax.sharding import PartitionSpec as P

BF = jnp.bfloat16
F32 = jnp.float32
MESH = pl.DeviceIdType.MESH
CH, TR, TC = 64, 16, 256
K = 9 * CH
LONG, SHORT = 64, 4
PLANE = 32
NZ = LONG // PLANE * SHORT
CHUNK = 32
NCHUNK = K // CHUNK
OWNERS = (10, 21, 12, 19, 2, 9, 22, 29, 4, 13, 15, 16, 27, 18, 6, 7, 24, 25)

NEAR = ((-1, 0), (1, 0), (0, -1), (0, 1), (-1, -1), (-1, 1), (1, -1), (1, 1))


PLANE_FLIPS = sorted(
    range(1, PLANE), key=lambda m: -((2 if m // 2 % 4 == 2 else min(m // 2 % 4, 1)) + (2 if m // 8 == 2 else min(m // 8, 1))))
ROW_FLIPS = [m for m in PLANE_FLIPS if m < 8]
COLUMN_FLIPS = [m for m in PLANE_FLIPS if m % 8 == 0]
Z_FLIPS = (4, 5, 3, 7, 6, 2, 1)


def nt_dot(a, b):
    return lax.dot_general(a, b, (((1,), (1,)), ((), ())), preferred_element_type=F32)


def dot(a, b):
    return jnp.dot(a, b, preferred_element_type=F32)


def arrived(ref, sem):
    pltpu.make_async_copy(ref, ref, sem).wait()


def kernel(scale, field_hbm, cot_hbm, w1_hbm, w2_hbm, both_ref,
           raw_f, raw_c, raw_w1, raw_w2, xf, a2, fs, cs, gs, ps, pleft, pright, gps, gleft, gright,
           w1c, w1t, w2own, w2halo, up_own, acc2, acc1, gb, ra, rb, fin, in_sem,
           f_send, f_recv, c_send, c_recv, p_send, p_recv, g_send, g_recv,
           a_send, a_recv, b_send, b_recv, o_send, o_recv, ready,
           relay, r_send, r_recv, w_send, w_recv):
    l = lax.axis_index("long")
    s = lax.axis_index("short")
    place = lax.rem(l, PLANE)
    base = l - place
    core = lax.rem(l, 2)
    z = lax.div(l, PLANE) * SHORT + s

    fetch = [pltpu.make_async_copy(src, dst, in_sem.at[i]) for i, (src, dst) in enumerate(
        ((field_hbm, raw_f), (cot_hbm, raw_c), (w1_hbm, raw_w1), (w2_hbm, raw_w2)))]
    for copy in fetch:
        copy.start()

    barrier = pltpu.get_barrier_semaphore()

    def greet(dev):
        pl.semaphore_signal(barrier, inc=1, device_id=dev, device_id_type=MESH)

    def there(dl, ds):
        ok = None
        for d, at, n in ((dl, l, LONG), (ds, s, SHORT)):
            if d == 0:
                continue
            here = at + d >= 0 if d < 0 else at + d < n
            ok = here if ok is None else jnp.logical_and(ok, here)
        return ok

    def flips(at, bits):
        return [b - 2 * b * lax.rem(lax.div(at, b), 2) for b in bits]

    place_flips = flips(place, (1, 2, 4, 8, 16))
    short_flips = flips(s, (1, 2))
    group_flip = PLANE - 2 * PLANE * lax.div(l, PLANE)

    def flipped(at, steps, m):
        for n, step in enumerate(steps):
            if m >> n & 1:
                at = at + step
        return at

    def plane_peer(m):
        return flipped(l, place_flips, m), s

    def z_flip(m):
        return (l + group_flip if m & 4 else l), flipped(s, short_flips, m & 3)

    def z_peer(k):
        other = lax.rem(z + k, NZ)
        return lax.div(other, SHORT) * PLANE + place, lax.rem(other, SHORT)

    first = [plane_peer(m) for m in ROW_FLIPS + COLUMN_FLIPS] + [z_peer(1), z_peer(NZ - 1)]
    greetings = jnp.int32(len(first))
    for dl, ds in NEAR:
        pl.when(there(dl, ds))(lambda dl=dl, ds=ds: greet((l + dl, s + ds)))
        greetings = greetings + there(dl, ds).astype(jnp.int32)
    for dev in first:
        greet(dev)

    def pass_on(n, devs):
        for dev in devs:
            pl.semaphore_signal(ready.at[n], inc=1, device_id=dev, device_id_type=MESH)

    def message(dl, ds, src, dst, send_sem, recv_sem, only=None):
        copy = pltpu.make_async_remote_copy(
            src_ref=src, dst_ref=dst, send_sem=send_sem, recv_sem=recv_sem,
            device_id=(l + dl, s + ds), device_id_type=MESH)
        ok = there(dl, ds) if only is None else only
        return (lambda: pl.when(ok)(lambda: copy.start()),
                lambda: pl.when(ok)(lambda: copy.wait_send()))

    def receive(ok, dst, sem):
        pl.when(ok)(lambda: arrived(dst, sem))

        @pl.when(jnp.logical_not(ok))
        def _():
            dst[...] = jnp.zeros(dst.shape, dst.dtype)

    seam_down = jnp.logical_and(place == PLANE - 1, l < LONG - 1)
    seam_up = jnp.logical_and(place == 0, l > 0)
    up, down = jnp.logical_and(l > 0, place != 0), jnp.logical_and(l < LONG - 1, place != PLANE - 1)
    f_out = [message(-1, 0, fs.at[1, pl.ds(4, 4)], fs.at[1, pl.ds(20, 4)], f_send.at[0], f_recv.at[1], up),
             message(1, 0, fs.at[1, pl.ds(16, 4)], fs.at[1, pl.ds(0, 4)], f_send.at[1], f_recv.at[0], down)]
    f_far = [message(-1, 0, fs.at[1, pl.ds(4, 4)], fs.at[1, pl.ds(20, 4)], f_send.at[0], f_recv.at[1], seam_up),
             message(1, 0, fs.at[1, pl.ds(16, 4)], fs.at[1, pl.ds(0, 4)], f_send.at[1], f_recv.at[0], seam_down)]
    c_out = [message(-1, 0, cs.at[1, pl.ds(8, 8)], cs.at[1, pl.ds(24, 8)], c_send.at[0], c_recv.at[1], up),
             message(1, 0, cs.at[1, pl.ds(16, 8)], cs.at[1, pl.ds(0, 8)], c_send.at[1], c_recv.at[0], down)]
    c_far = [message(-1, 0, cs.at[1, pl.ds(8, 4)], cs.at[1, pl.ds(24, 4)], c_send.at[0], c_recv.at[1], seam_up),
             message(1, 0, cs.at[1, pl.ds(16, 4)], cs.at[1, pl.ds(0, 4)], c_send.at[1], c_recv.at[0], seam_down)]
    relay_out, relay_on = [], []
    for n, hop in enumerate((2, 8)):
        for at_seam, way, low in ((seam_down, 1, 16), (seam_up, -1, 8)):
            rows = pl.ds(low + 4 + 2 * n, 2)
            relay_out.append(message(-way * hop, 0, cs.at[1, rows], relay, r_send.at[n], r_recv, at_seam))
            end = PLANE - 1 - hop if way == 1 else hop
            here = jnp.logical_and(place == end, l < PLANE if way == 1 else l >= LONG - PLANE)
            into = pl.ds((0 if way == 1 else 24) + 4 + 2 * n, 2)
            relay_on.append((here, message(
                way * (hop + 1), 0, relay, cs.at[1, into], w_send, w_recv.at[n], here)))
    g_out = [message(-1, 0, gs.at[1, pl.ds(4, 4)], gs.at[1, pl.ds(20, 4)], g_send.at[0], g_recv.at[7]),
             message(1, 0, gs.at[1, pl.ds(16, 4)], gs.at[1, pl.ds(0, 4)], g_send.at[1], g_recv.at[6])]
    p_out = []
    for side, (ds, into, g_into) in enumerate(((-1, pright, gright), (1, pleft, gleft))):
        p_out.append(message(0, ds, ps.at[side], into.at[pl.ds(1, 2)], p_send.at[side], p_recv.at[1 - side]))
        g_out.append(message(0, ds, gps.at[side], g_into.at[1], g_send.at[2 + side], g_recv.at[1 - side]))
    for half, dl in ((0, -1), (1, 1)):
        for side, (ds, into, g_into) in enumerate(((-1, pright, gright), (1, pleft, gleft))):
            out, back = 2 + 2 * half + side, 2 + 2 * (1 - half) + 1 - side
            p_out.append(message(
                dl, ds, ps.at[side, pl.ds(half, 1)], into.at[pl.ds(3 - 3 * half, 1)], p_send.at[out], p_recv.at[back]))
            g_out.append(message(
                dl, ds, gps.at[side], g_into.at[2 - 2 * half], g_send.at[2 + out], g_recv.at[back]))

    fetch[0].wait()
    own_f = jnp.swapaxes(raw_f[...], 0, 1)
    xf[...] = own_f
    fs[1, 4:20] = jnp.maximum(own_f, 0)
    fetch[1].wait()
    cs[1, 8:24] = jnp.swapaxes(raw_c[...], 0, 1)
    for half in range(2):
        for side in range(2):
            c8 = 0 if side == 0 else TC - 8
            c4 = 0 if side == 0 else TC - 4
            pieces = [cs[1, 8 + 8 * half + k][:, c8:c8 + 8] for k in range(8)]
            pieces += [fs[1, 4 + 8 * half + k][:, c4:c4 + 4] for k in range(8)]
            pieces += [jnp.zeros((CH, 32), BF)]
            ps[side, half] = jnp.concatenate(pieces, axis=1)

    pl.semaphore_wait(barrier, greetings)
    for start, _ in f_far + p_out + relay_out + f_out + c_out:
        start()
    pass_on(0, [plane_peer(m) for m in ROW_FLIPS])
    pass_on(1, [z_peer(1), z_peer(NZ - 1)])

    fetch[2].wait()
    fetch[3].wait()
    for t in range(9):
        w1c[:, CH * t:CH * (t + 1)] = raw_w1[t]
    w1t[...] = raw_w1[...].reshape(K, CH).T
    taps_of = [raw_w2[3 * a:3 * a + 3].reshape(3 * CH, CH).T for a in range(3)]
    for half in range(2):
        w2own[half] = jnp.concatenate([taps_of[1], taps_of[2 * half]], axis=1)
        w2halo[half] = taps_of[2 - 2 * half]

    for _, sent in f_far:
        sent()
    for start, _ in c_far:
        start()

    acc2[...] = jnp.zeros_like(acc2)
    acc1[...] = jnp.zeros_like(acc1)

    def shift_left(x, h, at, d):
        return jnp.concatenate([x[:, d:], h[:, at:at + d]], axis=1)

    def shift_right(x, h, at, d):
        return jnp.concatenate([h[:, at:at + d], x[:, :TC - d]], axis=1)

    def f_row(blk, k, e):
        x = fs[1, e]
        fs[0, e] = shift_right(x, pleft[blk], 64 + 4 * k, 4)
        fs[2, e] = shift_left(x, pright[blk], 64 + 4 * k, 4)

    def c_row(blk, k):
        e = 8 * blk + k
        x = cs[1, e]
        cs[2, e] = shift_right(x, pleft[blk], 8 * k, 8)
        cs[0, e] = shift_left(x, pright[blk], 8 * k, 8)

    def taps(ref, rows):
        return [ref[b, e] for e in rows for b in range(3)]

    def stack(parts):
        return jnp.concatenate(parts, axis=0)

    receive(there(0, -1), pleft.at[pl.ds(1, 2)], p_recv.at[0])
    receive(there(0, 1), pright.at[pl.ds(1, 2)], p_recv.at[1])
    for here, (start, _) in relay_on:
        pl.when(here)(lambda: arrived(relay, r_recv))
        start()
    pl.semaphore_wait(ready.at[0], len(ROW_FLIPS))
    pl.semaphore_wait(ready.at[1], 2)
    pass_on(2, [z_peer(2), z_peer(NZ - 2)])

    @pl.loop(1, 3)
    def _(blk):
        for k in range(8):
            f_row(blk, k, 8 * blk + k - 4)
            c_row(blk, k)

    def hidden_row(r):
        h = xf[r].astype(F32) + dot(w1c[...], stack(taps(fs, [r, r + 4, r + 8])))
        a2[r] = jnp.maximum(h.astype(BF), 0)

    @pl.loop(1, 3)
    def _(g):
        for k in range(4):
            hidden_row(4 * g + k)

    for half in range(2):
        @pl.loop(0, 2)
        def _(g):
            for k in range(4):
                r = 8 * half + 4 * g + k
                up_own[r] = dot(w2own[half], stack(taps(cs, [r + 8, r + 16 - 16 * half])))

    @pl.loop(0, 2)
    def _(i):
        half = (1 - core) + i * (2 * core - 1)
        ok = jnp.logical_or(jnp.logical_and(half == 0, l > 0), jnp.logical_and(half == 1, l < LONG - 1))
        receive(jnp.logical_and(ok, s > 0), pleft.at[pl.ds(3 * half, 1)], p_recv.at[2 + 2 * half])
        receive(jnp.logical_and(ok, s < SHORT - 1), pright.at[pl.ds(3 * half, 1)], p_recv.at[3 + 2 * half])
        receive(ok, fs.at[1, pl.ds(20 * half, 4)], f_recv.at[half])
        for k in range(4):
            e = 20 * half + k
            x = fs[1, e]
            for b, shift, pack in ((0, shift_right, pleft), (2, shift_left, pright)):
                low = shift(x, pack[3 * half], 64 + 4 * k, 4)
                high = shift(x, pack[3 * half], 64 + 4 * (k + 4), 4)
                fs[b, e] = jnp.where(half == 1, low, high)
        for k in range(4):
            hidden_row(12 * half + k)

        rows = [8 * half + k for k in range(8)]
        act = jnp.concatenate([a2[r] for r in rows], axis=1)
        own = nt_dot(
            jnp.concatenate([stack(taps(cs, [r + 8, r + 16 - 16 * half])) for r in rows], axis=1), act)
        acc2[1] += own[:3 * CH]
        acc2[2 * half] += own[3 * CH:]

        far = jnp.logical_or(jnp.logical_and(half == 1, seam_down), jnp.logical_and(half == 0, seam_up))
        edge = 24 * half

        @pl.when(far)
        def _():
            arrived(cs.at[1, pl.ds(edge, 4)], c_recv.at[half])
            for n in range(2):
                arrived(cs.at[1, pl.ds(edge + 4 + 2 * n, 2)], w_recv.at[n])

        pl.when(jnp.logical_not(far))(lambda: receive(ok, cs.at[1, pl.ds(edge, 8)], c_recv.at[half]))
        for k in range(8):
            c_row(3 * half, k)
        beyond = [stack(taps(cs, [24 * half + k])) for k in range(8)]
        for k, r in enumerate(rows):
            up = up_own[r] + dot(w2halo[half], beyond[k])
            gh = cs[1, r + 8].astype(F32) + jnp.where(a2[r].astype(F32) > 0, up, 0.0)
            gs[1, r + 4] = gh.astype(BF)
        acc2[2 - 2 * half] += nt_dot(jnp.concatenate(beyond, axis=1), act)
        acc1[...] += nt_dot(
            jnp.concatenate([gs[1, r + 4] for r in rows], axis=1),
            jnp.concatenate([stack(taps(fs, [r, r + 4, r + 8])) for r in rows], axis=1))

    def a_copy(j):
        owner = OWNERS[j]
        slot = place - (place > owner).astype(jnp.int32)
        return pltpu.make_async_remote_copy(
            src_ref=gb.at[pl.ds(CHUNK * j, CHUNK)], dst_ref=ra.at[slot],
            send_sem=a_send.at[j], recv_sem=a_recv,
            device_id=(base + owner, s), device_id_type=MESH)

    for t in range(9):
        gb[CH * t:CH * (t + 1), :] = jnp.concatenate(
            [acc2[t // 3, CH * (t % 3):CH * (t % 3 + 1), :], acc1[:, CH * t:CH * (t + 1)]], axis=1).astype(BF)
        for j in range(CH // CHUNK * t, CH // CHUNK * (t + 1)):
            pl.when(place != OWNERS[j])(lambda j=j: a_copy(j).start())
    pl.semaphore_wait(ready.at[2], 2)

    for start, _ in g_out[:2]:
        start()
    for side in range(2):
        c4 = 0 if side == 0 else TC - 4
        pieces = [gs[1, 4 + k][:, c4:c4 + 4] for k in range(16)] + [jnp.zeros((CH, 64), BF)]
        gps[side] = jnp.concatenate(pieces, axis=1)
    for start, _ in g_out[2:]:
        start()

    receive(there(-1, 0), gs.at[1, pl.ds(0, 4)], g_recv.at[6])
    receive(there(1, 0), gs.at[1, pl.ds(20, 4)], g_recv.at[7])
    for side, (ds, into) in enumerate(((-1, gleft), (1, gright))):
        receive(there(0, ds), into.at[1], g_recv.at[side])
        receive(there(-1, ds), into.at[0], g_recv.at[2 + side])
        receive(there(1, ds), into.at[2], g_recv.at[4 + side])

    def g_row(blk, e, at):
        x = gs[1, e]
        gs[2, e] = shift_right(x, gleft[blk], at, 4)
        gs[0, e] = shift_left(x, gright[blk], at, 4)

    for k in range(16):
        g_row(1, 4 + k, 4 * k)
    for k in range(4):
        g_row(0, k, 4 * (12 + k))
        g_row(2, 20 + k, 4 * k)

    @pl.loop(0, TR // 4)
    def _(g):
        for k in range(4):
            r = 4 * g + k
            back = dot(w1t[...], stack(taps(gs, [r + 8, r + 4, r])))
            out = gs[1, r + 4].astype(F32) + jnp.where(xf[r].astype(F32) > 0, back, 0.0)
            xf[r] = out.astype(BF)

    both_ref[:CH] = jnp.swapaxes(xf[...], 0, 1)

    mine = jnp.int32(0)
    is_owner = place < 0
    for j, owner in enumerate(OWNERS):
        mine = jnp.where(place == owner, j, mine)
        is_owner = jnp.logical_or(is_owner, place == owner)
    my_rows = pl.ds(pl.multiple_of(CHUNK * mine, CHUNK), CHUNK)

    def b_copy(k):
        return pltpu.make_async_remote_copy(
            src_ref=rb.at[0], dst_ref=rb.at[k], send_sem=b_send.at[k - 1], recv_sem=b_recv.at[k - 1],
            device_id=z_flip(k), device_id_type=MESH)

    def o_copy(n):
        return pltpu.make_async_remote_copy(
            src_ref=fin.at[my_rows], dst_ref=fin.at[my_rows], send_sem=o_send.at[n],
            recv_sem=o_recv, device_id=plane_peer(PLANE_FLIPS[n]), device_id_type=MESH)

    @pl.when(is_owner)
    def _():
        arrived(ra, a_recv)
        total = gb[my_rows, :].astype(F32)
        for i in range(PLANE - 1):
            total += ra[i].astype(F32)
        rb[0] = total.astype(BF)
        for k in Z_FLIPS:
            b_copy(k).start()

    @pl.when(is_owner)
    def _():
        full = rb[0].astype(F32)
        for k in reversed(Z_FLIPS):
            b_copy(k).wait_recv()
            full += rb[k].astype(F32)
        fin[my_rows, :] = (full * scale).astype(BF)
        for n in range(PLANE - 1):
            o_copy(n).start()

    for _, sent in f_out + p_out + c_out + c_far + g_out + relay_out + [out for _, out in relay_on]:
        sent()
    for j in range(NCHUNK):
        pl.when(place != OWNERS[j])(lambda j=j: a_copy(j).wait_send())

    pl.when(is_owner)(lambda: arrived(fin.at[pl.ds(0, K - CHUNK)], o_recv))
    pl.when(jnp.logical_not(is_owner))(lambda: arrived(fin, o_recv))
    for j in range(NCHUNK):
        both_ref[CH + j] = jnp.concatenate(
            [fin[CHUNK * j:CHUNK * j + TR, :], fin[CHUNK * j + TR:CHUNK * (j + 1), :]], axis=1)

    @pl.when(is_owner)
    def _():
        for k in Z_FLIPS:
            b_copy(k).wait_send()
        for n in range(PLANE - 1):
            o_copy(n).wait_send()


def finish(both, out_hbm, first_hbm, second_hbm, first, second, store):
    stores = [pltpu.make_async_copy(src, dst, store.at[i]) for i, (src, dst) in enumerate(
        ((both.at[pl.ds(0, CH)], out_hbm), (first, first_hbm), (second, second_hbm)))]
    stores[0].start()
    for t in range(9):
        for q in range(CH // TR):
            rows, lanes = slice(TR * q, TR * (q + 1)), slice(2 * CH * (q % 2), 2 * CH * (q % 2 + 1))
            part = both[CH + 2 * t + q // 2, :, lanes].astype(F32)
            first[t, rows] = part[:, CH:]
            second[t, rows] = part[:, :CH]
    stores[1].start()
    stores[2].start()
    for copy in stores:
        copy.wait()


def shards(field, cotangent, first_filter, second_filter):
    scale = 1.0 / math.sqrt(TR * LONG * TC * SHORT)
    hbm = pl.BlockSpec(memory_space=pltpu.HBM)
    vmem = pl.BlockSpec(memory_space=pltpu.VMEM)
    dma = pltpu.SemaphoreType.DMA

    def buf(*shape, dtype=BF):
        return pltpu.VMEM(shape, dtype)

    both = pl.pallas_call(
        lambda *refs: kernel(scale, *refs),
        out_shape=pltpu.VMEM((CH + NCHUNK, TR, TC), BF),
        in_specs=[hbm] * 4,
        out_specs=vmem,
        scratch_shapes=[
            buf(CH, TR, TC), buf(CH, TR, TC), buf(9, CH, CH), buf(9, CH, CH),
            buf(TR, CH, TC), buf(TR, CH, TC),
            buf(3, TR + 8, CH, TC), buf(3, TR + 16, CH, TC), buf(3, TR + 8, CH, TC),
            buf(2, 2, CH, 128), buf(4, CH, 128), buf(4, CH, 128),
            buf(2, CH, 128), buf(3, CH, 128), buf(3, CH, 128),
            buf(CH, K), buf(CH, K), buf(2, CH, 6 * CH), buf(2, CH, 3 * CH),
            buf(TR, CH, TC, dtype=F32),
            buf(3, 3 * CH, CH, dtype=F32), buf(CH, K, dtype=F32), buf(K, 2 * CH),
            buf(PLANE - 1, CHUNK, 2 * CH), buf(NZ, CHUNK, 2 * CH), buf(K, 2 * CH),
            dma((4,)),
            dma((2,)), dma((2,)), dma((2,)), dma((2,)), dma((6,)), dma((6,)), dma((8,)), dma((8,)),
            dma((NCHUNK,)), dma, dma((NZ - 1,)), dma((NZ - 1,)), dma((PLANE - 1,)), dma,
            pltpu.SemaphoreType.REGULAR((3,)),
            buf(2, CH, TC), dma((2,)), dma, dma, dma((2,)),
        ],
        compiler_params=pltpu.CompilerParams(
            collective_id=0, has_side_effects=True, vmem_limit_bytes=60 << 20),
        name="dilated_backward",
    )(field, cotangent, first_filter, second_filter)
    taps = jax.ShapeDtypeStruct((9, CH, CH), F32)
    return pl.pallas_call(
        finish,
        out_shape=(jax.ShapeDtypeStruct((CH, TR, TC), BF), taps, taps),
        in_specs=[vmem],
        out_specs=(hbm, hbm, hbm),
        scratch_shapes=[
            buf(9, CH, CH, dtype=F32), buf(9, CH, CH, dtype=F32), dma((3,))],
        compiler_params=pltpu.CompilerParams(vmem_limit_bytes=16 << 20),
        name="finish",
    )(both)


def solution(mesh):
    in_specs = (P(None, "long", "short"), P(None, "long", "short"), P(), P())
    out_specs = (P(None, "long", "short"), P(), P())
    return jax.shard_map(shards, mesh=mesh, in_specs=in_specs, out_specs=out_specs, check_vma=False)
```

```python
import math

import jax
import jax.numpy as jnp
from jax import lax
from jax.experimental import pallas as pl
from jax.experimental.pallas import tpu as pltpu
from jax.sharding import PartitionSpec as P

BF = jnp.bfloat16
F32 = jnp.float32
MESH = pl.DeviceIdType.MESH
CH, TR, TC = 64, 16, 256
K = 9 * CH
LONG, SHORT = 64, 4
PLANE = 32
NZ = LONG // PLANE * SHORT
CHUNK = 32
NCHUNK = K // CHUNK
OWNERS = (10, 21, 12, 19, 3, 9, 22, 28, 4, 13, 15, 16, 27, 18, 6, 7, 24, 25)

NEAR = ((-1, 0), (1, 0), (0, -1), (0, 1), (-1, -1), (-1, 1), (1, -1), (1, 1))


PLANE_FLIPS = sorted(
    range(1, PLANE), key=lambda m: -((2 if m // 2 % 4 == 2 else min(m // 2 % 4, 1)) + (2 if m // 8 == 2 else min(m // 8, 1))))
ROW_FLIPS = [m for m in PLANE_FLIPS if m < 8]
COLUMN_FLIPS = [m for m in PLANE_FLIPS if m % 8 == 0]
Z_FLIPS = (4, 5, 3, 7, 6, 2, 1)


def nt_dot(a, b):
    return lax.dot_general(a, b, (((1,), (1,)), ((), ())), preferred_element_type=F32)


def dot(a, b):
    return jnp.dot(a, b, preferred_element_type=F32)


def arrived(ref, sem):
    pltpu.make_async_copy(ref, ref, sem).wait()


def kernel(scale, field_hbm, cot_hbm, w1_hbm, w2_hbm, both_ref,
           raw_f, raw_c, raw_w1, raw_w2, xf, a2, fs, cs, gs, ps, pleft, pright, gps, gleft, gright,
           w1c, w1t, w2own, w2halo, up_own, acc2, acc1, gb, ra, rb, fin, in_sem,
           f_send, f_recv, c_send, c_recv, p_send, p_recv, g_send, g_recv,
           a_send, a_recv, b_send, b_recv, o_send, o_recv, ready,
           relay, r_send, r_recv, w_send, w_recv):
    l = lax.axis_index("long")
    s = lax.axis_index("short")
    place = lax.rem(l, PLANE)
    base = l - place
    core = lax.rem(l, 2)
    z = lax.div(l, PLANE) * SHORT + s

    fetch = [pltpu.make_async_copy(src, dst, in_sem.at[i]) for i, (src, dst) in enumerate(
        ((field_hbm, raw_f), (cot_hbm, raw_c), (w1_hbm, raw_w1), (w2_hbm, raw_w2)))]
    for copy in fetch:
        copy.start()

    barrier = pltpu.get_barrier_semaphore()

    def greet(dev):
        pl.semaphore_signal(barrier, inc=1, device_id=dev, device_id_type=MESH)

    def there(dl, ds):
        ok = None
        for d, at, n in ((dl, l, LONG), (ds, s, SHORT)):
            if d == 0:
                continue
            here = at + d >= 0 if d < 0 else at + d < n
            ok = here if ok is None else jnp.logical_and(ok, here)
        return ok

    def flips(at, bits):
        return [b - 2 * b * lax.rem(lax.div(at, b), 2) for b in bits]

    place_flips = flips(place, (1, 2, 4, 8, 16))
    short_flips = flips(s, (1, 2))
    group_flip = PLANE - 2 * PLANE * lax.div(l, PLANE)

    def flipped(at, steps, m):
        for n, step in enumerate(steps):
            if m >> n & 1:
                at = at + step
        return at

    def plane_peer(m):
        return flipped(l, place_flips, m), s

    def z_flip(m):
        return (l + group_flip if m & 4 else l), flipped(s, short_flips, m & 3)

    def z_peer(k):
        other = lax.rem(z + k, NZ)
        return lax.div(other, SHORT) * PLANE + place, lax.rem(other, SHORT)

    first = [plane_peer(m) for m in ROW_FLIPS + COLUMN_FLIPS] + [z_peer(1), z_peer(NZ - 1)]
    greetings = jnp.int32(len(first))
    for dl, ds in NEAR:
        pl.when(there(dl, ds))(lambda dl=dl, ds=ds: greet((l + dl, s + ds)))
        greetings = greetings + there(dl, ds).astype(jnp.int32)
    for dev in first:
        greet(dev)

    def pass_on(n, devs):
        for dev in devs:
            pl.semaphore_signal(ready.at[n], inc=1, device_id=dev, device_id_type=MESH)

    def message(dl, ds, src, dst, send_sem, recv_sem, only=None):
        copy = pltpu.make_async_remote_copy(
            src_ref=src, dst_ref=dst, send_sem=send_sem, recv_sem=recv_sem,
            device_id=(l + dl, s + ds), device_id_type=MESH)
        ok = there(dl, ds) if only is None else only
        return (lambda: pl.when(ok)(lambda: copy.start()),
                lambda: pl.when(ok)(lambda: copy.wait_send()))

    def receive(ok, dst, sem):
        pl.when(ok)(lambda: arrived(dst, sem))

        @pl.when(jnp.logical_not(ok))
        def _():
            dst[...] = jnp.zeros(dst.shape, dst.dtype)

    seam_down = jnp.logical_and(place == PLANE - 1, l < LONG - 1)
    seam_up = jnp.logical_and(place == 0, l > 0)
    up, down = jnp.logical_and(l > 0, place != 0), jnp.logical_and(l < LONG - 1, place != PLANE - 1)
    f_out = [message(-1, 0, fs.at[1, pl.ds(4, 4)], fs.at[1, pl.ds(20, 4)], f_send.at[0], f_recv.at[1], up),
             message(1, 0, fs.at[1, pl.ds(16, 4)], fs.at[1, pl.ds(0, 4)], f_send.at[1], f_recv.at[0], down)]
    f_far = [message(-1, 0, fs.at[1, pl.ds(4, 4)], fs.at[1, pl.ds(20, 4)], f_send.at[0], f_recv.at[1], seam_up),
             message(1, 0, fs.at[1, pl.ds(16, 4)], fs.at[1, pl.ds(0, 4)], f_send.at[1], f_recv.at[0], seam_down)]
    c_out = [message(-1, 0, cs.at[1, pl.ds(8, 8)], cs.at[1, pl.ds(24, 8)], c_send.at[0], c_recv.at[1], up),
             message(1, 0, cs.at[1, pl.ds(16, 8)], cs.at[1, pl.ds(0, 8)], c_send.at[1], c_recv.at[0], down)]
    c_far = [message(-1, 0, cs.at[1, pl.ds(8, 4)], cs.at[1, pl.ds(24, 4)], c_send.at[0], c_recv.at[1], seam_up),
             message(1, 0, cs.at[1, pl.ds(16, 4)], cs.at[1, pl.ds(0, 4)], c_send.at[1], c_recv.at[0], seam_down)]
    relay_out, relay_on = [], []
    for n, hop in enumerate((2, 8)):
        for at_seam, way, low in ((seam_down, 1, 16), (seam_up, -1, 8)):
            rows = pl.ds(low + 4 + 2 * n, 2)
            relay_out.append(message(-way * hop, 0, cs.at[1, rows], relay, r_send.at[n], r_recv, at_seam))
            end = PLANE - 1 - hop if way == 1 else hop
            here = jnp.logical_and(place == end, l < PLANE if way == 1 else l >= LONG - PLANE)
            into = pl.ds((0 if way == 1 else 24) + 4 + 2 * n, 2)
            relay_on.append((here, message(
                way * (hop + 1), 0, relay, cs.at[1, into], w_send, w_recv.at[n], here)))
    g_out = [message(-1, 0, gs.at[1, pl.ds(4, 4)], gs.at[1, pl.ds(20, 4)], g_send.at[0], g_recv.at[7]),
             message(1, 0, gs.at[1, pl.ds(16, 4)], gs.at[1, pl.ds(0, 4)], g_send.at[1], g_recv.at[6])]
    p_out = []
    for side, (ds, into, g_into) in enumerate(((-1, pright, gright), (1, pleft, gleft))):
        p_out.append(message(0, ds, ps.at[side], into.at[pl.ds(1, 2)], p_send.at[side], p_recv.at[1 - side]))
        g_out.append(message(0, ds, gps.at[side], g_into.at[1], g_send.at[2 + side], g_recv.at[1 - side]))
    for half, dl in ((0, -1), (1, 1)):
        for side, (ds, into, g_into) in enumerate(((-1, pright, gright), (1, pleft, gleft))):
            out, back = 2 + 2 * half + side, 2 + 2 * (1 - half) + 1 - side
            p_out.append(message(
                dl, ds, ps.at[side, pl.ds(half, 1)], into.at[pl.ds(3 - 3 * half, 1)], p_send.at[out], p_recv.at[back]))
            g_out.append(message(
                dl, ds, gps.at[side], g_into.at[2 - 2 * half], g_send.at[2 + out], g_recv.at[back]))

    fetch[0].wait()
    own_f = jnp.swapaxes(raw_f[...], 0, 1)
    xf[...] = own_f
    fs[1, 4:20] = jnp.maximum(own_f, 0)
    fetch[1].wait()
    cs[1, 8:24] = jnp.swapaxes(raw_c[...], 0, 1)
    for half in range(2):
        for side in range(2):
            c8 = 0 if side == 0 else TC - 8
            c4 = 0 if side == 0 else TC - 4
            pieces = [cs[1, 8 + 8 * half + k][:, c8:c8 + 8] for k in range(8)]
            pieces += [fs[1, 4 + 8 * half + k][:, c4:c4 + 4] for k in range(8)]
            pieces += [jnp.zeros((CH, 32), BF)]
            ps[side, half] = jnp.concatenate(pieces, axis=1)

    pl.semaphore_wait(barrier, greetings)
    for start, _ in f_far + p_out + relay_out + f_out + c_out:
        start()
    pass_on(0, [plane_peer(m) for m in ROW_FLIPS])
    pass_on(1, [z_peer(1), z_peer(NZ - 1)])

    fetch[2].wait()
    fetch[3].wait()
    for t in range(9):
        w1c[:, CH * t:CH * (t + 1)] = raw_w1[t]
    w1t[...] = raw_w1[...].reshape(K, CH).T
    taps_of = [raw_w2[3 * a:3 * a + 3].reshape(3 * CH, CH).T for a in range(3)]
    for half in range(2):
        w2own[half] = jnp.concatenate([taps_of[1], taps_of[2 * half]], axis=1)
        w2halo[half] = taps_of[2 - 2 * half]

    for _, sent in f_far:
        sent()
    for start, _ in c_far:
        start()

    acc2[...] = jnp.zeros_like(acc2)
    acc1[...] = jnp.zeros_like(acc1)

    def shift_left(x, h, at, d):
        return jnp.concatenate([x[:, d:], h[:, at:at + d]], axis=1)

    def shift_right(x, h, at, d):
        return jnp.concatenate([h[:, at:at + d], x[:, :TC - d]], axis=1)

    def f_row(blk, k, e):
        x = fs[1, e]
        fs[0, e] = shift_right(x, pleft[blk], 64 + 4 * k, 4)
        fs[2, e] = shift_left(x, pright[blk], 64 + 4 * k, 4)

    def c_row(blk, k):
        e = 8 * blk + k
        x = cs[1, e]
        cs[2, e] = shift_right(x, pleft[blk], 8 * k, 8)
        cs[0, e] = shift_left(x, pright[blk], 8 * k, 8)

    def taps(ref, rows):
        return [ref[b, e] for e in rows for b in range(3)]

    def stack(parts):
        return jnp.concatenate(parts, axis=0)

    receive(there(0, -1), pleft.at[pl.ds(1, 2)], p_recv.at[0])
    receive(there(0, 1), pright.at[pl.ds(1, 2)], p_recv.at[1])
    for here, (start, _) in relay_on:
        pl.when(here)(lambda: arrived(relay, r_recv))
        start()
    pl.semaphore_wait(ready.at[0], len(ROW_FLIPS))
    pl.semaphore_wait(ready.at[1], 2)
    pass_on(2, [z_peer(2), z_peer(NZ - 2)])

    @pl.loop(1, 3)
    def _(blk):
        for k in range(8):
            f_row(blk, k, 8 * blk + k - 4)
            c_row(blk, k)

    def hidden_row(r):
        h = xf[r].astype(F32) + dot(w1c[...], stack(taps(fs, [r, r + 4, r + 8])))
        a2[r] = jnp.maximum(h.astype(BF), 0)

    @pl.loop(1, 3)
    def _(g):
        for k in range(4):
            hidden_row(4 * g + k)

    for half in range(2):
        @pl.loop(0, 2)
        def _(g):
            for k in range(4):
                r = 8 * half + 4 * g + k
                up_own[r] = dot(w2own[half], stack(taps(cs, [r + 8, r + 16 - 16 * half])))

    @pl.loop(0, 2)
    def _(i):
        half = (1 - core) + i * (2 * core - 1)
        ok = jnp.logical_or(jnp.logical_and(half == 0, l > 0), jnp.logical_and(half == 1, l < LONG - 1))
        receive(jnp.logical_and(ok, s > 0), pleft.at[pl.ds(3 * half, 1)], p_recv.at[2 + 2 * half])
        receive(jnp.logical_and(ok, s < SHORT - 1), pright.at[pl.ds(3 * half, 1)], p_recv.at[3 + 2 * half])
        receive(ok, fs.at[1, pl.ds(20 * half, 4)], f_recv.at[half])
        for k in range(4):
            e = 20 * half + k
            x = fs[1, e]
            for b, shift, pack in ((0, shift_right, pleft), (2, shift_left, pright)):
                low = shift(x, pack[3 * half], 64 + 4 * k, 4)
                high = shift(x, pack[3 * half], 64 + 4 * (k + 4), 4)
                fs[b, e] = jnp.where(half == 1, low, high)
        for k in range(4):
            hidden_row(12 * half + k)

        rows = [8 * half + k for k in range(8)]
        act = jnp.concatenate([a2[r] for r in rows], axis=1)
        own = nt_dot(
            jnp.concatenate([stack(taps(cs, [r + 8, r + 16 - 16 * half])) for r in rows], axis=1), act)
        acc2[1] += own[:3 * CH]
        acc2[2 * half] += own[3 * CH:]

        far = jnp.logical_or(jnp.logical_and(half == 1, seam_down), jnp.logical_and(half == 0, seam_up))
        edge = 24 * half

        @pl.when(far)
        def _():
            arrived(cs.at[1, pl.ds(edge, 4)], c_recv.at[half])
            for n in range(2):
                arrived(cs.at[1, pl.ds(edge + 4 + 2 * n, 2)], w_recv.at[n])

        pl.when(jnp.logical_not(far))(lambda: receive(ok, cs.at[1, pl.ds(edge, 8)], c_recv.at[half]))
        for k in range(8):
            c_row(3 * half, k)
        beyond = [stack(taps(cs, [24 * half + k])) for k in range(8)]
        for k, r in enumerate(rows):
            up = up_own[r] + dot(w2halo[half], beyond[k])
            gh = cs[1, r + 8].astype(F32) + jnp.where(a2[r].astype(F32) > 0, up, 0.0)
            gs[1, r + 4] = gh.astype(BF)
        acc2[2 - 2 * half] += nt_dot(jnp.concatenate(beyond, axis=1), act)
        acc1[...] += nt_dot(
            jnp.concatenate([gs[1, r + 4] for r in rows], axis=1),
            jnp.concatenate([stack(taps(fs, [r, r + 4, r + 8])) for r in rows], axis=1))

    def a_copy(j):
        owner = OWNERS[j]
        slot = place - (place > owner).astype(jnp.int32)
        return pltpu.make_async_remote_copy(
            src_ref=gb.at[pl.ds(CHUNK * j, CHUNK)], dst_ref=ra.at[slot],
            send_sem=a_send.at[j], recv_sem=a_recv,
            device_id=(base + owner, s), device_id_type=MESH)

    for t in range(9):
        gb[CH * t:CH * (t + 1), :] = jnp.concatenate(
            [acc2[t // 3, CH * (t % 3):CH * (t % 3 + 1), :], acc1[:, CH * t:CH * (t + 1)]], axis=1).astype(BF)
        for j in range(CH // CHUNK * t, CH // CHUNK * (t + 1)):
            pl.when(place != OWNERS[j])(lambda j=j: a_copy(j).start())
    pl.semaphore_wait(ready.at[2], 2)

    for start, _ in g_out[:2]:
        start()
    for side in range(2):
        c4 = 0 if side == 0 else TC - 4
        pieces = [gs[1, 4 + k][:, c4:c4 + 4] for k in range(16)] + [jnp.zeros((CH, 64), BF)]
        gps[side] = jnp.concatenate(pieces, axis=1)
    for start, _ in g_out[2:]:
        start()

    receive(there(-1, 0), gs.at[1, pl.ds(0, 4)], g_recv.at[6])
    receive(there(1, 0), gs.at[1, pl.ds(20, 4)], g_recv.at[7])
    for side, (ds, into) in enumerate(((-1, gleft), (1, gright))):
        receive(there(0, ds), into.at[1], g_recv.at[side])
        receive(there(-1, ds), into.at[0], g_recv.at[2 + side])
        receive(there(1, ds), into.at[2], g_recv.at[4 + side])

    def g_row(blk, e, at):
        x = gs[1, e]
        gs[2, e] = shift_right(x, gleft[blk], at, 4)
        gs[0, e] = shift_left(x, gright[blk], at, 4)

    for k in range(16):
        g_row(1, 4 + k, 4 * k)
    for k in range(4):
        g_row(0, k, 4 * (12 + k))
        g_row(2, 20 + k, 4 * k)

    @pl.loop(0, TR // 4)
    def _(g):
        for k in range(4):
            r = 4 * g + k
            back = dot(w1t[...], stack(taps(gs, [r + 8, r + 4, r])))
            out = gs[1, r + 4].astype(F32) + jnp.where(xf[r].astype(F32) > 0, back, 0.0)
            xf[r] = out.astype(BF)

    both_ref[:CH] = jnp.swapaxes(xf[...], 0, 1)

    mine = jnp.int32(0)
    is_owner = place < 0
    for j, owner in enumerate(OWNERS):
        mine = jnp.where(place == owner, j, mine)
        is_owner = jnp.logical_or(is_owner, place == owner)
    my_rows = pl.ds(pl.multiple_of(CHUNK * mine, CHUNK), CHUNK)

    def b_copy(k):
        return pltpu.make_async_remote_copy(
            src_ref=rb.at[0], dst_ref=rb.at[k], send_sem=b_send.at[k - 1], recv_sem=b_recv.at[k - 1],
            device_id=z_flip(k), device_id_type=MESH)

    def o_copy(n):
        return pltpu.make_async_remote_copy(
            src_ref=fin.at[my_rows], dst_ref=fin.at[my_rows], send_sem=o_send.at[n],
            recv_sem=o_recv, device_id=plane_peer(PLANE_FLIPS[n]), device_id_type=MESH)

    @pl.when(is_owner)
    def _():
        arrived(ra, a_recv)
        total = gb[my_rows, :].astype(F32)
        for i in range(PLANE - 1):
            total += ra[i].astype(F32)
        rb[0] = total.astype(BF)
        for k in Z_FLIPS:
            b_copy(k).start()

    @pl.when(is_owner)
    def _():
        full = rb[0].astype(F32)
        for k in reversed(Z_FLIPS):
            b_copy(k).wait_recv()
            full += rb[k].astype(F32)
        fin[my_rows, :] = (full * scale).astype(BF)
        for n in range(PLANE - 1):
            o_copy(n).start()

    for _, sent in f_out + p_out + c_out + c_far + g_out + relay_out + [out for _, out in relay_on]:
        sent()
    for j in range(NCHUNK):
        pl.when(place != OWNERS[j])(lambda j=j: a_copy(j).wait_send())

    pl.when(is_owner)(lambda: arrived(fin.at[pl.ds(0, K - CHUNK)], o_recv))
    pl.when(jnp.logical_not(is_owner))(lambda: arrived(fin, o_recv))
    for j in range(NCHUNK):
        both_ref[CH + j] = jnp.concatenate(
            [fin[CHUNK * j:CHUNK * j + TR, :], fin[CHUNK * j + TR:CHUNK * (j + 1), :]], axis=1)

    @pl.when(is_owner)
    def _():
        for k in Z_FLIPS:
            b_copy(k).wait_send()
        for n in range(PLANE - 1):
            o_copy(n).wait_send()


def finish(both, out_hbm, first_hbm, second_hbm, first, second, store):
    stores = [pltpu.make_async_copy(src, dst, store.at[i]) for i, (src, dst) in enumerate(
        ((both.at[pl.ds(0, CH)], out_hbm), (first, first_hbm), (second, second_hbm)))]
    stores[0].start()
    for t in range(9):
        for q in range(CH // TR):
            rows, lanes = slice(TR * q, TR * (q + 1)), slice(2 * CH * (q % 2), 2 * CH * (q % 2 + 1))
            part = both[CH + 2 * t + q // 2, :, lanes].astype(F32)
            first[t, rows] = part[:, CH:]
            second[t, rows] = part[:, :CH]
    stores[1].start()
    stores[2].start()
    for copy in stores:
        copy.wait()


def shards(field, cotangent, first_filter, second_filter):
    scale = 1.0 / math.sqrt(TR * LONG * TC * SHORT)
    hbm = pl.BlockSpec(memory_space=pltpu.HBM)
    vmem = pl.BlockSpec(memory_space=pltpu.VMEM)
    dma = pltpu.SemaphoreType.DMA

    def buf(*shape, dtype=BF):
        return pltpu.VMEM(shape, dtype)

    both = pl.pallas_call(
        lambda *refs: kernel(scale, *refs),
        out_shape=pltpu.VMEM((CH + NCHUNK, TR, TC), BF),
        in_specs=[hbm] * 4,
        out_specs=vmem,
        scratch_shapes=[
            buf(CH, TR, TC), buf(CH, TR, TC), buf(9, CH, CH), buf(9, CH, CH),
            buf(TR, CH, TC), buf(TR, CH, TC),
            buf(3, TR + 8, CH, TC), buf(3, TR + 16, CH, TC), buf(3, TR + 8, CH, TC),
            buf(2, 2, CH, 128), buf(4, CH, 128), buf(4, CH, 128),
            buf(2, CH, 128), buf(3, CH, 128), buf(3, CH, 128),
            buf(CH, K), buf(CH, K), buf(2, CH, 6 * CH), buf(2, CH, 3 * CH),
            buf(TR, CH, TC, dtype=F32),
            buf(3, 3 * CH, CH, dtype=F32), buf(CH, K, dtype=F32), buf(K, 2 * CH),
            buf(PLANE - 1, CHUNK, 2 * CH), buf(NZ, CHUNK, 2 * CH), buf(K, 2 * CH),
            dma((4,)),
            dma((2,)), dma((2,)), dma((2,)), dma((2,)), dma((6,)), dma((6,)), dma((8,)), dma((8,)),
            dma((NCHUNK,)), dma, dma((NZ - 1,)), dma((NZ - 1,)), dma((PLANE - 1,)), dma,
            pltpu.SemaphoreType.REGULAR((3,)),
            buf(2, CH, TC), dma((2,)), dma, dma, dma((2,)),
        ],
        compiler_params=pltpu.CompilerParams(
            collective_id=0, has_side_effects=True, vmem_limit_bytes=60 << 20),
        name="dilated_backward",
    )(field, cotangent, first_filter, second_filter)
    taps = jax.ShapeDtypeStruct((9, CH, CH), F32)
    return pl.pallas_call(
        finish,
        out_shape=(jax.ShapeDtypeStruct((CH, TR, TC), BF), taps, taps),
        in_specs=[vmem],
        out_specs=(hbm, hbm, hbm),
        scratch_shapes=[
            buf(9, CH, CH, dtype=F32), buf(9, CH, CH, dtype=F32), dma((3,))],
        compiler_params=pltpu.CompilerParams(vmem_limit_bytes=16 << 20),
        name="finish",
    )(both)


def solution(mesh):
    in_specs = (P(None, "long", "short"), P(None, "long", "short"), P(), P())
    out_specs = (P(None, "long", "short"), P(), P())
    return jax.shard_map(shards, mesh=mesh, in_specs=in_specs, out_specs=out_specs, check_vma=False)
```
